32 devices in a mesh: leaf: 32 (over z, y, x, core).
Axes of the slice: x: 2, y: 2, z: 4, core: 2. Of those that a mesh axis runs over, the one named last changes fastest.
Arguments:
- points: bfloat16 [32768, 768], P('leaf'), may hold values from -4 to 4
- weights: bfloat16 [32768, 64], P('leaf'), may hold values from -0.0390625 to 0.0390625
- tree_slot: int32 [32768], P('leaf'), may hold values from 0 to 32767, as said below
- leaf_interp: bfloat16 [32, 256, 1024], P('leaf'), may hold values from -0.1875 to 0.1875
- skel_leaf: int32 [32, 256], P('leaf'), may hold values from 0 to 1023, as said below
- merge_interp: bfloat16 [32, 240, 512], P('leaf'), may hold values from -0.25 to 0.25
- merge_index: int32 [32, 240], P('leaf'), may hold values from 0 to 511, as said below
- near_mask: int32 [32, 8], P('leaf'), may hold values from 0 to 1, as said below
- far_mask: int32 [32, 4, 4], P('leaf'), may hold values from 0 to 1, as said below
Outputs:
- sums: float32 [32768, 64], P('leaf')
The draws below stay inside these ranges and needn't reach their ends.
Inputs may be any that keep to these rules, and one draw needn't show every extreme that they name: `tree_slot`: A permutation of the tree positions; each aligned block of 1024 input points sends exactly 32 points into the block of every leaf. `skel_leaf`: each row lists 256 distinct positions. `merge_index`: for every node of every level, the 256 entries of I_k are distinct. Symmetric: near_mask[l, 4 + s - 1] equals near_mask[l + s, 4 - s] for 1 <= s <= 4; entries that name a leaf outside the tree are 0. `far_mask`: entries that name a node outside its level are 0.
All inputs are finite; a program needn't handle non-finite values.
Results may differ from the reference program's by a relative error of at most 0.0042.
Values may be sent and summed in bfloat16 or wider, within the bound.
No kernel may reach another device: no remote copies, remote signals or barrier semaphores. Data moves between devices by JAX's collectives and lax.ppermute only.
A program may use at most 128 MiB of HBM per device.

```python
import math
import jax
import jax.numpy as jnp
from jax import lax

D = 768
COLS = 64
RANK = 256
LEVELS = 4
NWIN = 4
FWIN = 2
PTS_DEV = 1024
POINTS = 32768
MROWS = 240
N_LEAF = 32


def draw_tree_slot(key, part):
    per_peer = PTS_DEV // N_LEAF
    leaf_ids = jnp.arange(N_LEAF, dtype=jnp.int32)
    source_key = jax.random.fold_in(key, 11)
    target_key = jax.random.fold_in(key, 12)
    source_perm = jax.vmap(lambda leaf_index: jax.random.permutation(jax.random.fold_in(source_key, leaf_index), PTS_DEV))(leaf_ids)
    target_perm = jax.vmap(lambda leaf_index: jax.random.permutation(jax.random.fold_in(target_key, leaf_index), PTS_DEV))(leaf_ids)
    rank_in = jnp.argsort(source_perm, axis=1).astype(jnp.int32)
    dest_leaf = rank_in // per_peer
    within_peer = rank_in % per_peer
    position = target_perm[dest_leaf, leaf_ids[:, None] * per_peer + within_peer]
    return (dest_leaf * PTS_DEV + position).reshape(-1).astype(jnp.int32)


def log_uniform(key, shape, low, high):
    return jnp.exp(jax.random.uniform(key, shape, jnp.float32, math.log(low), math.log(high)))


def draw_points(key, part):
    slots = draw_tree_slot(key, part)
    group_count = PTS_DEV // 4
    group_of = (slots % PTS_DEV // 4).astype(jnp.int32)
    point_count = slots.shape[0]
    centre_key = jax.random.fold_in(key, 7001)
    noise_key = jax.random.fold_in(key, 7002)
    spread_key = jax.random.fold_in(key, 7003)
    centres = 0.45 * jax.random.normal(centre_key, (group_count, D), jnp.float32)
    noise = jax.random.normal(noise_key, (point_count, D), jnp.float32)
    spread = log_uniform(spread_key, (point_count, 1), 0.05, 0.25)
    values = centres[group_of] + spread * noise
    return jnp.clip(values, -4.0, 4.0).astype(jnp.bfloat16)


def draw_skel_leaf(key, part):
    leaf_ids = jnp.arange(N_LEAF, dtype=jnp.int32)
    picked = jax.vmap(lambda leaf_index: jax.random.permutation(jax.random.fold_in(key, leaf_index), PTS_DEV)[:RANK])(leaf_ids)
    return picked.astype(jnp.int32)


def draw_merge_index(key, part):
    pieces = []
    for tree_level in range(1, LEVELS + 1):
        node_count = N_LEAF >> tree_level
        piece_rows = RANK >> tree_level
        level_key = jax.random.fold_in(key, 100 + tree_level)
        node_ids = jnp.arange(node_count, dtype=jnp.int32)
        picked = jax.vmap(lambda node_index: jax.random.permutation(jax.random.fold_in(level_key, node_index), 2 * RANK)[:RANK])(node_ids)
        pieces.append(picked.reshape(N_LEAF, piece_rows))
    return jnp.concatenate(pieces, axis=1).astype(jnp.int32)


def draw_near_mask(key, part):
    coin_flips = (jax.random.randint(key, (N_LEAF, NWIN), 0, 4) > 0).astype(jnp.int32)
    leaf_ids = jnp.arange(N_LEAF, dtype=jnp.int32)[:, None]
    distances = jnp.arange(1, NWIN + 1, dtype=jnp.int32)[None, :]
    upward = jnp.where(leaf_ids + distances < N_LEAF, coin_flips, 0)
    partner = jnp.clip(leaf_ids - distances, 0, N_LEAF - 1)
    column_ids = jnp.broadcast_to(distances - 1, partner.shape)
    downward = jnp.where(leaf_ids - distances >= 0, upward[partner, column_ids], 0)
    return jnp.concatenate([downward[:, ::-1], upward], axis=1).astype(jnp.int32)


def draw_far_mask(key, part):
    coin_flips = (jax.random.randint(key, (N_LEAF, LEVELS, 2 * FWIN), 0, 4) > 0).astype(jnp.int32)
    node_steps = jnp.concatenate([jnp.arange(-FWIN, 0, dtype=jnp.int32), jnp.arange(1, FWIN + 1, dtype=jnp.int32)])
    tree_levels = jnp.arange(1, LEVELS + 1, dtype=jnp.int32)
    leaf_ids = jnp.arange(N_LEAF, dtype=jnp.int32)
    node_ids = jnp.right_shift(leaf_ids[:, None, None], tree_levels[None, :, None]) + node_steps[None, None, :]
    limits = jnp.right_shift(jnp.full((LEVELS,), N_LEAF, jnp.int32), tree_levels)[None, :, None]
    valid = (node_ids >= 0) & (node_ids < limits)
    return jnp.where(valid, coin_flips, 0).astype(jnp.int32)


def steps_of(own_key, dims, cuts, least, high):
    def one(dim, blocks):
        heights = jax.random.uniform(jax.random.fold_in(jax.random.fold_in(own_key, 6), dim), (blocks,), jnp.float32, least / len(cuts), high / len(cuts))
        return jnp.repeat(jnp.exp(heights), dims[dim] // blocks).reshape((-1,) + (1,) * (len(dims) - dim - 1))

    gain = one(*cuts[0])
    for cut in cuts[1:]:
        gain = gain * one(*cut)
    return gain


def centred(own_key, extent, scale, reach, split=(), kind=jnp.bfloat16):
    drawn = scale * jax.random.normal(own_key, extent, jnp.float32)
    if split:
        drawn = drawn * steps_of(own_key, extent, split, -0.22, 0.18)
    return jnp.clip(drawn, -reach, reach).astype(kind)


def setup_inputs(seed: int = 0) -> dict:
    key_of = jax.random.split(jax.random.key(seed), 10)
    points = draw_points(jax.random.fold_in(key_of[9], 71), 0)
    weights = centred(key_of[1], (POINTS, COLS), 0.0065, 0.0390625, ((0, 32),))
    tree_slot = draw_tree_slot(jax.random.fold_in(key_of[9], 71), 0)
    leaf_interp = centred(key_of[3], (N_LEAF, RANK, PTS_DEV), PTS_DEV ** -0.5, 0.1875, ((0, 32),))
    skel_leaf = draw_skel_leaf(jax.random.fold_in(key_of[9], 71), 0)
    merge_interp = centred(key_of[5], (N_LEAF, MROWS, 2 * RANK), (2 * RANK) ** -0.5, 0.25, ((0, 32),))
    merge_index = draw_merge_index(jax.random.fold_in(key_of[9], 71), 0)
    near_mask = draw_near_mask(jax.random.fold_in(key_of[9], 71), 0)
    far_mask = draw_far_mask(jax.random.fold_in(key_of[9], 71), 0)
    return dict(points=points, weights=weights, tree_slot=tree_slot, leaf_interp=leaf_interp, skel_leaf=skel_leaf, merge_interp=merge_interp, merge_index=merge_index, near_mask=near_mask, far_mask=far_mask)


def row_offset(block, scale_inv):
    squares = lax.optimization_barrier(jnp.sum(jnp.square(block.astype(jnp.float32)), axis=1))
    return (squares - block.shape[1]) * (0.5 * scale_inv)

def kernel_block(targets, target_shift, sources, source_shift, scale_inv):
    products = jnp.dot(targets, sources.T, preferred_element_type=jnp.float32)
    exponent = products * scale_inv - target_shift[:, None] - source_shift[None, :]
    return jnp.exp(exponent).astype(jnp.bfloat16)

def kernel_sum(targets, target_shift, sources, source_weight, scale_inv):
    kernel = kernel_block(targets, target_shift, sources, row_offset(sources, scale_inv), scale_inv)
    return jnp.dot(kernel, source_weight, preferred_element_type=jnp.float32)

def reference(points, weights, tree_slot, leaf_interp, skel_leaf, merge_interp, merge_index, near_mask, far_mask):
    scale_inv = 1.0 / (1.75 * math.sqrt(D))
    source_of = jnp.argsort(tree_slot).astype(jnp.int32)
    leaf_points = points[source_of].reshape(N_LEAF, PTS_DEV, D)
    leaf_weights = weights[source_of].reshape(N_LEAF, PTS_DEV, COLS)
    pick_rows = jax.vmap(lambda block, chosen: block[chosen])
    skeleton = pick_rows(leaf_points, skel_leaf)
    skeleton_weight = jnp.einsum('lrp,lpc->lrc', leaf_interp.astype(jnp.float32), leaf_weights.astype(jnp.float32)).astype(jnp.bfloat16)
    level_points = []
    level_weights = []
    offset = 0
    for tree_level in range(1, LEVELS + 1):
        node_count = N_LEAF >> tree_level
        piece_rows = RANK >> tree_level
        both_points = skeleton.reshape(node_count, 2 * RANK, D)
        both_weights = skeleton_weight.reshape(node_count, 2 * RANK, COLS)
        interp = merge_interp[:, offset:offset + piece_rows].reshape(node_count, RANK, 2 * RANK)
        chosen = merge_index[:, offset:offset + piece_rows].reshape(node_count, RANK)
        skeleton = pick_rows(both_points, chosen)
        skeleton_weight = jnp.einsum('nrs,nsc->nrc', interp.astype(jnp.float32), both_weights.astype(jnp.float32)).astype(jnp.bfloat16)
        level_points.append(skeleton)
        level_weights.append(skeleton_weight)
        offset += piece_rows
    near_steps = list(range(-NWIN, 0)) + list(range(1, NWIN + 1))
    far_steps = list(range(-FWIN, 0)) + list(range(1, FWIN + 1))

    def one_leaf(leaf_id):
        own_points = leaf_points[leaf_id]
        own_weights = leaf_weights[leaf_id]
        own_shift = row_offset(own_points, scale_inv)

        def evaluate(operands):
            return kernel_sum(own_points, own_shift, operands[0], operands[1], scale_inv)

        def nothing(operands):
            return jnp.zeros((PTS_DEV, COLS), jnp.float32)
        outputs = evaluate((own_points, own_weights))
        for column, leaf_step in enumerate(near_steps):
            source_leaf = jnp.clip(leaf_id + leaf_step, 0, N_LEAF - 1)
            outputs = outputs + lax.cond(near_mask[leaf_id, column] > 0, evaluate, nothing, (leaf_points[source_leaf], leaf_weights[source_leaf]))
        for tree_level in range(1, LEVELS + 1):
            for column, node_step in enumerate(far_steps):
                node_id = jnp.clip(jnp.right_shift(leaf_id, tree_level) + node_step, 0, (N_LEAF >> tree_level) - 1)
                outputs = outputs + lax.cond(far_mask[leaf_id, tree_level - 1, column] > 0, evaluate, nothing, (level_points[tree_level - 1][node_id], level_weights[tree_level - 1][node_id]))
        return outputs
    tree_sums = lax.map(one_leaf, jnp.arange(N_LEAF, dtype=jnp.int32)).reshape(POINTS, COLS)
    return tree_sums[tree_slot]
```

```python
import functools
import math

import jax
import jax.numpy as jnp
from jax import lax
from jax.experimental import pallas as pl
from jax.experimental.pallas import tpu as pltpu
from jax.sharding import PartitionSpec as P

LEVELS = 4
NWIN = 4
FWIN = 2
GROUP = 8
BF16 = jnp.bfloat16
F32 = jnp.float32
I32 = jnp.int32
NT = (((1,), (1,)), ((), ()))
TN = (((0,), (0,)), ((), ()))
CHUNK = 256


def call(kernel, grid_spec, out_shape, flops=0, moved=0, exps=0):
    return pl.pallas_call(
        kernel,
        grid_spec=grid_spec,
        out_shape=out_shape,
        compiler_params=pltpu.CompilerParams(vmem_limit_bytes=48 * 1024 * 1024),
        cost_estimate=pl.CostEstimate(flops=flops, bytes_accessed=moved, transcendentals=exps),
    )


def whole(shape):
    return pl.BlockSpec(shape, lambda *_: (0,) * len(shape))


def shapes(*specs):
    return [jax.ShapeDtypeStruct(shape, kind) for shape, kind in specs]


def mm(a, b):
    return jnp.dot(a, b, preferred_element_type=F32)


def mm_nt(a, b):
    return lax.dot_general(a, b, NT, preferred_element_type=F32)


def mm_tn(a, b):
    return lax.dot_general(a, b, TN, preferred_element_type=F32)


def device_of_leaf(leaf):
    group, chip = leaf // GROUP, (leaf // 2) % 4
    return group * GROUP + ((chip ^ (chip >> 1)) ^ ((group & 1) * 2)) * 2 + leaf % 2


def leaf_of_device(device):
    group, chip = device // GROUP, (device // 2) % 4 ^ ((device // GROUP & 1) * 2)
    return group * GROUP + (chip ^ (chip >> 1)) * 2 + device % 2


def move(value, target_of_leaf):
    leaves = lax.axis_size("leaf")
    pairs = []
    for leaf in range(leaves):
        target = target_of_leaf(leaf)
        if 0 <= target < leaves:
            pairs.append((device_of_leaf(leaf), device_of_leaf(target)))
    return lax.ppermute(value, "leaf", pairs)


def slot_sources(groups):
    slots = []
    for away in range(1, min(6, groups)):
        merge = away > 1 and groups <= 2 * away
        for steps in [(away, -away)] if merge else [(away,), (-away,)]:
            found = [[g + s for s in steps if 0 <= g + s < groups] for g in range(groups)]
            slots.append((away, [f[0] if f else -1 for f in found]))
    return slots


def send_slot(value, source):
    pairs = [
        (device_of_leaf(s * GROUP + i), device_of_leaf(g * GROUP + i))
        for g, s in enumerate(source)
        if s >= 0
        for i in range(GROUP)
    ]
    return lax.ppermute(value, "leaf", pairs)


LEAF, CORE, CHIP, NODE, AT, PHYS = range(6)
SLOT0 = 6


def iota(shape, dim):
    return lax.broadcasted_iota(I32, shape, dim)


def sort_kernel(rows, per_peer, leaves, lanes, slot_ref, points_ref, weights_ref, table_ref, send_ref, place_ref, place_s):
    step = pl.program_id(0)
    block = send_ref.shape[0]
    slot = slot_ref[...]

    @pl.when(step == 0)
    def _():
        dest = device_of_leaf(slot // rows)
        at = (iota((leaves, rows), 0) == dest).astype(BF16)
        earlier = (iota((rows, rows), 0) < iota((rows, rows), 1)).astype(BF16)
        rank = jnp.sum(at.astype(F32) * mm(at, earlier), axis=0, keepdims=True)
        place_s[...] = dest * per_peer + rank.astype(I32)
        place_ref[...] = place_s[...]

    pick = (iota((block, rows), 0) + step * block == place_s[...]).astype(BF16)
    width, columns = points_ref.shape[1], weights_ref.shape[0]
    wide = send_ref.shape[1]
    inner = slot % rows
    row = iota((16, rows), 0)
    parts = jnp.where(row == 0, inner // 32, jnp.where(row == 1, inner % 32, 0)).astype(F32).astype(BF16)
    send_ref[:, :width] = mm(pick, points_ref[...]).astype(BF16)
    send_ref[:, width : width + columns] = mm_nt(pick, weights_ref[...]).astype(BF16)
    send_ref[:, width + columns : width + columns + 16] = mm_nt(pick, parts).astype(BF16)
    send_ref[:, width + columns + 16 : wide - lanes] = jnp.zeros((block, wide - lanes - width - columns - 16), BF16)
    spread = (iota((block, per_peer), 0) % per_peer == iota((block, per_peer), 1)).astype(BF16)
    send_ref[:, wide - lanes :] = mm(spread, table_ref[...]).astype(BF16)


def tree_rows(extra):
    lane = iota((16, extra.shape[1]), 1)
    parts = jnp.where(lane == 0, 32.0, jnp.where(lane == 1, 1.0, 0.0)).astype(BF16)
    return mm_nt(parts, extra)[0:1].astype(I32)


def entries(table, low, high, leaf):
    lane = iota((1, GROUP), 1)
    return jnp.sum(jnp.where(lane == leaf, table[low:high], 0.0), axis=1, keepdims=True).astype(I32)


def table_of(table_ref, group):
    return jnp.transpose(table_ref[pl.ds(pl.multiple_of(group * GROUP, GROUP), GROUP)])


def bounds(rank):
    ends = [rank]
    for level in range(1, LEVELS + 1):
        ends.append(ends[-1] + (rank >> level))
    return ends


def node_picks(table, rank, level, first, count):
    low, high = bounds(rank)[level - 1 : level + 1]
    return jnp.concatenate([entries(table, low, high, first + i) for i in range(count)], axis=0)


def leaf_picks(table, rank, leaf, where):
    skeleton = (entries(table, 0, rank, leaf) == where).astype(BF16)
    index1 = node_picks(table, rank, 1, leaf // 2 * 2, 2) - rank * (leaf % 2)
    return skeleton, (index1 == iota((rank, rank), 1)).astype(BF16)


def level0_kernel(info, got_ref, interp_ref, table_ref, give_ref, keep_ref, weight0_ref):
    rank, columns = weight0_ref.shape
    rows, width = got_ref.shape[0], keep_ref.shape[1]
    half = rank // 2
    where = tree_rows(got_ref[:, width + columns :])
    order = (iota((rows, rows), 0) == where).astype(BF16)
    weights = mm(order, got_ref[:, width : width + columns]).astype(BF16)
    weight0 = mm(interp_ref[...], weights).astype(BF16)
    weight0_ref[...] = weight0
    table = table_of(table_ref, info[AT])
    skeleton, pick1 = leaf_picks(table, rank, info[LEAF] % GROUP, where)
    level0 = mm(skeleton, got_ref[:, :width]).astype(BF16)
    level1 = mm(pick1, level0).astype(BF16)
    core = info[CORE]

    def part(side):
        index2 = node_picks(table, rank, 2, 4 * info[NODE] + 2 * side, 2) - rank * (info[CHIP] % 2)
        return mm((index2 == iota((half, rank), 1)).astype(BF16), level1).astype(BF16)

    keep_ref[...] = part(core)
    give_ref[:, :width] = part(1 - core)
    give_ref[:, width : width + columns] = weight0[:half]
    give_ref[:, width + columns :] = weight0[half:]


def piece(info, pieces_ref, leaf):
    return pieces_ref.at[leaf % 2 ^ info[CORE], leaf // 2 ^ info[PHYS]]


def in_order(core, mine, other):
    return jnp.where(core == 0, jnp.concatenate([mine, other]), jnp.concatenate([other, mine]))


def level1_kernel(info, other_ref, keep_ref, weight0_ref, pieces_ref, out_ref, weight1_ref):
    rank, columns = weight1_ref.shape
    half, width = keep_ref.shape
    core = info[CORE]
    other0 = jnp.concatenate([other_ref[:, width : width + columns], other_ref[:, width + columns :]])
    both0 = in_order(core, weight0_ref[...], other0)
    pair = [mm(piece(info, pieces_ref, 2 * info[CHIP] + i)[:half], both0) for i in (0, 1)]
    weight1 = jnp.concatenate(pair).astype(BF16)
    weight1_ref[...] = weight1
    out_ref[:, :width] = keep_ref[...] + other_ref[:, :width]
    out_ref[:, width : width + columns] = weight1[:half]
    out_ref[:, width + columns :] = weight1[half:]


def level23_kernel(info, m0, m1, m2, m3, pieces_ref, out_ref, weight2_ref, weight3_ref, w1_s):
    half = m0.shape[0]
    rank = 2 * half
    columns = weight2_ref.shape[1]
    width = m0.shape[1] - 2 * columns
    core, chip, node = info[CORE], info[CHIP], info[NODE]
    for k, message in enumerate((m0, m1, m2, m3)):
        at = pl.ds(pl.multiple_of((chip ^ k) * rank, rank), rank)
        w1_s[at] = jnp.concatenate([message[:, width : width + columns], message[:, width + columns :]])
    r2, r3 = rank >> 2, rank >> 3
    for n in (0, 1):
        for i in range(4):
            rows2 = piece(info, pieces_ref, 4 * n + i)[half : half + r2]
            at = n * rank + i * r2
            weight2_ref[at : at + r2] = mm(rows2, w1_s[2 * n * rank : 2 * (n + 1) * rank]).astype(BF16)
    low = half + r2
    weight3 = jnp.concatenate(
        [mm(piece(info, pieces_ref, i)[low : low + r3], weight2_ref[...]) for i in range(GROUP)]
    )
    weight3_ref[...] = weight3.astype(BF16)
    own = m0[:, :width] + m1[:, :width]
    cross = m2[:, :width] + m3[:, :width]
    out_ref[:half, :width] = jnp.where(node == 0, own, cross)
    out_ref[half:, :width] = jnp.where(node == 0, cross, own)
    for n in (0, 1):
        at = pl.ds(pl.multiple_of(n * rank + core * half, half), half)
        out_ref[n * half : (n + 1) * half, width : width + columns] = weight2_ref[at]
    out_ref[:, width + columns :] = weight3.astype(BF16)


def level3_kernel(info, own_ref, other_ref, table_ref, out_ref):
    half = out_ref.shape[0]
    rank = 2 * half
    columns = 64
    width = own_ref.shape[1] - 2 * columns
    core = info[CORE]
    index = node_picks(table_of(table_ref, info[AT]), rank, 3, 4 * core, 4)
    entry = index % rank
    at = index // rank * half + entry % half
    hit = at == iota((half, rank), 1)
    mine = (hit & (entry // half == core)).astype(BF16)
    theirs = (hit & (entry // half != core)).astype(BF16)
    out_ref[:, :width] = (mm(mine, own_ref[:, :width]) + mm(theirs, other_ref[:, :width])).astype(BF16)
    out_ref[:, width : width + columns] = own_ref[:half, width + columns :]
    out_ref[:, width + columns :] = own_ref[half:, width + columns :]


def level4_kernel(info, weight3_ref, next_ref, before_ref, pieces_ref, out_ref):
    rank, columns = weight3_ref.shape
    low = rank - (rank >> 3)
    own = weight3_ref[...]
    sibling = jnp.where(info[AT] % 2 == 0, next_ref[:, columns:], before_ref[:, columns:])
    both = in_order(info[AT] % 2, own, sibling)
    r4 = rank >> 4
    for i in range(GROUP):
        out_ref[i * r4 : (i + 1) * r4] = mm(piece(info, pieces_ref, i)[low : low + r4], both).astype(BF16)


def far_masks(info, mask_ref, slots, source, node):
    row = info[LEAF]

    def at(level, step):
        column = jnp.clip(jnp.where(step < 0, step + FWIN, step + FWIN - 1), 0, 2 * FWIN - 1)
        value = mask_ref[row, 2 * NWIN + (level - 1) * 2 * FWIN + column]
        return jnp.where((step != 0) & (jnp.abs(step) <= FWIN) & (source >= 0), value, 0)

    two = [at(2, 2 * source + h - node) for h in (0, 1)]
    return two + [at(3, source - info[AT]), at(4, source // 2 - info[AT] // 2)]


def far_weight_kernel(away, info, mask_ref, own_ref, other_ref, cross_ref, table_ref, w4_ref, out_ref, w3_s, w4_s):
    slots = len(away)
    rank = w3_s.shape[1]
    half = rank // 2
    columns = w3_s.shape[2]
    core, node = info[CORE], info[NODE]
    blocks = own_ref.shape[0]
    starts, at = [], 0
    for distance in away:
        starts.append(at)
        at += rank if distance == 1 else half
    r4 = rank >> 4
    for i, distance in enumerate(away):
        s = starts[i]
        if distance == 1:
            w3_s[i] = own_ref[s : s + rank, columns:]
        else:
            w3_s[i] = jnp.concatenate([own_ref[s : s + half, :columns], own_ref[s : s + half, columns:]])
    out_ref[...] = jnp.zeros_like(out_ref)
    for i, distance in enumerate(away):
        source = info[SLOT0 + i]
        sibling = info[SLOT0 + slots + i]
        second = source % 2
        first_slot = jnp.where(second == 0, i, sibling)
        second_slot = jnp.where(second == 0, sibling, i)
        mask2a, mask2b, mask3, mask4 = far_masks(info, mask_ref, slots, source, 2 * info[AT] + node)
        mask2a, mask2b, mask3, mask4 = [m.astype(F32).astype(BF16) for m in (mask2a, mask2b, mask3, mask4)]
        w3 = w3_s[i]
        low4 = bounds(rank)[3]
        index = []
        for slot in (first_slot, second_slot):
            table = table_of(table_ref, jnp.maximum(info[SLOT0 + slot], 0))
            for j in range(GROUP):
                index.append(entries(table, low4, low4 + r4, j))
        index = jnp.concatenate(index) - rank * second
        w4 = jnp.concatenate([w4_ref[first_slot], w4_ref[second_slot]])
        w4 = mm_tn((index == iota((rank, rank), 1)).astype(BF16), w4).astype(BF16)
        s = starts[i]
        if distance == 1:
            index3 = node_picks(table_of(table_ref, jnp.maximum(source, 0)), rank, 3, 0, GROUP)
            for k, side in enumerate((core, 1 - core)):
                lane = iota((rank, rank), 1)
                code = lane // half * rank + side * half + lane % half
                hit = (index3 == code).astype(BF16)
                ref = own_ref if k == 0 else other_ref
                at = k * blocks + s
                out_ref[at : at + half, :columns] = ref[s : s + half, :columns] * mask2a
                out_ref[at + half : at + rank, :columns] = ref[s + half : s + rank, :columns] * mask2b
                out_ref[at : at + rank, columns : 2 * columns] = mm_tn(hit, w3).astype(BF16) * mask3
                out_ref[at : at + rank, 2 * columns :] = mm_tn(hit, w4).astype(BF16) * mask4
        else:
            w4_s[...] = w4
            for k, side in enumerate((core, 1 - core)):
                rows = pl.ds(pl.multiple_of(side * half, half), half)
                at = k * blocks + s
                out_ref[at : at + half, columns : 2 * columns] = w3_s[i, rows] * mask3
                out_ref[at : at + half, 2 * columns :] = w4_s[rows] * mask4
    mask2 = jnp.where(
        node == 0, mask_ref[info[LEAF], 2 * NWIN + 6], mask_ref[info[LEAF], 2 * NWIN + 5]
    )
    base = 2 * blocks
    for k, side in enumerate((core, 1 - core)):
        rows = pl.ds(pl.multiple_of((1 - node) * rank + side * half, half), half)
        at = base + k * half
        out_ref[at : at + half, :columns] = cross_ref[rows] * mask2.astype(F32).astype(BF16)


def row_offset(block, scale_inv):
    squares = jnp.sum(jnp.square(block.astype(F32)), axis=1, keepdims=True)
    return (squares - block.shape[1]) * (0.5 * scale_inv)


def as_row(column):
    return jnp.transpose(jnp.broadcast_to(column, (column.shape[0], 128)))[0:1]


def kernel_block(targets, sources, source_row, scale_inv):
    products = mm_nt(targets, sources)
    return jnp.exp(products * scale_inv - row_offset(targets, scale_inv) - source_row).astype(BF16)


def far_kernel(away, scale_inv, info, mask_ref, x_ref, own_ref, other_ref, half_ref, half_other_ref, w_ref, out_ref):
    step = pl.program_id(0)
    last = pl.num_programs(0) - 1
    columns = out_ref.shape[1]
    width = own_ref.shape[1] - 2 * columns
    rank = own_ref.shape[0]
    half = rank // 2
    slots = len(away)
    blocks = last * rank

    def add(sources, weights):
        kernel = kernel_block(x_ref[:, :width], sources, as_row(row_offset(sources, scale_inv)), scale_inv)
        sums = mm(kernel, weights)
        out_ref[...] += sums[:, :columns] + sums[:, columns : 2 * columns] + sums[:, 2 * columns :]

    @pl.when(step == 0)
    def _():
        out_ref[...] = jnp.zeros_like(out_ref)

    node = 2 * info[AT] + info[NODE]
    need, per_block = [], []
    for i, distance in enumerate(away):
        masks = far_masks(info, mask_ref, slots, info[SLOT0 + i], node)
        value = masks[2] + masks[3] + (masks[0] + masks[1] if distance == 1 else 0)
        if distance == 1:
            per_block.append(value)
        else:
            need.append(value)
    per_block += [need[i] + need[i + 1] for i in range(0, len(need), 2)]
    wanted = jnp.zeros((), I32)
    for i, value in enumerate(per_block):
        wanted = jnp.where(step == i, value, wanted)

    @pl.when(wanted > 0)
    def _():
        for k, ref in enumerate((own_ref, other_ref)):
            at = pl.ds(pl.multiple_of(k * blocks + step * rank, rank), rank)
            add(ref[:, :width], w_ref[at])

    @pl.when(step == last)
    def _():
        at = pl.ds(pl.multiple_of((1 - info[NODE]) * half, half), half)
        sources = jnp.concatenate([half_ref[at, :width], half_other_ref[at, :width]])
        add(sources, w_ref[2 * blocks :])


def halves(value):
    half = value.shape[1] // 2
    return value[:, :half] + value[:, half:]


def masked(weights, first, second):
    lane = iota((1, weights.shape[1]), 1)
    return (weights.astype(F32) * jnp.where(lane < weights.shape[1] // 2, first, second)).astype(BF16)


def own_kernel(scale_inv, width, info, mask_ref, own_ref, other_ref, out_ref, back_ref, acc, row_own, row_other):
    step = pl.program_id(0)
    tile, columns = out_ref.shape
    rows = own_ref.shape[0]
    half = rows // 2
    last = width + columns

    @pl.when(step == 0)
    def _():
        acc[...] = jnp.zeros_like(acc)
        row_own[...] = as_row(row_offset(own_ref[:, :width], scale_inv))
        row_other[...] = as_row(row_offset(other_ref[:, :width], scale_inv))

    start = pl.multiple_of(step * tile, tile)
    here = pl.ds(start, tile)
    mine = own_ref[here, :width]
    kernel = kernel_block(mine, own_ref[:, :width], row_own[...], scale_inv)
    out_ref[...] = mm(kernel, own_ref[:, width:last])
    near = mask_ref[info[LEAF] // 2 * 2, NWIN] > 0

    def pair(count):
        kernel = kernel_block(mine, other_ref[:count, :width], row_other[:, :count], scale_inv)
        out_ref[...] += mm(kernel, other_ref[:count, width:last])
        acc[:count] += mm_tn(kernel, own_ref[here, width:last])

    @pl.when(near & (info[CORE] == 0))
    def _():
        pair(half)

    @pl.when(near & (info[CORE] == 1) & (start >= half))
    def _():
        pair(rows)

    @pl.when(step == pl.num_programs(0) - 1)
    def _():
        back_ref[...] = acc[...]


def leaf_weights(x_ref, width, columns, weight1, table_ref, leaf):
    rank = weight1.shape[0]
    where = tree_rows(x_ref[:, width + columns :])
    skeleton, pick1 = leaf_picks(table_of(table_ref, leaf // GROUP), rank, leaf % GROUP, where)
    spread = mm_tn(skeleton, mm_tn(pick1, weight1).astype(BF16)).astype(BF16)
    return jnp.concatenate([x_ref[:, width : width + columns], spread], axis=1)


def pair_kernel(
    scale_inv, width, behind, per_leaf, info, mask_ref, a1_ref, a2_ref, wa_ref, r_ref, wr_ref, init_ref, acc_in_ref, table_ref,
    out1_ref, out2_ref, back_ref, acc, row_r, a_w, r_w,
):
    step = pl.program_id(0)
    tile, columns = out1_ref.shape
    core = info[CORE]
    chip = info[LEAF] // 2
    leaves = mask_ref.shape[0]
    r_leaf = jnp.minimum(2 * chip + 2, leaves - 2) + core

    @pl.when(step == 0)
    def _():
        acc[...] = acc_in_ref[...]
        row_r[...] = as_row(row_offset(r_ref[:, :width], scale_inv))
        r_w[...] = leaf_weights(r_ref, width, columns, wr_ref[...], table_ref, r_leaf)

    second = step >= per_leaf
    side = jnp.where(second, 1 - core, core)
    a_leaf = jnp.maximum(2 * chip - 2 * behind, 0) + side
    there = (2 * chip + 2 < leaves) & (chip >= behind)
    distance = 2 + 2 * behind + core - side
    near = jnp.where(distance <= NWIN, mask_ref[a_leaf, jnp.minimum(NWIN - 1 + distance, 2 * NWIN - 1)], 0)
    level1 = 2 * NWIN
    far_out = mask_ref[a_leaf, level1 + FWIN + behind]
    far_back = mask_ref[r_leaf, level1 + FWIN - 1 - behind]
    used = (near + far_out + far_back > 0) & there
    near, far_out, far_back = near.astype(F32), far_out.astype(F32), far_back.astype(F32)

    def part(a_ref, out_ref, at):
        base = pl.multiple_of(at * tile, tile)

        @pl.when(used)
        def _():
            @pl.when(at == 0)
            def _():
                a_w[...] = leaf_weights(a_ref, width, columns, wa_ref[...], table_ref, a_leaf)

            sources = masked(r_w[...], near, far_out)
            for start in range(0, tile, CHUNK):
                rows = pl.ds(base + start, CHUNK)
                kernel = kernel_block(a_ref[rows, :width], r_ref[:, :width], row_r[...], scale_inv)
                sums = halves(mm(kernel, sources))
                if out_ref is out2_ref and not behind:
                    sums += init_ref[rows]
                out_ref[start : start + CHUNK] = sums.astype(out_ref.dtype)
                acc[...] += mm_tn(masked(a_w[rows], near, far_back), kernel)

        @pl.when(jnp.logical_not(used))
        def _():
            if out_ref is out2_ref and not behind:
                out_ref[...] = init_ref[pl.ds(base, tile)].astype(out_ref.dtype)
            else:
                out_ref[...] = jnp.zeros_like(out_ref)

    @pl.when(jnp.logical_not(second))
    def _():
        part(a1_ref, out1_ref, step)

    @pl.when(second)
    def _():
        part(a2_ref, out2_ref, step - per_leaf)

    @pl.when(step == pl.num_programs(0) - 1)
    def _():
        if behind:
            back_ref[...] = halves(jnp.transpose(acc[...])).astype(back_ref.dtype)
        else:
            back_ref[...] = acc[...]


def home_kernel(place_ref, got_ref, out_ref):
    rows = got_ref.shape[0]
    pick = (iota((rows, rows), 0) == place_ref[...]).astype(BF16)
    out_ref[...] = mm_tn(got_ref[...], pick)


def local(
    points, weights, tree_slot, leaf_interp, skel_leaf, merge_interp, merge_index, near_mask, far_mask
):
    leaves = lax.axis_size("leaf")
    groups = leaves // GROUP
    rows, width = points.shape
    columns = weights.shape[1]
    per_peer = rows // leaves
    rank = skel_leaf.shape[1]
    lanes = 4 * rank // per_peer
    wide = width + -(-(columns + 16 + lanes) // 128) * 128
    half = rank // 2
    scale_inv = 1.0 / (1.75 * math.sqrt(width))
    message = width + 2 * columns
    slots = slot_sources(groups)
    away = [a for a, _ in slots]

    def prefetch(count, grid, ins, outs, scratch=()):
        return pltpu.PrefetchScalarGridSpec(
            num_scalar_prefetch=count, grid=grid, in_specs=ins, out_specs=outs, scratch_shapes=scratch
        )

    spare = 2 * rank - rank - merge_index.shape[1]
    picks = jnp.concatenate([skel_leaf, merge_index], axis=1)
    table = jnp.concatenate(
        [picks // 32, far_mask.reshape(1, -1), picks % 32, near_mask, jnp.zeros((1, spare - near_mask.shape[1]), I32)],
        axis=1,
    )
    table = table.astype(F32).astype(BF16).reshape(per_peer, lanes)

    send, place = call(
        functools.partial(sort_kernel, rows, per_peer, leaves, lanes),
        pl.GridSpec(
            grid=(4,),
            in_specs=[whole((1, rows)), whole((rows, width)), whole((columns, rows)), whole((per_peer, lanes))],
            out_specs=[pl.BlockSpec((rows // 4, wide), lambda i: (i, 0)), whole((1, rows))],
            scratch_shapes=[pltpu.VMEM((1, rows), I32)],
        ),
        shapes(((rows, wide), BF16), ((1, rows), I32)),
    )(tree_slot.reshape(1, rows), points, weights.T, table)
    got = lax.all_to_all(send, "leaf", split_axis=0, concat_axis=0, tiled=True)

    device = lax.axis_index("leaf")
    leaf = leaf_of_device(device)
    group = leaf // GROUP
    source = jnp.asarray([s for _, s in slots], I32)[:, group]
    sibling = jnp.argmax((source[None, :] == (source ^ 1)[:, None]).astype(I32), axis=1).astype(I32)
    info = jnp.concatenate(
        [
            jnp.stack([leaf, leaf % 2, leaf // 2 % 4, leaf // 4 % 2, group, device // 2 % 4]).astype(I32),
            source,
            sibling,
        ]
    )
    interp_in, merge_in, _ = lax.optimization_barrier((leaf_interp[0], merge_interp[0], place))
    interp = lax.ppermute(interp_in, "leaf", [(i, device_of_leaf(i)) for i in range(leaves)])
    near_pieces = jnp.stack(
        [merge_in]
        + [lax.ppermute(merge_in, "leaf", [(i, i ^ (2 * k)) for i in range(leaves)]) for k in (1, 2, 3)]
    )
    pieces = jnp.stack([near_pieces, lax.ppermute(near_pieces, "leaf", [(i, i ^ 1) for i in range(leaves)])])
    piece_shape = pieces.shape

    coded = got[:, wide - lanes :].reshape(leaves, 4 * rank).astype(F32)
    tables = coded[:, : 2 * rank] * 32.0 + coded[:, 2 * rank :]
    mask_at = rank + merge_index.shape[1]
    masks = jnp.concatenate(
        [
            coded[:, 2 * rank + mask_at : 2 * rank + mask_at + 2 * NWIN],
            coded[:, mask_at : mask_at + LEVELS * 2 * FWIN],
        ],
        axis=1,
    ).astype(I32)
    table_shape = tables.shape

    other = move(got, lambda i: i ^ 1)
    behind = move(got, lambda i: i + 2)
    ahead = move(got, lambda i: i - 2)

    give, keep, weight0 = call(
        level0_kernel,
        prefetch(1, (), [whole((rows, wide)), whole((rank, rows)), whole(table_shape)],
                 [whole((half, message)), whole((half, width)), whole((rank, columns))]),
        shapes(((half, message), BF16), ((half, width), BF16), ((rank, columns), BF16)),
    )(info, got, interp, tables)
    sent, weight1 = call(
        level1_kernel,
        prefetch(1, (), [whole((half, message)), whole((half, width)), whole((rank, columns)), whole(piece_shape)],
                 [whole((half, message)), whole((rank, columns))]),
        shapes(((half, message), BF16), ((rank, columns), BF16)),
    )(info, move(give, lambda i: i ^ 1), keep, weight0, pieces)
    behind1 = move(weight1, lambda i: i + 2)
    ahead1 = move(weight1, lambda i: i - 2)
    half2, weight2, weight3 = call(
        level23_kernel,
        prefetch(1, (), [whole((half, message))] * 4 + [whole(piece_shape)],
                 [whole((rank, message)), whole((2 * rank, columns)), whole((rank, columns))],
                 [pltpu.VMEM((4 * rank, columns), BF16)]),
        shapes(((rank, message), BF16), ((2 * rank, columns), BF16), ((rank, columns), BF16)),
    )(info, sent, *[move(sent, lambda i, k=k: i ^ (2 * k)) for k in (1, 2, 3)], pieces)
    half2_other = move(half2, lambda i: i ^ 1)
    half3 = call(
        level3_kernel,
        prefetch(1, (), [whole((rank, message))] * 2 + [whole(table_shape)], whole((half, message))),
        jax.ShapeDtypeStruct((half, message), BF16),
    )(info, half2, half2_other, tables)
    far_parts = [send_slot(half2 if a == 1 else half3, s) for a, s in slots]
    extra = pl.BlockSpec((rank, 2 * columns), lambda *_: (0, width // (2 * columns)))
    half4 = call(
        level4_kernel,
        prefetch(1, (1,), [whole((rank, columns)), extra, extra, whole(piece_shape)], whole((half, columns))),
        jax.ShapeDtypeStruct((half, columns), BF16),
    )(info, weight3, far_parts[0], far_parts[1], pieces)
    weight4 = jnp.stack([send_slot(half4, s) for _, s in slots])
    far_own = jnp.concatenate(far_parts)
    far_other = move(far_own, lambda i: i ^ 1)

    tile = rows // 4
    own_sum, other_sum = call(
        functools.partial(own_kernel, scale_inv, width),
        prefetch(2, (4,), [whole((rows, wide))] * 2,
                 [pl.BlockSpec((tile, columns), lambda i, *_: (i, 0)), whole((rows, columns))],
                 [pltpu.VMEM((rows, columns), F32), pltpu.VMEM((1, rows), F32), pltpu.VMEM((1, rows), F32)]),
        shapes(((rows, columns), F32), ((rows, columns), F32)),
        flops=3 * rows * rows * wide, exps=3 * rows * rows // 2, moved=4 * rows * wide,
    )(info, masks, got, other)

    blocks = far_own.shape[0] // rank
    far_rows = (2 * blocks + 1) * rank
    extra = pl.BlockSpec((blocks * rank, 2 * columns), lambda *_: (0, width // (2 * columns)))
    far_w = call(
        functools.partial(far_weight_kernel, away),
        prefetch(2, (1,), [extra, extra, whole((2 * rank, columns)), whole(table_shape), whole(weight4.shape)],
                 whole((far_rows, 3 * columns)),
                 [pltpu.VMEM((len(slots), rank, columns), BF16), pltpu.VMEM((rank, columns), BF16)]),
        jax.ShapeDtypeStruct((far_rows, 3 * columns), BF16),
    )(info, masks, far_own, far_other, weight2, tables, weight4)
    block = pl.BlockSpec((rank, message), lambda i, *_: (jnp.minimum(i, blocks - 1), 0))
    far_sum = call(
        functools.partial(far_kernel, away, scale_inv),
        prefetch(2, (blocks + 1,),
                 [whole((rows, wide)), block, block, whole((rank, message)), whole((rank, message)), whole((far_rows, 3 * columns))],
                 whole((rows, columns))),
        jax.ShapeDtypeStruct((rows, columns), F32),
        flops=2 * rows * far_rows * wide, exps=rows * far_rows, moved=4 * rows * wide,
    )(info, masks, got, far_own, far_other, half2, half2_other, far_w)

    tile = rows // 2
    per_leaf = rows // tile

    def pairs(behind_chip, a1, a2, a_w, init, acc_in, out_kinds):
        back = ((rows, columns), BF16) if behind_chip else ((2 * columns, rows), F32)
        return call(
            functools.partial(pair_kernel, scale_inv, width, behind_chip, per_leaf),
            prefetch(2, (2 * per_leaf,),
                     [whole((rows, wide))] * 2 + [whole((rank, columns)), whole((rows, wide)), whole((rank, columns)),
                      whole((rows, columns)), whole((2 * columns, rows)), whole(table_shape)],
                     [pl.BlockSpec((tile, columns), lambda i, *_: (jnp.minimum(i, per_leaf - 1), 0)),
                      pl.BlockSpec((tile, columns), lambda i, *_: (jnp.maximum(i - per_leaf, 0), 0)),
                      whole(back[0])],
                     [pltpu.VMEM((2 * columns, rows), F32), pltpu.VMEM((1, rows), F32),
                      pltpu.VMEM((rows, 2 * columns), BF16), pltpu.VMEM((rows, 2 * columns), BF16)]),
            shapes(((rows, columns), out_kinds[0]), ((rows, columns), out_kinds[1]), back),
            flops=4 * rows * rows * wide, exps=2 * rows * rows, moved=8 * rows * wide,
        )(info, masks, a1, a2, a_w, ahead, ahead1, init, acc_in, tables)

    zero = jnp.zeros((2 * columns, rows), F32)
    next_own, next_other, acc = pairs(0, got, other, weight1, other_sum, zero, (F32, BF16))
    behind_other = move(behind, lambda i: i ^ 1)
    behind_sum, behind_other_sum, ahead_sum = pairs(
        1, behind, behind_other, behind1, other_sum, acc, (BF16, BF16)
    )

    own = own_sum + far_sum + next_own
    own = own + move(next_other, lambda i: i ^ 1)
    own = own + move(behind_sum, lambda i: i - 2)
    own = own + move(behind_other_sum, lambda i: (i ^ 1) - 2)
    own = own + move(ahead_sum, lambda i: i + 2)
    home = lax.all_to_all(own.astype(BF16), "leaf", split_axis=0, concat_axis=0, tiled=True)
    return call(
        home_kernel,
        pl.GridSpec(grid=(), in_specs=[whole((1, rows)), whole((rows, columns))], out_specs=whole((columns, rows))),
        jax.ShapeDtypeStruct((columns, rows), F32),
    )(place, home).T


def solution(mesh):
    placed = (
        P("leaf", None),
        P("leaf", None),
        P("leaf"),
        P("leaf", None, None),
        P("leaf", None),
        P("leaf", None, None),
        P("leaf", None),
        P("leaf", None),
        P("leaf", None, None),
    )
    return jax.shard_map(
        local, mesh=mesh, in_specs=placed, out_specs=P("leaf", None), check_vma=False
    )
```

```python
import functools
import math

import jax
import jax.numpy as jnp
from jax import lax
from jax.experimental import pallas as pl
from jax.experimental.pallas import tpu as pltpu
from jax.sharding import PartitionSpec as P

LEVELS = 4
NWIN = 4
FWIN = 2
GROUP = 8
BF16 = jnp.bfloat16
F32 = jnp.float32
I32 = jnp.int32
NT = (((1,), (1,)), ((), ()))
TN = (((0,), (0,)), ((), ()))
CHUNK = 256


def call(kernel, grid_spec, out_shape, vmem=40, flops=0):
    return pl.pallas_call(
        kernel,
        grid_spec=grid_spec,
        out_shape=out_shape,
        compiler_params=pltpu.CompilerParams(vmem_limit_bytes=vmem * 1024 * 1024),
        cost_estimate=pl.CostEstimate(flops=flops, bytes_accessed=0, transcendentals=0),
    )


def after(value, *others):
    return lax.optimization_barrier((value, *others))[0]


def whole(shape):
    return pl.BlockSpec(shape, lambda *_: (0,) * len(shape))


def shapes(*specs):
    return [jax.ShapeDtypeStruct(shape, kind) for shape, kind in specs]


def mm(a, b):
    return jnp.dot(a, b, preferred_element_type=F32)


def mm_nt(a, b):
    return lax.dot_general(a, b, NT, preferred_element_type=F32)


def mm_tn(a, b):
    return lax.dot_general(a, b, TN, preferred_element_type=F32)


def device_of_leaf(leaf):
    group, chip = leaf // GROUP, (leaf // 2) % 4
    return group * GROUP + ((chip ^ (chip >> 1)) ^ ((group & 1) * 2)) * 2 + leaf % 2


def leaf_of_device(device):
    group, chip = device // GROUP, (device // 2) % 4 ^ ((device // GROUP & 1) * 2)
    return group * GROUP + (chip ^ (chip >> 1)) * 2 + device % 2


def move(value, target_of_leaf):
    leaves = lax.axis_size("leaf")
    pairs = []
    for leaf in range(leaves):
        target = target_of_leaf(leaf)
        if 0 <= target < leaves:
            pairs.append((device_of_leaf(leaf), device_of_leaf(target)))
    return lax.ppermute(value, "leaf", pairs)


def slot_sources(groups):
    slots = []
    for away in range(1, min(6, groups)):
        merge = away > 1 and groups <= 2 * away
        for steps in [(away, -away)] if merge else [(away,), (-away,)]:
            found = [[g + s for s in steps if 0 <= g + s < groups] for g in range(groups)]
            slots.append((away, [f[0] if f else -1 for f in found]))
    return slots


def send_each(value, source):
    pairs = [
        (device_of_leaf(s * GROUP + i), device_of_leaf(g * GROUP + i))
        for g, s in enumerate(source)
        if s >= 0
        for i in range(GROUP)
    ]
    return lax.ppermute(value, "leaf", pairs)


LEAF, CORE, CHIP, NODE, AT, PHYS = range(6)
SLOT0 = 6


def iota(shape, dim):
    return lax.broadcasted_iota(I32, shape, dim)


def sort_kernel(
    rows, per_peer, leaves, lanes, slot_ref, points_ref, weights_ref, skel_ref, merge_ref, near_ref, far_ref,
    send_ref, place_ref, place_s, table_s,
):
    step = pl.program_id(0)
    block = send_ref.shape[0]
    slot = slot_ref[...]

    @pl.when(step == 0)
    def _():
        dest = device_of_leaf(slot // rows)
        at = (iota((leaves, rows), 0) == dest).astype(BF16)
        earlier = (iota((rows, rows), 0) < iota((rows, rows), 1)).astype(BF16)
        rank = jnp.sum(at.astype(F32) * mm(at, earlier), axis=0, keepdims=True)
        place_s[...] = dest * per_peer + rank.astype(I32)
        place_ref[...] = place_s[...]
        skel, merge = skel_ref[...], merge_ref[...]
        end = skel.shape[1] + merge.shape[1]
        second = 2 * skel.shape[1]
        table = jnp.zeros((per_peer, lanes), F32)
        for base, values in (
            (0, skel // 32),
            (skel.shape[1], merge // 32),
            (end, far_ref[...]),
            (second, skel % 32),
            (second + skel.shape[1], merge % 32),
            (second + end, near_ref[...]),
        ):
            count = values.shape[1]
            row = (base + iota((per_peer, count), 1)) // lanes == iota((per_peer, count), 0)
            spread = jnp.where(row, values, 0).astype(F32).astype(BF16)
            fold = ((base + iota((count, lanes), 0)) % lanes == iota((count, lanes), 1)).astype(BF16)
            table += mm(spread, fold)
        table_s[...] = table.astype(BF16)

    pick = (iota((block, rows), 0) + step * block == place_s[...]).astype(BF16)
    width, columns = points_ref.shape[1], weights_ref.shape[0]
    wide = send_ref.shape[1]
    inner = slot % rows
    row = iota((16, rows), 0)
    parts = jnp.where(row == 0, inner // 32, jnp.where(row == 1, inner % 32, 0)).astype(F32).astype(BF16)
    send_ref[:, :width] = mm(pick, points_ref[...]).astype(BF16)
    send_ref[:, width : width + columns] = mm_nt(pick, weights_ref[...]).astype(BF16)
    send_ref[:, width + columns : width + columns + 16] = mm_nt(pick, parts).astype(BF16)
    send_ref[:, width + columns + 16 : wide - lanes] = jnp.zeros((block, wide - lanes - width - columns - 16), BF16)
    spread = (iota((block, per_peer), 0) % per_peer == iota((block, per_peer), 1)).astype(BF16)
    send_ref[:, wide - lanes :] = mm(spread, table_s[...]).astype(BF16)


def tree_rows(extra):
    lane = iota((16, extra.shape[1]), 1)
    parts = jnp.where(lane == 0, 32.0, jnp.where(lane == 1, 1.0, 0.0)).astype(BF16)
    return mm_nt(parts, extra)[0:1].astype(I32)


def entries(table, low, high, leaf):
    lane = iota((1, GROUP), 1)
    return jnp.sum(jnp.where(lane == leaf, table[low:high], 0.0), axis=1, keepdims=True).astype(I32)


def table_of(table_ref, group):
    return jnp.transpose(table_ref[pl.ds(pl.multiple_of(group * GROUP, GROUP), GROUP)])


def bounds(rank):
    ends = [rank]
    for level in range(1, LEVELS + 1):
        ends.append(ends[-1] + (rank >> level))
    return ends


def node_picks(table, rank, level, first, count):
    low, high = bounds(rank)[level - 1 : level + 1]
    rows = high - low
    several = jnp.concatenate([table[low:high]] * count)
    lane = iota((1, GROUP), 1) - first
    row = iota((rows * count, 1), 0) // rows
    return jnp.sum(jnp.where(lane == row, several, 0.0), axis=1, keepdims=True).astype(I32)


def leaf_picks(table, rank, leaf, where):
    skeleton = (entries(table, 0, rank, leaf) == where).astype(BF16)
    index1 = node_picks(table, rank, 1, leaf // 2 * 2, 2) - rank * (leaf % 2)
    return skeleton, (index1 == iota((rank, rank), 1)).astype(BF16)


def level0_kernel(info, got_ref, interp_ref, table_ref, give_ref, keep_ref, weight0_ref):
    rank, columns = weight0_ref.shape
    rows, width = got_ref.shape[0], keep_ref.shape[1]
    half = rank // 2
    where = tree_rows(got_ref[:, width + columns :])
    order = (iota((rows, rows), 0) == where).astype(BF16)
    weights = mm(order, got_ref[:, width : width + columns]).astype(BF16)
    weight0 = mm(interp_ref[...], weights).astype(BF16)
    weight0_ref[...] = weight0
    table = table_of(table_ref, info[AT])
    skeleton, pick1 = leaf_picks(table, rank, info[LEAF] % GROUP, where)
    level0 = mm(skeleton, got_ref[:, :width]).astype(BF16)
    level1 = mm(pick1, level0).astype(BF16)
    core = info[CORE]

    def part(side):
        index2 = node_picks(table, rank, 2, 4 * info[NODE] + 2 * side, 2) - rank * (info[CHIP] % 2)
        return mm((index2 == iota((half, rank), 1)).astype(BF16), level1).astype(BF16)

    keep_ref[...] = part(core)
    give_ref[:, :width] = part(1 - core)
    give_ref[:, width : width + columns] = weight0[:half]
    give_ref[:, width + columns :] = weight0[half:]


def piece(info, pieces_ref, leaf):
    return pieces_ref.at[leaf % 2 ^ info[CORE], leaf // 2 ^ info[PHYS]]


def in_order(core, mine, other):
    return jnp.where(core == 0, jnp.concatenate([mine, other]), jnp.concatenate([other, mine]))


def level1_kernel(info, other_ref, keep_ref, weight0_ref, own_piece_ref, other_piece_ref, out_ref, weight1_ref):
    rank, columns = weight1_ref.shape
    half, width = keep_ref.shape
    core = info[CORE]
    other0 = jnp.concatenate([other_ref[:, width : width + columns], other_ref[:, width + columns :]])
    both0 = in_order(core, weight0_ref[...], other0)
    weight1 = in_order(core, mm(own_piece_ref[...], both0), mm(other_piece_ref[...], both0)).astype(BF16)
    weight1_ref[...] = weight1
    out_ref[:, :width] = keep_ref[...] + other_ref[:, :width]
    out_ref[:, width : width + columns] = weight1[:half]
    out_ref[:, width + columns :] = weight1[half:]


def level23_kernel(info, m0, m1, m2, m3, pieces_ref, out_ref, weight2_ref, weight3_ref, w1_s):
    half = m0.shape[0]
    rank = 2 * half
    columns = weight2_ref.shape[1]
    width = m0.shape[1] - 2 * columns
    core, chip, node = info[CORE], info[CHIP], info[NODE]
    for k, message in enumerate((m0, m1, m2, m3)):
        at = pl.ds(pl.multiple_of((chip ^ k) * rank, rank), rank)
        w1_s[at] = jnp.concatenate([message[:, width : width + columns], message[:, width + columns :]])
    r2, r3 = rank >> 2, rank >> 3
    for n in (0, 1):
        for i in range(4):
            rows2 = piece(info, pieces_ref, 4 * n + i)[:r2]
            at = n * rank + i * r2
            weight2_ref[at : at + r2] = mm(rows2, w1_s[2 * n * rank : 2 * (n + 1) * rank]).astype(BF16)
    low = r2
    weight3 = jnp.concatenate(
        [mm(piece(info, pieces_ref, i)[low : low + r3], weight2_ref[...]) for i in range(GROUP)]
    )
    weight3_ref[...] = weight3.astype(BF16)
    own = m0[:, :width] + m1[:, :width]
    cross = m2[:, :width] + m3[:, :width]
    out_ref[:half, :width] = jnp.where(node == 0, own, cross)
    out_ref[half:, :width] = jnp.where(node == 0, cross, own)
    for n in (0, 1):
        at = pl.ds(pl.multiple_of(n * rank + core * half, half), half)
        out_ref[n * half : (n + 1) * half, width : width + columns] = weight2_ref[at]
    out_ref[:, width + columns :] = weight3.astype(BF16)


def level3_kernel(info, own_ref, other_ref, table_ref, out_ref):
    half = out_ref.shape[0]
    rank = 2 * half
    columns = 64
    width = own_ref.shape[1] - 2 * columns
    core = info[CORE]
    index = node_picks(table_of(table_ref, info[AT]), rank, 3, 4 * core, 4)
    entry = index % rank
    at = index // rank * half + entry % half
    hit = at == iota((half, rank), 1)
    mine = (hit & (entry // half == core)).astype(BF16)
    theirs = (hit & (entry // half != core)).astype(BF16)
    out_ref[:, :width] = (mm(mine, own_ref[:, :width]) + mm(theirs, other_ref[:, :width])).astype(BF16)
    out_ref[:, width : width + columns] = own_ref[:half, width + columns :]
    out_ref[:, width + columns :] = own_ref[half:, width + columns :]


def level4_kernel(info, weight3_ref, next_ref, before_ref, pieces_ref, out_ref):
    rank, columns = weight3_ref.shape
    low = (rank >> 2) + (rank >> 3)
    own = weight3_ref[...]
    sibling = jnp.where(info[AT] % 2 == 0, next_ref[:, columns:], before_ref[:, columns:])
    both = in_order(info[AT] % 2, own, sibling)
    r4 = rank >> 4
    for i in range(GROUP):
        out_ref[i * r4 : (i + 1) * r4] = mm(piece(info, pieces_ref, i)[low : low + r4], both).astype(BF16)


def far_masks(info, mask_ref, leaf, source):
    def at(level, step):
        column = jnp.clip(jnp.where(step < 0, step + FWIN, step + FWIN - 1), 0, 2 * FWIN - 1)
        value = mask_ref[leaf, 2 * NWIN + (level - 1) * 2 * FWIN + column]
        return jnp.where((step != 0) & (jnp.abs(step) <= FWIN) & (source >= 0), value, 0)

    node = 2 * info[AT] + info[NODE]
    return [
        at(2, 2 * source - node),
        at(2, 2 * source + 1 - node),
        at(3, source - info[AT]),
        at(4, source // 2 - info[AT] // 2),
    ]


def row_offset(block, scale_inv):
    squares = jnp.sum(jnp.square(block.astype(F32)), axis=1, keepdims=True)
    return (squares - block.shape[1]) * (0.5 * scale_inv)


def as_row(column):
    return jnp.transpose(jnp.broadcast_to(column, (column.shape[0], 128)))[0:1]


def kernel_block(targets, target_column, sources, source_row, scale_inv):
    products = mm_nt(targets, sources)
    return jnp.exp(products * scale_inv - target_column - source_row).astype(BF16)


def as_bf16(value):
    return value.astype(F32).astype(BF16)


def far_kernel(away, parents, scale_inv, width, info, mask_ref, x1_ref, x2_ref, c1_ref, c2_ref, half_ref, w2_ref, w4_ref, table_ref,
               init1_ref, init2_ref, pairs_ref, *rest):
    parts, (result, out1_ref, out2_ref, w_s, w4_s) = rest[: len(away)], rest[len(away) :]
    columns = out1_ref.shape[1]
    half = half_ref.shape[0] // 2
    rank = 2 * half
    core, node = info[CORE], info[NODE]
    offsets = (c1_ref, c2_ref)
    out1_ref[...] = init1_ref[...]
    out2_ref[...] = init2_ref[...]
    side = [info[LEAF], info[LEAF] ^ 1]

    def run(sources, weights, masks):
        row = as_row(row_offset(sources, scale_inv))
        count = weights.shape[0] // 2
        for x_ref, offset, out_ref, mask in zip((x1_ref, x2_ref), offsets, (out1_ref, out2_ref), masks, strict=True):
            scaled = jnp.concatenate(
                [
                    jnp.concatenate([weights[i * count : (i + 1) * count, j * columns : (j + 1) * columns] * as_bf16(mask[i][j])
                                     for j in range(3)], axis=1)
                    for i in (0, 1)
                ]
            )
            kernel = kernel_block(x_ref[:, :width], offset[...], sources, row, scale_inv)
            sums = mm(kernel, scaled)
            out_ref[...] += sums[:, :columns] + sums[:, columns : 2 * columns] + sums[:, 2 * columns :]

    def spread_of(i, distance, part, source):
        if distance == 1:
            w3 = part[:, width + columns :]
        else:
            w3 = jnp.concatenate([part[:, width : width + columns], part[:, width + columns :]])
        step = source // 2 - info[AT] // 2
        parent = 0 if parents == 1 else jnp.clip(jnp.where(step < 0, step + FWIN, step + FWIN - 1), 0, 2 * FWIN - 1)
        even = source - source % 2
        index = [node_picks(table_of(table_ref, group), rank, 4, 0, GROUP) for group in (even, even + 1)]
        index = jnp.concatenate(index) - rank * (source % 2)
        w4 = in_order(info[AT] % 2, w4_ref[2 * parent], w4_ref[2 * parent + 1])
        w4 = mm_tn((index == iota((rank, rank), 1)).astype(BF16), w4).astype(BF16)
        if distance == 1:
            index3 = node_picks(table_of(table_ref, source), rank, 3, 0, GROUP)
            lane = iota((rank, rank), 1)
            hit = (index3 == lane // half * rank + core * half + lane % half).astype(BF16)
            both = mm_tn(hit, jnp.concatenate([w3, w4], axis=1)).astype(BF16)
            return jnp.concatenate([part[:, width : width + columns], both], axis=1)
        w4_s[:, :columns] = w3
        w4_s[:, columns:] = w4
        rows = pl.ds(pl.multiple_of(core * half, half), half)
        return jnp.concatenate([jnp.zeros((half, columns), BF16), w4_s[rows]], axis=1)

    zero = jnp.zeros((), I32)
    joined = away.index(2) if 2 in away else -1
    for i, distance in enumerate(away):
        source = info[SLOT0 + i]
        known = jnp.maximum(source, 0)
        masks = [far_masks(info, mask_ref, leaf, source) for leaf in side]
        if distance == 1:
            used = sum(sum(m) for m in masks) > 0
            lists = [[[m[0], m[2], m[3]], [m[1], m[2], m[3]]] for m in masks]
        else:
            used = sum(m[2] + m[3] for m in masks) > 0
            lists = [[[zero, m[2], m[3]]] * 2 for m in masks]
        if i != joined:

            @pl.when(used)
            def _(i=i, distance=distance, known=known, lists=lists):
                run(parts[i][:, :width], spread_of(i, distance, parts[i], known), lists)

            continue
        cross = pl.ds(pl.multiple_of((1 - node) * half, half), half)
        column = jnp.where(node == 0, 2 * NWIN + 2 * FWIN + FWIN, 2 * NWIN + 2 * FWIN + FWIN - 1)
        w_s[:half, :columns] = w2_ref[pl.ds(pl.multiple_of((1 - node) * rank + core * half, half), half)]
        w_s[:half, columns:] = jnp.zeros((half, 2 * columns), BF16)
        w_s[half:] = spread_of(i, distance, parts[i], known)
        lists = [
            [[mask_ref[leaf, column], zero, zero], entry[0]] for leaf, entry in zip(side, lists, strict=True)
        ]
        run(jnp.concatenate([half_ref[cross, :width], parts[i][:, :width]]), w_s[...], lists)
    result[:, :columns] = out1_ref[...].astype(BF16)
    result[:, columns : 2 * columns] = out2_ref[...].astype(BF16)
    result[:, 2 * columns :] = pairs_ref[...]


def halves(value):
    half = value.shape[1] // 2
    return value[:, :half] + value[:, half:]


def masked(weights, first, second):
    lane = iota((1, weights.shape[1]), 1)
    return (weights.astype(F32) * jnp.where(lane < weights.shape[1] // 2, first, second)).astype(BF16)


def own_kernel(scale_inv, width, info, mask_ref, own_ref, other_ref, out_ref, back_ref, column_ref, column_other_ref):
    rows, columns = out_ref.shape
    half = rows // 2
    last = width + columns
    own_column = row_offset(own_ref[:, :width], scale_inv)
    other_column = row_offset(other_ref[:, :width], scale_inv)
    column_ref[...] = own_column
    column_other_ref[...] = other_column
    kernel = kernel_block(own_ref[:, :width], own_column, own_ref[:, :width], as_row(own_column), scale_inv)
    out_ref[...] = mm(kernel, own_ref[:, width:last])
    back_ref[...] = jnp.zeros_like(back_ref)
    near = mask_ref[info[LEAF] // 2 * 2, NWIN] > 0

    def pair(first, count):
        mine = own_ref[first:, :width]
        theirs = other_ref[:count, :width]
        kernel = kernel_block(mine, own_column[first:], theirs, as_row(other_column[:count]), scale_inv)
        out_ref[first:] += mm(kernel, other_ref[:count, width:last])
        back_ref[:count] = mm_tn(kernel, own_ref[first:, width:last])

    @pl.when(near & (info[CORE] == 0))
    def _():
        pair(0, half)

    @pl.when(near & (info[CORE] == 1))
    def _():
        pair(half, rows)


def leaf_weights(x, width, columns, weight1, table_ref, leaf):
    rank = weight1.shape[0]
    half = rank // 2
    extra = x[:, width:]
    row = iota((extra.shape[1], 128), 0)
    parts = jnp.where(row == columns, 32.0, jnp.where(row == columns + 1, 1.0, 0.0)).astype(BF16)
    where = mm(extra, parts)
    group = table_ref[pl.ds(pl.multiple_of(leaf // GROUP * GROUP, GROUP), GROUP), : rank + half]
    at = iota((GROUP, 1), 0)

    def of(index, low, high):
        return jnp.sum(jnp.where(at == index, group[:, low:high], 0.0), axis=0, keepdims=True)

    base = leaf % GROUP // 2 * 2
    index1 = jnp.concatenate([of(base + i, rank, rank + half) for i in (0, 1)], axis=1)
    index1 = index1 - (leaf % 2 * rank).astype(F32)
    pick1 = (iota((rank, rank), 0).astype(F32) == index1).astype(BF16)
    level0 = mm(pick1, weight1).astype(BF16)
    skeleton = of(leaf % GROUP, 0, rank)
    hit = [(where == skeleton[:, i : i + 128]).astype(BF16) for i in range(0, rank, 128)]
    spread = mm(jnp.concatenate(hit, axis=1), level0).astype(BF16)
    return jnp.concatenate([extra[:, :columns], spread], axis=1)


def pair_masks(info, mask_ref):
    core = info[CORE]
    chip = info[LEAF] // 2
    leaves = mask_ref.shape[0]
    r_leaf = jnp.minimum(2 * chip + 2, leaves - 2) + core
    level1 = 2 * NWIN
    masks, names = [], []
    for behind in (0, 1):
        for side in (core, 1 - core):
            leaf = jnp.maximum(2 * chip - 2 * behind, 0) + side
            there = (2 * chip + 2 < leaves) & (chip >= behind)
            distance = 2 + 2 * behind + core - side
            near = jnp.where(distance <= NWIN, mask_ref[leaf, jnp.minimum(NWIN - 1 + distance, 2 * NWIN - 1)], 0)
            values = (near, mask_ref[leaf, level1 + FWIN + behind], mask_ref[r_leaf, level1 + FWIN - 1 - behind])
            masks.append([jnp.where(there, v, 0) for v in values])
            names.append(leaf)
    return masks, names, r_leaf


def pair_sums(scale_inv, width, jobs, r, r_row, r_weights, acc):
    sums = []
    for mask, ref, column, weights in jobs:
        near, far_out, far_back = (m.astype(F32) for m in mask)
        kernel = kernel_block(ref[:, :width], column, r, r_row, scale_inv)
        sums.append(halves(mm(kernel, masked(r_weights, near, far_out))))
        acc += mm_tn(masked(weights, near, far_back), kernel)
    return sums, acc


def next_kernel(scale_inv, width, info, mask_ref, q1, q2, c1, c2, r, w_q, w_r, init1, init2, table_ref,
                out1, out2, acc, wr, rr):
    columns = out1.shape[1]
    masks, names, r_leaf = pair_masks(info, mask_ref)
    weights = [
        leaf_weights(ref, width, columns, w_q[...], table_ref, leaf) for ref, leaf in zip((q1, q2), names[:2], strict=True)
    ]
    wr[...] = leaf_weights(r, width, columns, w_r[...], table_ref, r_leaf)
    r_column = row_offset(r[:, :width], scale_inv)
    r_row = as_row(r_column)
    rr[...] = r_row
    jobs = zip(masks[:2], (q1, q2), (c1[...], c2[...]), weights, strict=True)
    sums, total = pair_sums(scale_inv, width, jobs, r[:, :width], r_row, wr[...], jnp.zeros(acc.shape, F32))
    out1[...] = init1[...] + sums[0]
    out2[...] = init2[...] + sums[1]
    acc[...] = total


def before_kernel(scale_inv, width, info, mask_ref, p1, p2, r, w_p, acc, wr, rr, table_ref, result):
    columns = result.shape[1] // 3
    masks, names, _ = pair_masks(info, mask_ref)
    weights = [
        leaf_weights(ref, width, columns, w_p[...], table_ref, leaf) for ref, leaf in zip((p1, p2), names[2:], strict=True)
    ]
    offsets = [row_offset(ref[:, :width], scale_inv) for ref in (p1, p2)]
    jobs = zip(masks[2:], (p1, p2), offsets, weights, strict=True)
    sums, total = pair_sums(scale_inv, width, jobs, r[:, :width], rr[...], wr[...], acc[...])
    for i, value in enumerate((*sums, halves(jnp.transpose(total)))):
        result[:, i * columns : (i + 1) * columns] = value.astype(BF16)


def home_kernel(leaves, place_ref, got_ref, out_ref, sum_s):
    columns, rows = out_ref.shape
    count = rows // leaves
    for leaf in range(leaves):
        sources = (leaf, leaf ^ 1, leaf + 2, (leaf ^ 1) + 2, leaf - 2)
        total = 0.0
        for part, source in enumerate(sources):
            if 0 <= source < leaves:
                at = device_of_leaf(source) * count
                total += got_ref[at : at + count, part * columns : (part + 1) * columns].astype(F32)
        at = device_of_leaf(leaf) * count
        sum_s[at : at + count] = total
    total = sum_s[...]
    high = total.astype(BF16)
    low = (total - high.astype(F32)).astype(BF16)
    pick = (iota((rows, rows), 0) == place_ref[...]).astype(BF16)
    both = mm_tn(jnp.concatenate([high, low], axis=1), pick)
    out_ref[...] = both[:columns] + both[columns:]


def local(
    points, weights, tree_slot, leaf_interp, skel_leaf, merge_interp, merge_index, near_mask, far_mask
):
    leaves = lax.axis_size("leaf")
    groups = leaves // GROUP
    rows, width = points.shape
    columns = weights.shape[1]
    per_peer = rows // leaves
    rank = skel_leaf.shape[1]
    lanes = 4 * rank // per_peer
    wide = width + -(-(columns + 16 + lanes) // 128) * 128
    half = rank // 2
    scale_inv = 1.0 / (1.75 * math.sqrt(width))
    message = width + 2 * columns
    slots = slot_sources(groups)
    away = [a for a, _ in slots]

    def prefetch(count, grid, ins, outs, scratch=()):
        return pltpu.PrefetchScalarGridSpec(
            num_scalar_prefetch=count, grid=grid, in_specs=ins, out_specs=outs, scratch_shapes=scratch
        )

    send, place = call(
        functools.partial(sort_kernel, rows, per_peer, leaves, lanes),
        pl.GridSpec(
            grid=(4,),
            in_specs=[whole((1, rows)), whole((rows, width)), whole((columns, rows))]
            + [whole((1, count)) for count in (rank, merge_index.shape[1], 2 * NWIN, LEVELS * 2 * FWIN)],
            out_specs=[pl.BlockSpec((rows // 4, wide), lambda i: (i, 0)), whole((1, rows))],
            scratch_shapes=[pltpu.VMEM((1, rows), I32), pltpu.VMEM((per_peer, lanes), BF16)],
        ),
        shapes(((rows, wide), BF16), ((1, rows), I32)),
        vmem=62,
    )(tree_slot.reshape(1, rows), points, weights.T, skel_leaf, merge_index, near_mask, far_mask.reshape(1, -1))
    got = lax.all_to_all(send, "leaf", split_axis=0, concat_axis=0, tiled=True)

    device = lax.axis_index("leaf")
    leaf = leaf_of_device(device)
    group = leaf // GROUP
    source = jnp.asarray([s for _, s in slots], I32)[:, group]
    info = jnp.concatenate(
        [jnp.stack([leaf, leaf % 2, leaf // 2 % 4, leaf // 4 % 2, group, device // 2 % 4]).astype(I32), source]
    )
    interp_in, merge_in, _ = lax.optimization_barrier((leaf_interp[0], merge_interp[0], place))
    to_holder = [(i, device_of_leaf(i)) for i in range(leaves)]
    interp = lax.ppermute(interp_in, "leaf", to_holder)
    first = lax.ppermute(merge_in[:half], "leaf", to_holder)
    upper = merge_in[half:]
    uppers = [lax.ppermute(upper, "leaf", [(i, i ^ (2 * k)) for i in range(leaves)]) for k in (1, 2, 3)]
    got, interp, info, first, *uppers = lax.optimization_barrier((got, interp, info, first, *uppers))
    first_other = move(first, lambda i: i ^ 1)
    group_pieces = jnp.stack([upper] + uppers)
    pieces = jnp.stack([group_pieces, move(group_pieces, lambda i: i ^ 1)])
    piece_shape = pieces.shape

    coded = got[:, wide - lanes :].reshape(leaves, 4 * rank).astype(F32)
    tables = coded[:, : 2 * rank] * 32.0 + coded[:, 2 * rank :]
    mask_at = rank + merge_index.shape[1]
    masks = jnp.concatenate(
        [
            coded[:, 2 * rank + mask_at : 2 * rank + mask_at + 2 * NWIN],
            coded[:, mask_at : mask_at + LEVELS * 2 * FWIN],
        ],
        axis=1,
    ).astype(I32)
    table_shape = tables.shape

    other = move(got, lambda i: i ^ 1)
    behind = move(got, lambda i: i + 2)
    ahead = move(got, lambda i: i - 2)

    give, keep, weight0 = call(
        level0_kernel,
        prefetch(1, (), [whole((rows, wide)), whole((rank, rows)), whole(table_shape)],
                 [whole((half, message)), whole((half, width)), whole((rank, columns))]),
        shapes(((half, message), BF16), ((half, width), BF16), ((rank, columns), BF16)),
    )(info, got, interp, tables)
    sent, weight1 = call(
        level1_kernel,
        prefetch(1, (), [whole((half, message)), whole((half, width)), whole((rank, columns))] + [whole((half, 2 * rank))] * 2,
                 [whole((half, message)), whole((rank, columns))]),
        shapes(((half, message), BF16), ((rank, columns), BF16)),
    )(info, move(give, lambda i: i ^ 1), keep, weight0, first, first_other)
    plane = [move(sent, lambda i, k=k: i ^ (2 * k)) for k in (1, 2, 3)]
    own_sum, other_sum, own_column, other_column = call(
        functools.partial(own_kernel, scale_inv, width),
        prefetch(2, (), [whole((rows, wide))] * 2, [whole((rows, columns))] * 2 + [whole((rows, 1))] * 2),
        shapes(*[((rows, columns), F32)] * 2, *[((rows, 1), F32)] * 2),
        flops=3 * rows * rows * width,
    )(info, masks, got, after(other, sent))
    weight1_sent = after(weight1, own_sum)
    behind1 = move(weight1_sent, lambda i: i + 2)
    ahead1 = move(weight1_sent, lambda i: i - 2)

    half2, weight2, weight3 = call(
        level23_kernel,
        prefetch(1, (), [whole((half, message))] * 4 + [whole(piece_shape)],
                 [whole((rank, message)), whole((2 * rank, columns)), whole((rank, columns))],
                 [pltpu.VMEM((4 * rank, columns), BF16)]),
        shapes(((rank, message), BF16), ((2 * rank, columns), BF16), ((rank, columns), BF16)),
    )(info, after(sent, own_sum, behind1, ahead1, behind, ahead), *plane, pieces)
    half2_other = move(half2, lambda i: i ^ 1)
    half3 = call(
        level3_kernel,
        prefetch(1, (), [whole((rank, message))] * 2 + [whole(table_shape)], whole((half, message))),
        jax.ShapeDtypeStruct((half, message), BF16),
    )(info, half2, half2_other, tables)
    far_parts = [send_each(half2 if a == 1 else half3, s) for a, s in slots]
    extra = pl.BlockSpec((rank, 2 * columns), lambda *_: (0, width // (2 * columns)))
    leaf_x, weight_1, sums = whole((rows, wide)), whole((rank, columns)), whole((rows, columns))
    leaf_w, leaf_c, row_c, acc_shape = (rows, 2 * columns), (rows, 1), (1, rows), (2 * columns, rows)
    next_1, next_2, acc, ahead_w, ahead_row = call(
        functools.partial(next_kernel, scale_inv, width),
        prefetch(2, (), [leaf_x] * 2 + [whole(leaf_c)] * 2 + [leaf_x] + [weight_1] * 2 + [sums] * 2 + [whole(table_shape)],
                 [sums] * 2 + [whole(acc_shape), whole(leaf_w), whole(row_c)]),
        shapes(((rows, columns), F32), ((rows, columns), F32), (acc_shape, F32), (leaf_w, BF16), (row_c, F32)),
    )(info, masks, after(got, half3), other, own_column, other_column, ahead, weight1, ahead1, own_sum, other_sum, tables)

    behind_other = move(after(behind, half3), lambda i: i ^ 1)
    pair_sum = call(
        functools.partial(before_kernel, scale_inv, width),
        prefetch(2, (), [leaf_x] * 3 + [weight_1, whole(acc_shape), whole(leaf_w), whole(row_c), whole(table_shape)],
                 whole((rows, 3 * columns))),
        jax.ShapeDtypeStruct((rows, 3 * columns), BF16),
        flops=4 * rows * rows * width,
    )(info, masks, behind, behind_other, ahead, behind1, acc, ahead_w, ahead_row, tables)

    half4 = call(
        level4_kernel,
        prefetch(1, (1,), [whole((rank, columns)), extra, extra, whole(piece_shape)], whole((half, columns))),
        jax.ShapeDtypeStruct((half, columns), BF16),
    )(info, after(weight3, pair_sum), far_parts[0], far_parts[1], pieces)
    nodes4 = groups // 2
    steps4 = [(-1, 1)] if nodes4 == 2 else [(s,) for s in (-2, -1, 1, 2)]
    weight4 = []
    for steps in steps4:
        for h in (0, 1):
            found = [[2 * (g // 2 + s) + (g % 2 ^ h) for s in steps if 0 <= g // 2 + s < nodes4] for g in range(groups)]
            weight4.append(send_each(half4, [f[0] if f else -1 for f in found]))
    weight4 = jnp.stack(weight4)
    all_sums = call(
        functools.partial(far_kernel, away, len(steps4), scale_inv, width),
        prefetch(2, (), [leaf_x] * 2 + [whole(leaf_c)] * 2 + [whole((rank, message)), whole((2 * rank, columns)),
                 whole(weight4.shape), whole(table_shape), sums, sums, whole((rows, 3 * columns))]
                 + [whole(p.shape) for p in far_parts], whole((rows, 5 * columns)),
                 [pltpu.VMEM((rows, columns), F32)] * 2
                 + [pltpu.VMEM((rank, 3 * columns), BF16), pltpu.VMEM((rank, 2 * columns), BF16)]),
        jax.ShapeDtypeStruct((rows, 5 * columns), BF16),
        flops=4 * rows * rows * width,
    )(info, masks, got, other, own_column, other_column, half2, weight2, weight4, tables, next_1, next_2, pair_sum,
      *far_parts)

    home = lax.all_to_all(all_sums, "leaf", split_axis=0, concat_axis=0, tiled=True)
    return call(
        functools.partial(home_kernel, leaves),
        pl.GridSpec(grid=(), in_specs=[whole((1, rows)), whole((rows, 5 * columns))], out_specs=whole((columns, rows)),
                    scratch_shapes=[pltpu.VMEM((rows, columns), F32)]),
        jax.ShapeDtypeStruct((columns, rows), F32),
    )(place, home).T


def solution(mesh):
    placed = (
        P("leaf", None),
        P("leaf", None),
        P("leaf"),
        P("leaf", None, None),
        P("leaf", None),
        P("leaf", None, None),
        P("leaf", None),
        P("leaf", None),
        P("leaf", None, None),
    )
    return jax.shard_map(
        local, mesh=mesh, in_specs=placed, out_specs=P("leaf", None), check_vma=False
    )
```

```python
import functools
import math

import jax
import jax.numpy as jnp
from jax import lax
from jax.experimental import pallas as pl
from jax.experimental.pallas import tpu as pltpu
from jax.sharding import PartitionSpec as P

LEVELS = 4
NWIN = 4
FWIN = 2
GROUP = 8
BF16 = jnp.bfloat16
F32 = jnp.float32
I32 = jnp.int32
NT = (((1,), (1,)), ((), ()))
TN = (((0,), (0,)), ((), ()))
CHUNK = 256


def call(kernel, grid_spec, out_shape, vmem=40, flops=0):
    return pl.pallas_call(
        kernel,
        grid_spec=grid_spec,
        out_shape=out_shape,
        compiler_params=pltpu.CompilerParams(vmem_limit_bytes=vmem * 1024 * 1024),
        cost_estimate=pl.CostEstimate(flops=flops, bytes_accessed=0, transcendentals=0),
    )


def after(value, *others):
    return lax.optimization_barrier((value, *others))[0]


def whole(shape):
    return pl.BlockSpec(shape, lambda *_: (0,) * len(shape))


def shapes(*specs):
    return [jax.ShapeDtypeStruct(shape, kind) for shape, kind in specs]


def mm(a, b):
    return jnp.dot(a, b, preferred_element_type=F32)


def mm_nt(a, b):
    return lax.dot_general(a, b, NT, preferred_element_type=F32)


def mm_tn(a, b):
    return lax.dot_general(a, b, TN, preferred_element_type=F32)


def device_of_leaf(leaf):
    group, chip = leaf // GROUP, (leaf // 2) % 4
    return group * GROUP + ((chip ^ (chip >> 1)) ^ ((group & 1) * 2)) * 2 + leaf % 2


def leaf_of_device(device):
    group, chip = device // GROUP, (device // 2) % 4 ^ ((device // GROUP & 1) * 2)
    return group * GROUP + (chip ^ (chip >> 1)) * 2 + device % 2


def move(value, target_of_leaf):
    leaves = lax.axis_size("leaf")
    pairs = []
    for leaf in range(leaves):
        target = target_of_leaf(leaf)
        if 0 <= target < leaves:
            pairs.append((device_of_leaf(leaf), device_of_leaf(target)))
    return lax.ppermute(value, "leaf", pairs)


def slot_sources(groups):
    slots = []
    for away in range(1, min(6, groups)):
        merge = away > 1 and groups <= 2 * away
        for steps in [(away, -away)] if merge else [(away,), (-away,)]:
            found = [[g + s for s in steps if 0 <= g + s < groups] for g in range(groups)]
            slots.append((away, [f[0] if f else -1 for f in found]))
    return slots


def send_each(value, source):
    pairs = [(s * GROUP + i, g * GROUP + i) for g, s in enumerate(source) if s >= 0 for i in range(GROUP)]
    return lax.ppermute(value, "leaf", pairs)


LEAF, CORE, CHIP, NODE, AT, PHYS = range(6)
SLOT0 = 6


def iota(shape, dim):
    return lax.broadcasted_iota(I32, shape, dim)


def sort_kernel(
    rows, per_peer, leaves, lanes, slot_ref, points_ref, weights_ref, skel_ref, merge_ref, near_ref, far_ref,
    send_ref, place_ref, place_s, table_s,
):
    step = pl.program_id(0)
    block, wide = send_ref.shape
    slot = slot_ref[...]

    @pl.when(step == 0)
    def _():
        dest = device_of_leaf(slot // rows)
        at = (iota((leaves, rows), 0) == dest).astype(BF16)
        earlier = (iota((rows, rows), 0) < iota((rows, rows), 1)).astype(BF16)
        rank = jnp.sum(at.astype(F32) * mm(at, earlier), axis=0, keepdims=True)
        place_s[...] = dest * per_peer + rank.astype(I32)
        place_ref[...] = place_s[...]
        skel, merge = skel_ref[...], merge_ref[...]
        end = skel.shape[1] + merge.shape[1]
        second = 2 * skel.shape[1]
        table = jnp.zeros((per_peer, lanes), F32)
        for base, values in (
            (0, skel // 32),
            (skel.shape[1], merge // 32),
            *((end + 2 * FWIN * i, far_ref[0, i : i + 1]) for i in range(LEVELS)),
            (second, skel % 32),
            (second + skel.shape[1], merge % 32),
            (second + end, near_ref[...]),
        ):
            count = values.shape[1]
            row = (base + iota((per_peer, count), 1)) // lanes == iota((per_peer, count), 0)
            spread = jnp.where(row, values, 0).astype(F32).astype(BF16)
            fold = ((base + iota((count, lanes), 0)) % lanes == iota((count, lanes), 1)).astype(BF16)
            table += mm(spread, fold)
        table_s[...] = table.astype(BF16)

    pick = (iota((block, rows), 0) + step * block == place_s[...]).astype(BF16)
    width, columns = points_ref.shape[1], weights_ref.shape[0]
    inner = slot % rows
    row = iota((16, rows), 0)
    parts = jnp.where(row == 0, inner // 32, jnp.where(row == 1, inner % 32, 0)).astype(F32).astype(BF16)
    spread = (iota((block, per_peer), 0) % per_peer == iota((block, per_peer), 1)).astype(BF16)
    values = (
        (0, mm(pick, points_ref[...])),
        (width, mm_nt(pick, weights_ref[...])),
        (width + columns, mm_nt(pick, parts)),
        (width + columns + 16, jnp.zeros((block, wide - lanes - width - columns - 16), F32)),
        (wide - lanes, mm(spread, table_s[...])),
    )
    for at, value in values:
        send_ref[:, at : at + value.shape[1]] = value.astype(BF16)


def join(whole_ref, first_ref, second_ref):
    cut = first_ref.shape[0]
    whole_ref[:cut] = first_ref[...]
    whole_ref[cut:] = second_ref[...]


def tree_rows(extra):
    lane = iota((16, extra.shape[1]), 1)
    parts = jnp.where(lane == 0, 32.0, jnp.where(lane == 1, 1.0, 0.0)).astype(BF16)
    return mm_nt(parts, extra)[0:1].astype(I32)


def entries(table, low, high, leaf):
    lane = iota((1, GROUP), 1)
    return jnp.sum(jnp.where(lane == leaf, table[low:high], 0.0), axis=1, keepdims=True).astype(I32)


def table_of(table_ref, group):
    return jnp.transpose(table_ref[pl.ds(pl.multiple_of(group * GROUP, GROUP), GROUP)])


def bounds(rank):
    ends = [rank]
    for level in range(1, LEVELS + 1):
        ends.append(ends[-1] + (rank >> level))
    return ends


def node_picks(table, rank, level, first, count):
    low, high = bounds(rank)[level - 1 : level + 1]
    rows = high - low
    several = jnp.concatenate([table[low:high]] * count)
    lane = iota((1, GROUP), 1) - first
    row = iota((rows * count, 1), 0) // rows
    return jnp.sum(jnp.where(lane == row, several, 0.0), axis=1, keepdims=True).astype(I32)


def leaf_picks(table, rank, leaf, where):
    skeleton = (entries(table, 0, rank, leaf) == where).astype(BF16)
    index1 = node_picks(table, rank, 1, leaf // 2 * 2, 2) - rank * (leaf % 2)
    return skeleton, (index1 == iota((rank, rank), 1)).astype(BF16)


def level0_kernel(info, got_ref, interp_ref, table_ref, give_ref, keep_ref, weight0_ref):
    rank, columns = weight0_ref.shape
    rows, width = got_ref.shape[0], keep_ref.shape[1]
    half = rank // 2
    where = tree_rows(got_ref[:, width + columns :])
    order = (iota((rows, rows), 0) == where).astype(BF16)
    weights = mm(order, got_ref[:, width : width + columns]).astype(BF16)
    weight0 = mm(interp_ref[...], weights).astype(BF16)
    weight0_ref[...] = weight0
    table = table_of(table_ref, info[AT])
    skeleton, pick1 = leaf_picks(table, rank, info[LEAF] % GROUP, where)
    level0 = mm(skeleton, got_ref[:, :width]).astype(BF16)
    level1 = mm(pick1, level0).astype(BF16)
    core = info[CORE]

    def part(side):
        index2 = node_picks(table, rank, 2, 4 * info[NODE] + 2 * side, 2) - rank * (info[CHIP] % 2)
        return mm((index2 == iota((half, rank), 1)).astype(BF16), level1).astype(BF16)

    keep_ref[...] = part(core)
    give_ref[:, :width] = part(1 - core)
    give_ref[:, width : width + columns] = weight0[:half]
    give_ref[:, width + columns :] = weight0[half:]


def piece(info, pieces_ref, leaf):
    return pieces_ref.at[leaf % 2 ^ info[CORE], leaf // 2 ^ info[PHYS]]


def in_order(core, mine, other):
    return jnp.where(core == 0, jnp.concatenate([mine, other]), jnp.concatenate([other, mine]))


def level1_kernel(info, other_ref, keep_ref, weight0_ref, own_piece_ref, other_piece_ref, out_ref, weight1_ref):
    rank, columns = weight1_ref.shape
    half, width = keep_ref.shape
    core = info[CORE]
    other0 = jnp.concatenate([other_ref[:, width : width + columns], other_ref[:, width + columns :]])
    both0 = in_order(core, weight0_ref[...], other0)
    weight1 = in_order(core, mm(own_piece_ref[...], both0), mm(other_piece_ref[...], both0)).astype(BF16)
    weight1_ref[...] = weight1
    out_ref[:, :width] = keep_ref[...] + other_ref[:, :width]
    out_ref[:, width : width + columns] = weight1[:half]
    out_ref[:, width + columns :] = weight1[half:]


def level23_kernel(info, m0, m1, m2, m3, pieces_ref, out_ref, weight2_ref, weight3_ref, w1_s):
    half = m0.shape[0]
    rank = 2 * half
    columns = weight2_ref.shape[1]
    width = m0.shape[1] - 2 * columns
    core, chip, node = info[CORE], info[CHIP], info[NODE]
    for k, message in enumerate((m0, m1, m2, m3)):
        at = pl.ds(pl.multiple_of((chip ^ k) * rank, rank), rank)
        w1_s[at] = jnp.concatenate([message[:, width : width + columns], message[:, width + columns :]])
    r2, r3 = rank >> 2, rank >> 3
    for n in (0, 1):
        for i in range(4):
            rows2 = piece(info, pieces_ref, 4 * n + i)[:r2]
            at = n * rank + i * r2
            weight2_ref[at : at + r2] = mm(rows2, w1_s[2 * n * rank : 2 * (n + 1) * rank]).astype(BF16)
    low = r2
    weight3 = jnp.concatenate(
        [mm(piece(info, pieces_ref, i)[low : low + r3], weight2_ref[...]) for i in range(GROUP)]
    )
    weight3_ref[...] = weight3.astype(BF16)
    own = m0[:, :width] + m1[:, :width]
    cross = m2[:, :width] + m3[:, :width]
    out_ref[:half, :width] = jnp.where(node == 0, own, cross)
    out_ref[half:, :width] = jnp.where(node == 0, cross, own)
    for n in (0, 1):
        at = pl.ds(pl.multiple_of(n * rank + core * half, half), half)
        out_ref[n * half : (n + 1) * half, width : width + columns] = weight2_ref[at]
    out_ref[:, width + columns :] = weight3.astype(BF16)


def level3_kernel(info, own_ref, other_ref, table_ref, out_ref):
    half = out_ref.shape[0]
    rank = 2 * half
    columns = 64
    width = own_ref.shape[1] - 2 * columns
    core = info[CORE]
    index = node_picks(table_of(table_ref, info[AT]), rank, 3, 4 * core, 4)
    entry = index % rank
    at = index // rank * half + entry % half
    hit = at == iota((half, rank), 1)
    mine = (hit & (entry // half == core)).astype(BF16)
    theirs = (hit & (entry // half != core)).astype(BF16)
    out_ref[:, :width] = (mm(mine, own_ref[:, :width]) + mm(theirs, other_ref[:, :width])).astype(BF16)
    out_ref[:, width : width + columns] = own_ref[:half, width + columns :]
    out_ref[:, width + columns :] = own_ref[half:, width + columns :]


def level4_kernel(info, weight3_ref, next_ref, before_ref, pieces_ref, out_ref):
    rank, columns = weight3_ref.shape
    low = (rank >> 2) + (rank >> 3)
    sibling = jnp.where(info[AT] % 2 == 0, next_ref[:, columns:], before_ref[:, columns:])
    both = in_order(info[AT] % 2, weight3_ref[...], sibling)
    r4 = rank >> 4
    for i in range(GROUP):
        out_ref[i * r4 : (i + 1) * r4] = mm(piece(info, pieces_ref, i)[low : low + r4], both).astype(BF16)


def far_masks(info, mask_ref, leaf, source):
    def at(level, step):
        column = jnp.clip(jnp.where(step < 0, step + FWIN, step + FWIN - 1), 0, 2 * FWIN - 1)
        value = mask_ref[leaf, 2 * NWIN + (level - 1) * 2 * FWIN + column]
        return jnp.where((step != 0) & (jnp.abs(step) <= FWIN) & (source >= 0), value, 0)

    node = 2 * info[AT] + info[NODE]
    return [
        at(2, 2 * source - node),
        at(2, 2 * source + 1 - node),
        at(3, source - info[AT]),
        at(4, source // 2 - info[AT] // 2),
    ]


def row_offset(block, scale_inv):
    squares = jnp.sum(jnp.square(block.astype(F32)), axis=1, keepdims=True)
    return (squares - block.shape[1]) * (0.5 * scale_inv)


def as_row(column):
    return jnp.transpose(jnp.broadcast_to(column, (column.shape[0], 128)))[0:1]


def kernel_block(targets, target_column, sources, source_row, scale_inv):
    products = mm_nt(targets, sources)
    return jnp.exp(products * scale_inv - target_column - source_row).astype(BF16)


def as_bf16(value):
    return value.astype(F32).astype(BF16)


def far_kernel(away, parents, sides, share, scale_inv, width, info, mask_ref, x1_ref, x2_ref, c1_ref, c2_ref, half_ref, w2_ref, table_ref,
               init1_ref, init2_ref, pairs_ref, *rest):
    parts, rest = rest[: len(away)], rest[len(away) :]
    w4_refs, (result, out1_ref, out2_ref, w_s, w4_s) = rest[: 2 * parents], rest[2 * parents :]
    columns = out1_ref.shape[1]
    half = half_ref.shape[0] // 2
    rank = 2 * half
    core, node = info[CORE], info[NODE]
    offsets = (c1_ref, c2_ref)
    out1_ref[...] = init1_ref[...]
    out2_ref[...] = init2_ref[...]
    side = [info[LEAF], info[LEAF] ^ 1]

    def run(sources, weights, masks):
        row = as_row(row_offset(sources, scale_inv))
        count = weights.shape[0] // 2
        for x_ref, offset, out_ref, mask in zip((x1_ref, x2_ref), offsets, (out1_ref, out2_ref), masks, strict=True):
            scaled = jnp.concatenate(
                [
                    jnp.concatenate([weights[i * count : (i + 1) * count, j * columns : (j + 1) * columns] * as_bf16(mask[i][j])
                                     for j in range(3)], axis=1)
                    for i in (0, 1)
                ]
            )
            kernel = kernel_block(x_ref[:, :width], offset[...], sources, row, scale_inv)
            sums = mm(kernel, scaled)
            out_ref[...] += sums[:, :columns] + sums[:, columns : 2 * columns] + sums[:, 2 * columns :]

    def spread_of(i, distance, part, source):
        if distance == 1:
            w3 = part[:, width + columns :]
        else:
            w3 = jnp.concatenate([part[:, width : width + columns], part[:, width + columns :]])
        step = source // 2 - info[AT] // 2
        parent = jnp.clip(jnp.where(step < 0, step + FWIN, step + FWIN - 1), 0, 2 * FWIN - 1)
        same, cross = w4_refs[0][...], w4_refs[1][...]
        for k in range(1, parents):
            same = jnp.where(parent == k, w4_refs[2 * k][...], same)
            cross = jnp.where(parent == k, w4_refs[2 * k + 1][...], cross)
        even = source - source % 2
        index = [node_picks(table_of(table_ref, group), rank, 4, 0, GROUP) for group in (even, even + 1)]
        index = jnp.concatenate(index) - rank * (source % 2)
        w4 = in_order(info[AT] % 2, same, cross)
        w4 = mm_tn((index == iota((rank, rank), 1)).astype(BF16), w4).astype(BF16)
        if distance == 1:
            index3 = node_picks(table_of(table_ref, source), rank, 3, 0, GROUP)
            lane = iota((rank, rank), 1)
            hit = (index3 == lane // half * rank + core * half + lane % half).astype(BF16)
            both = mm_tn(hit, jnp.concatenate([w3, w4], axis=1)).astype(BF16)
            return jnp.concatenate([part[:, width : width + columns], both], axis=1)
        w4_s[:, :columns] = w3
        w4_s[:, columns:] = w4
        rows = pl.ds(pl.multiple_of(core * half, half), half)
        return jnp.concatenate([jnp.zeros((half, columns), BF16), w4_s[rows]], axis=1)

    zero = jnp.zeros((), I32)
    joined = away.index(2) if 2 in away else -1
    for i, distance in enumerate(away):
        source = info[SLOT0 + i]
        known = jnp.maximum(source, 0)
        masks = [far_masks(info, mask_ref, leaf, source) for leaf in side]
        if distance == 1:
            used = sum(sum(m) for m in masks) > 0
            lists = [[[m[0], m[2], m[3]], [m[1], m[2], m[3]]] for m in masks]
        else:
            used = sum(m[2] + m[3] for m in masks) > 0
            lists = [[[zero, m[2], m[3]]] * 2 for m in masks]
        if i != joined:

            @pl.when(used)
            def _(i=i, distance=distance, known=known, lists=lists):
                run(parts[i][:, :width], spread_of(i, distance, parts[i], known), lists)

            continue
        cross = pl.ds(pl.multiple_of((1 - node) * half, half), half)
        column = jnp.where(node == 0, 2 * NWIN + 2 * FWIN + FWIN, 2 * NWIN + 2 * FWIN + FWIN - 1)
        w_s[:half, :columns] = w2_ref[pl.ds(pl.multiple_of((1 - node) * rank + core * half, half), half)]
        w_s[:half, columns:] = jnp.zeros((half, 2 * columns), BF16)
        w_s[half:] = spread_of(i, distance, parts[i], known)
        lists = [
            [[mask_ref[leaf, column], zero, zero], entry[0]] for leaf, entry in zip(side, lists, strict=True)
        ]
        run(jnp.concatenate([half_ref[cross, :width], parts[i][:, :width]]), w_s[...], lists)
    parts = (out1_ref[...].astype(BF16), out2_ref[...].astype(BF16), pairs_ref[...])
    at = 0
    for i in range(sides):
        for value in parts:
            lanes = value.shape[1]
            if sides == 2:
                value = value.reshape(-1, 2, share, lanes)[:, i].reshape(-1, lanes)
            result[:, at : at + lanes] = value
            at += lanes


def halves(value):
    half = value.shape[1] // 2
    return value[:, :half] + value[:, half:]


def masked(weights, first, second):
    lane = iota((1, weights.shape[1]), 1)
    return (weights.astype(F32) * jnp.where(lane < weights.shape[1] // 2, first, second)).astype(BF16)


def own_kernel(scale_inv, width, info, mask_ref, own_ref, other_ref, out_ref, back_ref, column_ref, column_other_ref):
    rows, columns = out_ref.shape
    half = rows // 2
    last = width + columns
    own_column = row_offset(own_ref[:, :width], scale_inv)
    other_column = row_offset(other_ref[:, :width], scale_inv)
    column_ref[...] = own_column
    column_other_ref[...] = other_column
    kernel = kernel_block(own_ref[:, :width], own_column, own_ref[:, :width], as_row(own_column), scale_inv)
    out_ref[...] = mm(kernel, own_ref[:, width:last])
    back_ref[...] = jnp.zeros_like(back_ref)
    near = mask_ref[info[LEAF] // 2 * 2, NWIN] > 0

    def pair(first, count):
        mine = own_ref[first:, :width]
        theirs = other_ref[:count, :width]
        kernel = kernel_block(mine, own_column[first:], theirs, as_row(other_column[:count]), scale_inv)
        out_ref[first:] += mm(kernel, other_ref[:count, width:last])
        back_ref[:count] = mm_tn(kernel, own_ref[first:, width:last])

    @pl.when(near & (info[CORE] == 0))
    def _():
        pair(0, half)

    @pl.when(near & (info[CORE] == 1))
    def _():
        pair(half, rows)


def leaf_weights(x, width, columns, weight1, table_ref, leaf):
    rank = weight1.shape[0]
    half = rank // 2
    extra = x[:, width:]
    row = iota((extra.shape[1], 128), 0)
    parts = jnp.where(row == columns, 32.0, jnp.where(row == columns + 1, 1.0, 0.0)).astype(BF16)
    where = mm(extra, parts)
    group = table_ref[pl.ds(pl.multiple_of(leaf // GROUP * GROUP, GROUP), GROUP), : rank + half]
    at = iota((GROUP, 1), 0)

    def of(index, low, high):
        return jnp.sum(jnp.where(at == index, group[:, low:high], 0.0), axis=0, keepdims=True)

    base = leaf % GROUP // 2 * 2
    index1 = jnp.concatenate([of(base + i, rank, rank + half) for i in (0, 1)], axis=1)
    index1 = index1 - (leaf % 2 * rank).astype(F32)
    pick1 = (iota((rank, rank), 0).astype(F32) == index1).astype(BF16)
    level0 = mm(pick1, weight1).astype(BF16)
    skeleton = of(leaf % GROUP, 0, rank)
    hit = [(where == skeleton[:, i : i + 128]).astype(BF16) for i in range(0, rank, 128)]
    spread = mm(jnp.concatenate(hit, axis=1), level0).astype(BF16)
    return jnp.concatenate([extra[:, :columns], spread], axis=1)


def pair_masks(info, mask_ref):
    core = info[CORE]
    chip = info[LEAF] // 2
    leaves = mask_ref.shape[0]
    r_leaf = jnp.minimum(2 * chip + 2, leaves - 2) + core
    level1 = 2 * NWIN
    masks, names = [], []
    for behind in (0, 1):
        for side in (core, 1 - core):
            leaf = jnp.maximum(2 * chip - 2 * behind, 0) + side
            there = (2 * chip + 2 < leaves) & (chip >= behind)
            distance = 2 + 2 * behind + core - side
            near = jnp.where(distance <= NWIN, mask_ref[leaf, jnp.minimum(NWIN - 1 + distance, 2 * NWIN - 1)], 0)
            values = (near, mask_ref[leaf, level1 + FWIN + behind], mask_ref[r_leaf, level1 + FWIN - 1 - behind])
            masks.append([jnp.where(there, v, 0) for v in values])
            names.append(leaf)
    return masks, names, r_leaf


def pair_sums(scale_inv, width, jobs, r, r_row, r_weights, acc):
    sums = []
    for mask, ref, column, weights in jobs:
        near, far_out, far_back = (m.astype(F32) for m in mask)
        kernel = kernel_block(ref[:, :width], column, r, r_row, scale_inv)
        sums.append(halves(mm(kernel, masked(r_weights, near, far_out))))
        acc += mm_tn(masked(weights, near, far_back), kernel)
    return sums, acc


def pair_kernel(scale_inv, width, info, mask_ref, q1, q2, c1, c2, p1a, p1b, p2a, p2b, ra, rb, w_all, w_cross,
                init1, init2, table_ref, out1, out2, result, p1, p2, r):
    for ref, parts in ((p1, (p1a, p1b)), (p2, (p2a, p2b)), (r, (ra, rb))):
        join(ref, *parts)
    columns = out1.shape[1]
    masks, names, r_leaf = pair_masks(info, mask_ref)
    refs = (q1, q2, p1, p2)
    chip, rank = info[CHIP], w_cross.shape[0]
    last = w_all.shape[0] // rank - 1

    def of(index, inside):
        at = pl.ds(pl.multiple_of(jnp.clip(index, 0, last) * rank, rank), rank)
        return jnp.where(inside, w_all[at], w_cross[...])

    w_q, w_p, w_r = of(chip, True), of(chip - 1, chip > 0), of(chip + 1, chip < last)
    r_weights = leaf_weights(r, width, columns, w_r, table_ref, r_leaf)
    r_row = as_row(row_offset(r[:, :width], scale_inv))
    acc = jnp.zeros((2 * columns, r.shape[0]), F32)
    sums = []
    for i, (mask, ref, leaf) in enumerate(zip(masks, refs, names, strict=True)):
        weights = leaf_weights(ref, width, columns, w_q if i < 2 else w_p, table_ref, leaf)
        column = (c1, c2)[i][...] if i < 2 else row_offset(ref[:, :width], scale_inv)
        near, far_out, far_back = (m.astype(F32) for m in mask)
        kernel = kernel_block(ref[:, :width], column, r[:, :width], r_row, scale_inv)
        sums.append(halves(mm(kernel, masked(r_weights, near, far_out))))
        acc += mm_tn(masked(weights, near, far_back), kernel)
    out1[...] = init1[...] + sums[0]
    out2[...] = init2[...] + sums[1]
    for i, value in enumerate((sums[2], sums[3], halves(jnp.transpose(acc)))):
        result[:, i * columns : (i + 1) * columns] = value.astype(BF16)


def home_kernel(leaves, sides, place_ref, got_ref, out_ref, sum_s):
    columns, rows = out_ref.shape
    count = rows // leaves // sides
    for leaf in range(leaves):
        sources = (leaf, leaf ^ 1, leaf + 2, (leaf ^ 1) + 2, leaf - 2)
        for i in range(sides):
            total = 0.0
            for part, source in enumerate(sources):
                if 0 <= source < leaves:
                    at, lane = device_of_leaf(source) * count, (5 * i + part) * columns
                    total += got_ref[at : at + count, lane : lane + columns].astype(F32)
            at = (device_of_leaf(leaf) * sides + i) * count
            sum_s[at : at + count] = total
    total = sum_s[...]
    high = total.astype(BF16)
    low = (total - high.astype(F32)).astype(BF16)
    pick = (iota((rows, rows), 0) == place_ref[...]).astype(BF16)
    both = mm_tn(jnp.concatenate([high, low], axis=1), pick)
    out_ref[...] = both[:columns] + both[columns:]


def local(
    points, weights, tree_slot, leaf_interp, skel_leaf, merge_interp, merge_index, near_mask, far_mask
):
    leaves = lax.axis_size("leaf")
    groups = leaves // GROUP
    rows, width = points.shape
    columns = weights.shape[1]
    per_peer = rows // leaves
    rank = skel_leaf.shape[1]
    lanes = 4 * rank // per_peer
    wide = width + -(-(columns + 16 + lanes) // 128) * 128
    half = rank // 2
    scale_inv = 1.0 / (1.75 * math.sqrt(width))
    message = width + 2 * columns
    slots = slot_sources(groups)
    away = [a for a, _ in slots]

    def prefetch(count, grid, ins, outs, scratch=()):
        return pltpu.PrefetchScalarGridSpec(
            num_scalar_prefetch=count, grid=grid, in_specs=ins, out_specs=outs, scratch_shapes=scratch
        )

    send, place = call(
        functools.partial(sort_kernel, rows, per_peer, leaves, lanes),
        pl.GridSpec(
            grid=(4,),
            in_specs=[whole((1, rows)), whole((rows, width)), whole((columns, rows))]
            + [whole(a.shape) for a in (skel_leaf, merge_index, near_mask, far_mask)],
            out_specs=[
                pl.BlockSpec((rows // 4, wide), lambda i: (i, 0)),
                whole((1, rows)),
            ],
            scratch_shapes=[pltpu.VMEM((1, rows), I32), pltpu.VMEM((per_peer, lanes), BF16)],
        ),
        shapes(((rows, wide), BF16), ((1, rows), I32)),
        vmem=62,
    )(tree_slot.reshape(1, rows), points, weights.T, skel_leaf, merge_index, near_mask, far_mask)
    got = lax.all_to_all(send, "leaf", split_axis=0, concat_axis=0, tiled=True)

    def halo(value):
        def inside(by):
            return lambda i: i + by if (i + by) // GROUP == i // GROUP else -1

        return move(value, inside(2)), move(value, inside(-2))

    ends = []
    for g in range(1, groups):
        for i in (0, 1):
            pair = device_of_leaf(g * GROUP - 2 + i), device_of_leaf(g * GROUP + i)
            ends += [pair, pair[::-1]]

    def over_end(value):
        return lax.ppermute(value, "leaf", ends)


    device = lax.axis_index("leaf")
    leaf = leaf_of_device(device)
    group = leaf // GROUP
    source = jnp.asarray([s for _, s in slots], I32)[:, group]
    info = jnp.concatenate(
        [jnp.stack([leaf, leaf % 2, leaf // 2 % 4, leaf // 4 % 2, group, device // 2 % 4]).astype(I32), source]
    )
    interp_in, merge_in, _ = lax.optimization_barrier((leaf_interp[0], merge_interp[0], place))
    to_holder = [(i, device_of_leaf(i)) for i in range(leaves)]
    interp = lax.ppermute(interp_in, "leaf", to_holder)
    first = lax.ppermute(merge_in[:half], "leaf", to_holder)
    upper = merge_in[half:]
    uppers = [lax.ppermute(upper, "leaf", [(i, i ^ (2 * k)) for i in range(leaves)]) for k in (1, 2, 3)]
    got, interp, info, first, *uppers = lax.optimization_barrier((got, interp, info, first, *uppers))
    cut = rows * 3 // 8
    got_a, got_b = got[:cut], got[cut:]
    behind_a, ahead_a = halo(got_a)
    over_a = over_end(got_a)
    other = move(got, lambda i: i ^ 1)
    first_other = move(first, lambda i: i ^ 1)
    group_pieces = jnp.stack([upper] + uppers)
    pieces = jnp.stack([group_pieces, move(group_pieces, lambda i: i ^ 1)])
    piece_shape = pieces.shape

    coded = got[:, wide - lanes :].reshape(leaves, 4 * rank).astype(F32)
    high, low = coded[:, : 2 * rank], coded[:, 2 * rank :]
    tables = high * 32.0 + low
    mask_at = rank + merge_index.shape[1]
    masks = jnp.concatenate(
        [
            low[:, mask_at : mask_at + 2 * NWIN],
            high[:, mask_at : mask_at + LEVELS * 2 * FWIN],
        ],
        axis=1,
    ).astype(I32)
    table_shape = tables.shape

    leaf_x, joined = whole((rows, wide)), pltpu.VMEM((rows, wide), BF16)
    own_sum, other_sum, own_column, other_column = call(
        functools.partial(own_kernel, scale_inv, width),
        prefetch(2, (), [leaf_x] * 2, [whole((rows, columns))] * 2 + [whole((rows, 1))] * 2),
        shapes(*[((rows, columns), F32)] * 2, *[((rows, 1), F32)] * 2),
        flops=3 * rows * rows * width,
    )(info, masks, got, other)

    give, keep, weight0 = call(
        level0_kernel,
        prefetch(1, (), [leaf_x, whole((rank, rows)), whole(table_shape)],
                 [whole((half, message)), whole((half, width)), whole((rank, columns))]),
        shapes(((half, message), BF16), ((half, width), BF16), ((rank, columns), BF16)),
    )(info, after(got, own_sum), interp, tables)
    sent, weight1 = call(
        level1_kernel,
        prefetch(1, (), [whole((half, message)), whole((half, width)), whole((rank, columns))] + [whole((half, 2 * rank))] * 2,
                 [whole((half, message)), whole((rank, columns))]),
        shapes(((half, message), BF16), ((rank, columns), BF16)),
    )(info, move(give, lambda i: i ^ 1), keep, weight0, first, first_other)
    sent, behind_a, ahead_a, over_a = lax.optimization_barrier((sent, behind_a, ahead_a, over_a))
    over_b = over_end(after(got_b, over_a))

    def merged(behind, ahead, over):
        chip = leaf // 2 % 4
        return jnp.where(chip == 0, over, behind), jnp.where(chip == 3, over, ahead)

    behind_a, ahead_a = merged(behind_a, ahead_a, over_a)
    plane = [move(sent, lambda i, k=k: i ^ (2 * k)) for k in (1, 2, 3)]
    cross1 = over_end(after(weight1, sent))
    behind_other_a = move(behind_a, lambda i: i ^ 1)
    behind_b, ahead_b = halo(after(got_b, *plane))
    half2, weight2, weight3, weight1_all = call(
        level23_kernel,
        prefetch(1, (), [whole((half, message))] * 4 + [whole(piece_shape)],
                 [whole((rank, message)), whole((2 * rank, columns)), whole((rank, columns)), whole((4 * rank, columns))]),
        shapes(((rank, message), BF16), ((2 * rank, columns), BF16), ((rank, columns), BF16), ((4 * rank, columns), BF16)),
    )(info, after(sent, behind_other_a), *plane, pieces)
    half2_other = move(half2, lambda i: i ^ 1)
    half3 = call(
        level3_kernel,
        prefetch(1, (), [whole((rank, message))] * 2 + [whole(table_shape)], whole((half, message))),
        jax.ShapeDtypeStruct((half, message), BF16),
    )(info, half2, half2_other, tables)
    half3_late = after(half3, over_b)
    far_parts = [send_each(half2 if a == 1 else half3_late, s) for a, s in slots]
    extra = pl.BlockSpec((rank, 2 * columns), lambda *_: (0, width // (2 * columns)))
    half4 = call(
        level4_kernel,
        prefetch(1, (1,), [whole((rank, columns)), extra, extra, whole(piece_shape)], whole((half, columns))),
        jax.ShapeDtypeStruct((half, columns), BF16),
    )(info, after(weight3, half3), far_parts[0], far_parts[1], pieces)
    nodes4 = groups // 2
    steps4 = [(-1, 1)] if nodes4 == 2 else [(s,) for s in (-2, -1, 1, 2)]
    weight4 = []
    for steps in steps4:
        for h in (0, 1):
            found = [[2 * (g // 2 + s) + (g % 2 ^ h) for s in steps if 0 <= g // 2 + s < nodes4] for g in range(groups)]
            weight4.append(send_each(half4, [f[0] if f else -1 for f in found]))
    weight_1, sums, leaf_c = whole((rank, columns)), whole((rows, columns)), whole((rows, 1))
    behind_b, ahead_b = merged(behind_b, ahead_b, over_b)
    before_b = after(behind_b, ahead_b, half3, *far_parts[:2])
    behind_other = [behind_other_a, move(before_b, lambda i: i ^ 1)]
    pair_1, pair_2, pair_sum = call(
        functools.partial(pair_kernel, scale_inv, width),
        prefetch(2, (), [leaf_x] * 2 + [leaf_c] * 2 + [whole((cut, wide)), whole((rows - cut, wide))] * 3 + [whole((4 * rank, columns)), weight_1] + [sums] * 2 + [whole(table_shape)],
                 [sums] * 2 + [whole((rows, 3 * columns))], [joined] * 3),
        shapes(((rows, columns), F32), ((rows, columns), F32), ((rows, 3 * columns), BF16)),
        flops=8 * rows * rows * width,
    )(info, masks, after(got, half4), other, own_column, other_column, behind_a, behind_b,
      *behind_other, ahead_a, ahead_b, weight1_all, cross1, own_sum, other_sum, tables)

    sides = 2 if per_peer % 32 == 0 else 1
    all_sums = call(
        functools.partial(far_kernel, away, len(steps4), sides, per_peer // sides, scale_inv, width),
        prefetch(2, (), [leaf_x] * 2 + [leaf_c] * 2 + [whole((rank, message)), whole((2 * rank, columns)),
                 whole(table_shape), sums, sums, whole((rows, 3 * columns))]
                 + [whole(p.shape) for p in (*far_parts, *weight4)], whole((rows // sides, 5 * sides * columns)),
                 [pltpu.VMEM((rows, columns), F32)] * 2
                 + [pltpu.VMEM((rank, 3 * columns), BF16), pltpu.VMEM((rank, 2 * columns), BF16)]),
        jax.ShapeDtypeStruct((rows // sides, 5 * sides * columns), BF16),
        flops=4 * rows * rows * width,
    )(info, masks, got, other, own_column, other_column, half2, weight2, tables, pair_1, pair_2, pair_sum,
      *far_parts, *weight4)

    home = lax.all_to_all(all_sums, "leaf", split_axis=0, concat_axis=0, tiled=True)
    return call(
        functools.partial(home_kernel, leaves, sides),
        pl.GridSpec(grid=(), in_specs=[whole((1, rows)), whole((rows // sides, 5 * sides * columns))], out_specs=whole((columns, rows)),
                    scratch_shapes=[pltpu.VMEM((rows, columns), F32)]),
        jax.ShapeDtypeStruct((columns, rows), F32),
    )(place, home).T


def solution(mesh):
    placed = (
        P("leaf", None),
        P("leaf", None),
        P("leaf"),
        P("leaf", None, None),
        P("leaf", None),
        P("leaf", None, None),
        P("leaf", None),
        P("leaf", None),
        P("leaf", None, None),
    )
    return jax.shard_map(
        local, mesh=mesh, in_specs=placed, out_specs=P("leaf", None), check_vma=False
    )
```

```python
import functools
import math

import jax
import jax.numpy as jnp
from jax import lax
from jax.experimental import pallas as pl
from jax.experimental.pallas import tpu as pltpu
from jax.sharding import PartitionSpec as P

LEVELS = 4
NWIN = 4
FWIN = 2
GROUP = 8
BF16 = jnp.bfloat16
F32 = jnp.float32
I32 = jnp.int32
NT = (((1,), (1,)), ((), ()))
TN = (((0,), (0,)), ((), ()))
CHUNK = 256


def call(kernel, grid_spec, out_shape, vmem=40, flops=0):
    return pl.pallas_call(
        kernel,
        grid_spec=grid_spec,
        out_shape=out_shape,
        compiler_params=pltpu.CompilerParams(vmem_limit_bytes=vmem * 1024 * 1024),
        cost_estimate=pl.CostEstimate(flops=flops, bytes_accessed=0, transcendentals=0),
    )


def after(value, *others):
    return lax.optimization_barrier((value, *others))[0]


def whole(shape):
    return pl.BlockSpec(shape, lambda *_: (0,) * len(shape))


def shapes(*specs):
    return [jax.ShapeDtypeStruct(shape, kind) for shape, kind in specs]


def mm(a, b):
    return jnp.dot(a, b, preferred_element_type=F32)


def mm_nt(a, b):
    return lax.dot_general(a, b, NT, preferred_element_type=F32)


def mm_tn(a, b):
    return lax.dot_general(a, b, TN, preferred_element_type=F32)


def device_of_leaf(leaf):
    group, chip = leaf // GROUP, (leaf // 2) % 4
    return group * GROUP + ((chip ^ (chip >> 1)) ^ ((group & 1) * 2)) * 2 + leaf % 2


def leaf_of_device(device):
    group, chip = device // GROUP, (device // 2) % 4 ^ ((device // GROUP & 1) * 2)
    return group * GROUP + (chip ^ (chip >> 1)) * 2 + device % 2


def move(value, target_of_leaf):
    leaves = lax.axis_size("leaf")
    pairs = []
    for leaf in range(leaves):
        target = target_of_leaf(leaf)
        if 0 <= target < leaves:
            pairs.append((device_of_leaf(leaf), device_of_leaf(target)))
    return lax.ppermute(value, "leaf", pairs)


def slot_sources(groups):
    slots = []
    for away in range(1, min(6, groups)):
        merge = away > 1 and groups <= 2 * away
        for steps in [(away, -away)] if merge else [(away,), (-away,)]:
            found = [[g + s for s in steps if 0 <= g + s < groups] for g in range(groups)]
            slots.append((away, [f[0] if f else -1 for f in found]))
    return slots


def send_each(value, source):
    pairs = [(s * GROUP + i, g * GROUP + i) for g, s in enumerate(source) if s >= 0 for i in range(GROUP)]
    return lax.ppermute(value, "leaf", pairs)


LEAF, CORE, CHIP, NODE, AT, PHYS = range(6)
SLOT0 = 6


def iota(shape, dim):
    return lax.broadcasted_iota(I32, shape, dim)


def sort_kernel(
    rows, per_peer, leaves, lanes, slot_ref, points_ref, weights_ref, skel_ref, merge_ref, near_ref, far_ref,
    send_ref, place_ref, place_s, table_s,
):
    step = pl.program_id(0)
    block, wide = send_ref.shape
    slot = slot_ref[...]

    @pl.when(step == 0)
    def _():
        dest = device_of_leaf(slot // rows)
        at = (iota((leaves, rows), 0) == dest).astype(BF16)
        earlier = (iota((rows, rows), 0) < iota((rows, rows), 1)).astype(BF16)
        rank = jnp.sum(at.astype(F32) * mm(at, earlier), axis=0, keepdims=True)
        place_s[...] = dest * per_peer + rank.astype(I32)
        place_ref[...] = place_s[...]
        skel, merge = skel_ref[...], merge_ref[...]
        end = skel.shape[1] + merge.shape[1]
        second = 2 * skel.shape[1]
        table = jnp.zeros((per_peer, lanes), F32)
        for base, values in (
            (0, skel // 32),
            (skel.shape[1], merge // 32),
            *((end + 2 * FWIN * i, far_ref[0, i : i + 1]) for i in range(LEVELS)),
            (second, skel % 32),
            (second + skel.shape[1], merge % 32),
            (second + end, near_ref[...]),
        ):
            count = values.shape[1]
            row = (base + iota((per_peer, count), 1)) // lanes == iota((per_peer, count), 0)
            spread = jnp.where(row, values, 0).astype(F32).astype(BF16)
            fold = ((base + iota((count, lanes), 0)) % lanes == iota((count, lanes), 1)).astype(BF16)
            table += mm(spread, fold)
        table_s[...] = table.astype(BF16)

    pick = (iota((block, rows), 0) + step * block == place_s[...]).astype(BF16)
    width, columns = points_ref.shape[1], weights_ref.shape[0]
    inner = slot % rows
    row = iota((16, rows), 0)
    parts = jnp.where(row == 0, inner // 32, jnp.where(row == 1, inner % 32, 0)).astype(F32).astype(BF16)
    spread = (iota((block, per_peer), 0) % per_peer == iota((block, per_peer), 1)).astype(BF16)
    values = (
        (0, mm(pick, points_ref[...])),
        (width, mm_nt(pick, weights_ref[...])),
        (width + columns, mm_nt(pick, parts)),
        (width + columns + 16, jnp.zeros((block, wide - lanes - width - columns - 16), F32)),
        (wide - lanes, mm(spread, table_s[...])),
    )
    for at, value in values:
        send_ref[:, at : at + value.shape[1]] = value.astype(BF16)


def join(whole_ref, first_ref, second_ref):
    cut = first_ref.shape[0]
    whole_ref[:cut] = first_ref[...]
    whole_ref[cut:] = second_ref[...]


def tree_rows(extra):
    lane = iota((16, extra.shape[1]), 1)
    parts = jnp.where(lane == 0, 32.0, jnp.where(lane == 1, 1.0, 0.0)).astype(BF16)
    return mm_nt(parts, extra)[0:1].astype(I32)


def entries(table, low, high, leaf):
    lane = iota((1, GROUP), 1)
    return jnp.sum(jnp.where(lane == leaf, table[low:high], 0.0), axis=1, keepdims=True).astype(I32)


def table_of(table_ref, group):
    return jnp.transpose(table_ref[pl.ds(pl.multiple_of(group * GROUP, GROUP), GROUP)])


def bounds(rank):
    ends = [rank]
    for level in range(1, LEVELS + 1):
        ends.append(ends[-1] + (rank >> level))
    return ends


def node_picks(table, rank, level, first, count):
    low, high = bounds(rank)[level - 1 : level + 1]
    rows = high - low
    several = jnp.concatenate([table[low:high]] * count)
    lane = iota((1, GROUP), 1) - first
    row = iota((rows * count, 1), 0) // rows
    return jnp.sum(jnp.where(lane == row, several, 0.0), axis=1, keepdims=True).astype(I32)


def leaf_picks(table, rank, leaf, where):
    skeleton = (entries(table, 0, rank, leaf) == where).astype(BF16)
    index1 = node_picks(table, rank, 1, leaf // 2 * 2, 2) - rank * (leaf % 2)
    return skeleton, (index1 == iota((rank, rank), 1)).astype(BF16)


def level0_kernel(info, got_ref, interp_ref, table_ref, give_ref, keep_ref, weight0_ref):
    rank, columns = weight0_ref.shape
    rows, width = got_ref.shape[0], keep_ref.shape[1]
    half = rank // 2
    where = tree_rows(got_ref[:, width + columns :])
    order = (iota((rows, rows), 0) == where).astype(BF16)
    weights = mm(order, got_ref[:, width : width + columns]).astype(BF16)
    weight0 = mm(interp_ref[...], weights).astype(BF16)
    weight0_ref[...] = weight0
    table = table_of(table_ref, info[AT])
    skeleton, pick1 = leaf_picks(table, rank, info[LEAF] % GROUP, where)
    level0 = mm(skeleton, got_ref[:, :width]).astype(BF16)
    level1 = mm(pick1, level0).astype(BF16)
    core = info[CORE]

    def part(side):
        index2 = node_picks(table, rank, 2, 4 * info[NODE] + 2 * side, 2) - rank * (info[CHIP] % 2)
        return mm((index2 == iota((half, rank), 1)).astype(BF16), level1).astype(BF16)

    keep_ref[...] = part(core)
    give_ref[:, :width] = part(1 - core)
    give_ref[:, width : width + columns] = weight0[:half]
    give_ref[:, width + columns :] = weight0[half:]


def piece(info, pieces_ref, leaf):
    return pieces_ref.at[leaf % 2 ^ info[CORE], leaf // 2 ^ info[PHYS]]


def in_order(core, mine, other):
    return jnp.where(core == 0, jnp.concatenate([mine, other]), jnp.concatenate([other, mine]))


def level1_kernel(info, other_ref, keep_ref, weight0_ref, own_piece_ref, other_piece_ref, out_ref, weight1_ref):
    rank, columns = weight1_ref.shape
    half, width = keep_ref.shape
    core = info[CORE]
    other0 = jnp.concatenate([other_ref[:, width : width + columns], other_ref[:, width + columns :]])
    both0 = in_order(core, weight0_ref[...], other0)
    weight1 = in_order(core, mm(own_piece_ref[...], both0), mm(other_piece_ref[...], both0)).astype(BF16)
    weight1_ref[...] = weight1
    out_ref[:, :width] = keep_ref[...] + other_ref[:, :width]
    out_ref[:, width : width + columns] = weight1[:half]
    out_ref[:, width + columns :] = weight1[half:]


def level23_kernel(info, m0, m1, m2, m3, pieces_ref, out_ref, weight2_ref, weight3_ref, w1_s):
    half = m0.shape[0]
    rank = 2 * half
    columns = weight2_ref.shape[1]
    width = m0.shape[1] - 2 * columns
    core, chip, node = info[CORE], info[CHIP], info[NODE]
    for k, message in enumerate((m0, m1, m2, m3)):
        at = pl.ds(pl.multiple_of((chip ^ k) * rank, rank), rank)
        w1_s[at] = jnp.concatenate([message[:, width : width + columns], message[:, width + columns :]])
    r2, r3 = rank >> 2, rank >> 3
    for n in (0, 1):
        for i in range(4):
            rows2 = piece(info, pieces_ref, 4 * n + i)[:r2]
            at = n * rank + i * r2
            weight2_ref[at : at + r2] = mm(rows2, w1_s[2 * n * rank : 2 * (n + 1) * rank]).astype(BF16)
    low = r2
    weight3 = jnp.concatenate(
        [mm(piece(info, pieces_ref, i)[low : low + r3], weight2_ref[...]) for i in range(GROUP)]
    )
    weight3_ref[...] = weight3.astype(BF16)
    own = m0[:, :width] + m1[:, :width]
    cross = m2[:, :width] + m3[:, :width]
    out_ref[:half, :width] = jnp.where(node == 0, own, cross)
    out_ref[half:, :width] = jnp.where(node == 0, cross, own)
    for n in (0, 1):
        at = pl.ds(pl.multiple_of(n * rank + core * half, half), half)
        out_ref[n * half : (n + 1) * half, width : width + columns] = weight2_ref[at]
    out_ref[:, width + columns :] = weight3.astype(BF16)


def level3_kernel(info, own_ref, other_ref, table_ref, out_ref):
    half = out_ref.shape[0]
    rank = 2 * half
    columns = 64
    width = own_ref.shape[1] - 2 * columns
    core = info[CORE]
    index = node_picks(table_of(table_ref, info[AT]), rank, 3, 4 * core, 4)
    entry = index % rank
    at = index // rank * half + entry % half
    hit = at == iota((half, rank), 1)
    mine = (hit & (entry // half == core)).astype(BF16)
    theirs = (hit & (entry // half != core)).astype(BF16)
    out_ref[:, :width] = (mm(mine, own_ref[:, :width]) + mm(theirs, other_ref[:, :width])).astype(BF16)
    out_ref[:, width : width + columns] = own_ref[:half, width + columns :]
    out_ref[:, width + columns :] = own_ref[half:, width + columns :]


def level4_kernel(info, weight3_ref, next_ref, before_ref, pieces_ref, out_ref):
    rank, columns = weight3_ref.shape
    low = (rank >> 2) + (rank >> 3)
    sibling = jnp.where(info[AT] % 2 == 0, next_ref[:, columns:], before_ref[:, columns:])
    both = in_order(info[AT] % 2, weight3_ref[...], sibling)
    r4 = rank >> 4
    for i in range(GROUP):
        out_ref[i * r4 : (i + 1) * r4] = mm(piece(info, pieces_ref, i)[low : low + r4], both).astype(BF16)


def far_masks(info, mask_ref, leaf, source):
    def at(level, step):
        column = jnp.clip(jnp.where(step < 0, step + FWIN, step + FWIN - 1), 0, 2 * FWIN - 1)
        value = mask_ref[leaf, 2 * NWIN + (level - 1) * 2 * FWIN + column]
        return jnp.where((step != 0) & (jnp.abs(step) <= FWIN) & (source >= 0), value, 0)

    node = 2 * info[AT] + info[NODE]
    return [
        at(2, 2 * source - node),
        at(2, 2 * source + 1 - node),
        at(3, source - info[AT]),
        at(4, source // 2 - info[AT] // 2),
    ]


def row_offset(block, scale_inv):
    squares = jnp.sum(jnp.square(block.astype(F32)), axis=1, keepdims=True)
    return (squares - block.shape[1]) * (0.5 * scale_inv)


def as_row(column):
    return jnp.transpose(jnp.broadcast_to(column, (column.shape[0], 128)))[0:1]


def kernel_block(targets, target_column, sources, source_row, scale_inv):
    products = mm_nt(targets, sources)
    return jnp.exp(products * scale_inv - target_column - source_row).astype(BF16)


def as_bf16(value):
    return value.astype(F32).astype(BF16)


def far_kernel(away, parents, sides, share, scale_inv, width, info, mask_ref, x1_ref, x2_ref, c1_ref, c2_ref, half_ref, w2_ref, table_ref,
               init1_ref, init2_ref, pairs_ref, *rest):
    parts, rest = rest[: len(away)], rest[len(away) :]
    w4_refs, (result, out1_ref, out2_ref, w_s, w4_s) = rest[: 2 * parents], rest[2 * parents :]
    columns = out1_ref.shape[1]
    half = half_ref.shape[0] // 2
    rank = 2 * half
    core, node = info[CORE], info[NODE]
    offsets = (c1_ref, c2_ref)
    out1_ref[...] = init1_ref[...]
    out2_ref[...] = init2_ref[...]
    side = [info[LEAF], info[LEAF] ^ 1]

    def run(sources, weights, masks):
        row = as_row(row_offset(sources, scale_inv))
        count = weights.shape[0] // 2
        for x_ref, offset, out_ref, mask in zip((x1_ref, x2_ref), offsets, (out1_ref, out2_ref), masks, strict=True):
            scaled = jnp.concatenate(
                [
                    jnp.concatenate([weights[i * count : (i + 1) * count, j * columns : (j + 1) * columns] * as_bf16(mask[i][j])
                                     for j in range(3)], axis=1)
                    for i in (0, 1)
                ]
            )
            kernel = kernel_block(x_ref[:, :width], offset[...], sources, row, scale_inv)
            sums = mm(kernel, scaled)
            out_ref[...] += sums[:, :columns] + sums[:, columns : 2 * columns] + sums[:, 2 * columns :]

    def spread_of(i, distance, part, source):
        if distance == 1:
            w3 = part[:, width + columns :]
        else:
            w3 = jnp.concatenate([part[:, width : width + columns], part[:, width + columns :]])
        step = source // 2 - info[AT] // 2
        parent = jnp.clip(jnp.where(step < 0, step + FWIN, step + FWIN - 1), 0, 2 * FWIN - 1)
        same, cross = w4_refs[0][...], w4_refs[1][...]
        for k in range(1, parents):
            same = jnp.where(parent == k, w4_refs[2 * k][...], same)
            cross = jnp.where(parent == k, w4_refs[2 * k + 1][...], cross)
        even = source - source % 2
        index = [node_picks(table_of(table_ref, group), rank, 4, 0, GROUP) for group in (even, even + 1)]
        index = jnp.concatenate(index) - rank * (source % 2)
        w4 = in_order(info[AT] % 2, same, cross)
        w4 = mm_tn((index == iota((rank, rank), 1)).astype(BF16), w4).astype(BF16)
        if distance == 1:
            index3 = node_picks(table_of(table_ref, source), rank, 3, 0, GROUP)
            lane = iota((rank, rank), 1)
            hit = (index3 == lane // half * rank + core * half + lane % half).astype(BF16)
            both = mm_tn(hit, jnp.concatenate([w3, w4], axis=1)).astype(BF16)
            return jnp.concatenate([part[:, width : width + columns], both], axis=1)
        w4_s[:, :columns] = w3
        w4_s[:, columns:] = w4
        rows = pl.ds(pl.multiple_of(core * half, half), half)
        return jnp.concatenate([jnp.zeros((half, columns), BF16), w4_s[rows]], axis=1)

    zero = jnp.zeros((), I32)
    joined = away.index(2) if 2 in away else -1
    for i, distance in enumerate(away):
        source = info[SLOT0 + i]
        known = jnp.maximum(source, 0)
        masks = [far_masks(info, mask_ref, leaf, source) for leaf in side]
        if distance == 1:
            used = sum(sum(m) for m in masks) > 0
            lists = [[[m[0], m[2], m[3]], [m[1], m[2], m[3]]] for m in masks]
        else:
            used = sum(m[2] + m[3] for m in masks) > 0
            lists = [[[zero, m[2], m[3]]] * 2 for m in masks]
        if i != joined:

            @pl.when(used)
            def _(i=i, distance=distance, known=known, lists=lists):
                run(parts[i][:, :width], spread_of(i, distance, parts[i], known), lists)

            continue
        cross = pl.ds(pl.multiple_of((1 - node) * half, half), half)
        column = jnp.where(node == 0, 2 * NWIN + 2 * FWIN + FWIN, 2 * NWIN + 2 * FWIN + FWIN - 1)
        w_s[:half, :columns] = w2_ref[pl.ds(pl.multiple_of((1 - node) * rank + core * half, half), half)]
        w_s[:half, columns:] = jnp.zeros((half, 2 * columns), BF16)
        w_s[half:] = spread_of(i, distance, parts[i], known)
        lists = [
            [[mask_ref[leaf, column], zero, zero], entry[0]] for leaf, entry in zip(side, lists, strict=True)
        ]
        run(jnp.concatenate([half_ref[cross, :width], parts[i][:, :width]]), w_s[...], lists)
    parts = (out1_ref[...].astype(BF16), out2_ref[...].astype(BF16), pairs_ref[...])
    at = 0
    for i in range(sides):
        for value in parts:
            lanes = value.shape[1]
            if sides == 2:
                value = value.reshape(-1, 2, share, lanes)[:, i].reshape(-1, lanes)
            result[:, at : at + lanes] = value
            at += lanes


def halves(value):
    half = value.shape[1] // 2
    return value[:, :half] + value[:, half:]


def masked(weights, first, second):
    lane = iota((1, weights.shape[1]), 1)
    return (weights.astype(F32) * jnp.where(lane < weights.shape[1] // 2, first, second)).astype(BF16)


def own_kernel(scale_inv, width, info, mask_ref, own_ref, other_ref, out_ref, back_ref, column_ref, column_other_ref):
    rows, columns = out_ref.shape
    half = rows // 2
    last = width + columns
    own_column = row_offset(own_ref[:, :width], scale_inv)
    other_column = row_offset(other_ref[:, :width], scale_inv)
    column_ref[...] = own_column
    column_other_ref[...] = other_column
    kernel = kernel_block(own_ref[:, :width], own_column, own_ref[:, :width], as_row(own_column), scale_inv)
    out_ref[...] = mm(kernel, own_ref[:, width:last])
    back_ref[...] = jnp.zeros_like(back_ref)
    near = mask_ref[info[LEAF] // 2 * 2, NWIN] > 0

    def pair(first, count):
        mine = own_ref[first:, :width]
        theirs = other_ref[:count, :width]
        kernel = kernel_block(mine, own_column[first:], theirs, as_row(other_column[:count]), scale_inv)
        out_ref[first:] += mm(kernel, other_ref[:count, width:last])
        back_ref[:count] = mm_tn(kernel, own_ref[first:, width:last])

    @pl.when(near & (info[CORE] == 0))
    def _():
        pair(0, half)

    @pl.when(near & (info[CORE] == 1))
    def _():
        pair(half, rows)


def leaf_weights(x, width, columns, weight1, table_ref, leaf):
    rank = weight1.shape[0]
    half = rank // 2
    extra = x[:, width:]
    row = iota((extra.shape[1], 128), 0)
    parts = jnp.where(row == columns, 32.0, jnp.where(row == columns + 1, 1.0, 0.0)).astype(BF16)
    where = mm(extra, parts)
    group = table_ref[pl.ds(pl.multiple_of(leaf // GROUP * GROUP, GROUP), GROUP), : rank + half]
    at = iota((GROUP, 1), 0)

    def of(index, low, high):
        return jnp.sum(jnp.where(at == index, group[:, low:high], 0.0), axis=0, keepdims=True)

    base = leaf % GROUP // 2 * 2
    index1 = jnp.concatenate([of(base + i, rank, rank + half) for i in (0, 1)], axis=1)
    index1 = index1 - (leaf % 2 * rank).astype(F32)
    pick1 = (iota((rank, rank), 0).astype(F32) == index1).astype(BF16)
    level0 = mm(pick1, weight1).astype(BF16)
    skeleton = of(leaf % GROUP, 0, rank)
    hit = [(where == skeleton[:, i : i + 128]).astype(BF16) for i in range(0, rank, 128)]
    spread = mm(jnp.concatenate(hit, axis=1), level0).astype(BF16)
    return jnp.concatenate([extra[:, :columns], spread], axis=1)


def pair_masks(info, mask_ref):
    core = info[CORE]
    chip = info[LEAF] // 2
    leaves = mask_ref.shape[0]
    r_leaf = jnp.minimum(2 * chip + 2, leaves - 2) + core
    level1 = 2 * NWIN
    masks, names = [], []
    for behind in (0, 1):
        for side in (core, 1 - core):
            leaf = jnp.maximum(2 * chip - 2 * behind, 0) + side
            there = (2 * chip + 2 < leaves) & (chip >= behind)
            distance = 2 + 2 * behind + core - side
            near = jnp.where(distance <= NWIN, mask_ref[leaf, jnp.minimum(NWIN - 1 + distance, 2 * NWIN - 1)], 0)
            values = (near, mask_ref[leaf, level1 + FWIN + behind], mask_ref[r_leaf, level1 + FWIN - 1 - behind])
            masks.append([jnp.where(there, v, 0) for v in values])
            names.append(leaf)
    return masks, names, r_leaf


def pair_sums(scale_inv, width, jobs, r, r_row, r_weights, acc):
    sums = []
    for mask, ref, column, weights in jobs:
        near, far_out, far_back = (m.astype(F32) for m in mask)
        kernel = kernel_block(ref[:, :width], column, r, r_row, scale_inv)
        sums.append(halves(mm(kernel, masked(r_weights, near, far_out))))
        acc += mm_tn(masked(weights, near, far_back), kernel)
    return sums, acc


def pair_kernel(scale_inv, width, info, mask_ref, q1, q2, c1, c2, p1a, p1b, p2a, p2b, ra, rb, w_all, w_cross,
                init1, init2, table_ref, out1, out2, result, p1, p2, r):
    for ref, parts in ((p1, (p1a, p1b)), (p2, (p2a, p2b)), (r, (ra, rb))):
        join(ref, *parts)
    columns = out1.shape[1]
    masks, names, r_leaf = pair_masks(info, mask_ref)
    refs = (q1, q2, p1, p2)
    chip, rank = info[CHIP], w_cross.shape[0]
    last = w_all.shape[0] // rank - 1

    def of(index, inside):
        at = pl.ds(pl.multiple_of(jnp.clip(index, 0, last) * rank, rank), rank)
        return jnp.where(inside, w_all[at], w_cross[...])

    w_q, w_p, w_r = of(chip, True), of(chip - 1, chip > 0), of(chip + 1, chip < last)
    r_weights = leaf_weights(r, width, columns, w_r, table_ref, r_leaf)
    r_row = as_row(row_offset(r[:, :width], scale_inv))
    acc = jnp.zeros((2 * columns, r.shape[0]), F32)
    sums = []
    for i, (mask, ref, leaf) in enumerate(zip(masks, refs, names, strict=True)):
        weights = leaf_weights(ref, width, columns, w_q if i < 2 else w_p, table_ref, leaf)
        column = (c1, c2)[i][...] if i < 2 else row_offset(ref[:, :width], scale_inv)
        near, far_out, far_back = (m.astype(F32) for m in mask)
        kernel = kernel_block(ref[:, :width], column, r[:, :width], r_row, scale_inv)
        sums.append(halves(mm(kernel, masked(r_weights, near, far_out))))
        acc += mm_tn(masked(weights, near, far_back), kernel)
    out1[...] = init1[...] + sums[0]
    out2[...] = init2[...] + sums[1]
    for i, value in enumerate((sums[2], sums[3], halves(jnp.transpose(acc)))):
        result[:, i * columns : (i + 1) * columns] = value.astype(BF16)


def home_kernel(leaves, sides, place_ref, got_ref, out_ref, sum_s):
    columns, rows = out_ref.shape
    count = rows // leaves // sides
    for leaf in range(leaves):
        sources = (leaf, leaf ^ 1, leaf + 2, (leaf ^ 1) + 2, leaf - 2)
        for i in range(sides):
            total = 0.0
            for part, source in enumerate(sources):
                if 0 <= source < leaves:
                    at, lane = device_of_leaf(source) * count, (5 * i + part) * columns
                    total += got_ref[at : at + count, lane : lane + columns].astype(F32)
            at = (device_of_leaf(leaf) * sides + i) * count
            sum_s[at : at + count] = total
    total = sum_s[...]
    high = total.astype(BF16)
    low = (total - high.astype(F32)).astype(BF16)
    pick = (iota((rows, rows), 0) == place_ref[...]).astype(BF16)
    both = mm_tn(jnp.concatenate([high, low], axis=1), pick)
    out_ref[...] = both[:columns] + both[columns:]


def local(
    points, weights, tree_slot, leaf_interp, skel_leaf, merge_interp, merge_index, near_mask, far_mask
):
    leaves = lax.axis_size("leaf")
    groups = leaves // GROUP
    rows, width = points.shape
    columns = weights.shape[1]
    per_peer = rows // leaves
    rank = skel_leaf.shape[1]
    lanes = 4 * rank // per_peer
    wide = width + -(-(columns + 16 + lanes) // 128) * 128
    half = rank // 2
    scale_inv = 1.0 / (1.75 * math.sqrt(width))
    message = width + 2 * columns
    slots = slot_sources(groups)
    away = [a for a, _ in slots]

    def prefetch(count, grid, ins, outs, scratch=()):
        return pltpu.PrefetchScalarGridSpec(
            num_scalar_prefetch=count, grid=grid, in_specs=ins, out_specs=outs, scratch_shapes=scratch
        )

    send, place = call(
        functools.partial(sort_kernel, rows, per_peer, leaves, lanes),
        pl.GridSpec(
            grid=(4,),
            in_specs=[whole((1, rows)), whole((rows, width)), whole((columns, rows))]
            + [whole(a.shape) for a in (skel_leaf, merge_index, near_mask, far_mask)],
            out_specs=[
                pl.BlockSpec((rows // 4, wide), lambda i: (i, 0)),
                whole((1, rows)),
            ],
            scratch_shapes=[pltpu.VMEM((1, rows), I32), pltpu.VMEM((per_peer, lanes), BF16)],
        ),
        shapes(((rows, wide), BF16), ((1, rows), I32)),
        vmem=62,
    )(tree_slot.reshape(1, rows), points, weights.T, skel_leaf, merge_index, near_mask, far_mask)
    got = lax.all_to_all(send, "leaf", split_axis=0, concat_axis=0, tiled=True)

    def halo(value):
        def inside(by):
            return lambda i: i + by if (i + by) // GROUP == i // GROUP else -1

        return move(value, inside(2)), move(value, inside(-2))

    ends = []
    for g in range(1, groups):
        for i in (0, 1):
            pair = device_of_leaf(g * GROUP - 2 + i), device_of_leaf(g * GROUP + i)
            ends += [pair, pair[::-1]]

    def over_end(value):
        return lax.ppermute(value, "leaf", ends)


    device = lax.axis_index("leaf")
    leaf = leaf_of_device(device)
    group = leaf // GROUP
    source = jnp.asarray([s for _, s in slots], I32)[:, group]
    info = jnp.concatenate(
        [jnp.stack([leaf, leaf % 2, leaf // 2 % 4, leaf // 4 % 2, group, device // 2 % 4]).astype(I32), source]
    )
    interp_in, merge_in, _ = lax.optimization_barrier((leaf_interp[0], merge_interp[0], place))
    to_holder = [(i, device_of_leaf(i)) for i in range(leaves)]
    interp = lax.ppermute(interp_in, "leaf", to_holder)
    first = lax.ppermute(merge_in[:half], "leaf", to_holder)
    upper = merge_in[half:]
    uppers = [lax.ppermute(upper, "leaf", [(i, i ^ (2 * k)) for i in range(leaves)]) for k in (1, 2, 3)]
    got, interp, info, first, *uppers = lax.optimization_barrier((got, interp, info, first, *uppers))
    cut = rows * 3 // 8
    got_a, got_b = got[:cut], got[cut:]
    behind_a, ahead_a = halo(got_a)
    over_a = over_end(got_a)
    other = move(got, lambda i: i ^ 1)
    first_other = move(first, lambda i: i ^ 1)
    group_pieces = jnp.stack([upper] + uppers)
    pieces = jnp.stack([group_pieces, move(group_pieces, lambda i: i ^ 1)])
    piece_shape = pieces.shape

    coded = got[:, wide - lanes :].reshape(leaves, 4 * rank).astype(F32)
    high, low = coded[:, : 2 * rank], coded[:, 2 * rank :]
    tables = high * 32.0 + low
    mask_at = rank + merge_index.shape[1]
    masks = jnp.concatenate(
        [
            low[:, mask_at : mask_at + 2 * NWIN],
            high[:, mask_at : mask_at + LEVELS * 2 * FWIN],
        ],
        axis=1,
    ).astype(I32)
    table_shape = tables.shape

    leaf_x, joined = whole((rows, wide)), pltpu.VMEM((rows, wide), BF16)
    own_sum, other_sum, own_column, other_column = call(
        functools.partial(own_kernel, scale_inv, width),
        prefetch(2, (), [leaf_x] * 2, [whole((rows, columns))] * 2 + [whole((rows, 1))] * 2),
        shapes(*[((rows, columns), F32)] * 2, *[((rows, 1), F32)] * 2),
        flops=3 * rows * rows * width,
    )(info, masks, got, other)

    give, keep, weight0 = call(
        level0_kernel,
        prefetch(1, (), [leaf_x, whole((rank, rows)), whole(table_shape)],
                 [whole((half, message)), whole((half, width)), whole((rank, columns))]),
        shapes(((half, message), BF16), ((half, width), BF16), ((rank, columns), BF16)),
    )(info, after(got, own_sum), interp, tables)
    sent, weight1 = call(
        level1_kernel,
        prefetch(1, (), [whole((half, message)), whole((half, width)), whole((rank, columns))] + [whole((half, 2 * rank))] * 2,
                 [whole((half, message)), whole((rank, columns))]),
        shapes(((half, message), BF16), ((rank, columns), BF16)),
    )(info, move(give, lambda i: i ^ 1), keep, weight0, first, first_other)
    sent, behind_a, ahead_a, over_a, pieces = lax.optimization_barrier((sent, behind_a, ahead_a, over_a, pieces))
    over_b = over_end(after(got_b, over_a))

    def merged(behind, ahead, over):
        chip = leaf // 2 % 4
        return jnp.where(chip == 0, over, behind), jnp.where(chip == 3, over, ahead)

    behind_a, ahead_a = merged(behind_a, ahead_a, over_a)
    plane = [move(sent, lambda i, k=k: i ^ (2 * k)) for k in (1, 2, 3)]
    cross1 = over_end(after(weight1, sent))
    behind_other_a = move(behind_a, lambda i: i ^ 1)
    behind_b, ahead_b = halo(after(got_b, *plane))
    half2, weight2, weight3, weight1_all = call(
        level23_kernel,
        prefetch(1, (), [whole((half, message))] * 4 + [whole(piece_shape)],
                 [whole((rank, message)), whole((2 * rank, columns)), whole((rank, columns)), whole((4 * rank, columns))]),
        shapes(((rank, message), BF16), ((2 * rank, columns), BF16), ((rank, columns), BF16), ((4 * rank, columns), BF16)),
    )(info, after(sent, behind_other_a), *plane, pieces)
    half2_other = move(half2, lambda i: i ^ 1)
    half3 = call(
        level3_kernel,
        prefetch(1, (), [whole((rank, message))] * 2 + [whole(table_shape)], whole((half, message))),
        jax.ShapeDtypeStruct((half, message), BF16),
    )(info, half2, half2_other, tables)
    half3_late = after(half3, over_b)
    far_parts = [send_each(half2 if a == 1 else half3_late, s) for a, s in slots]
    extra = pl.BlockSpec((rank, 2 * columns), lambda *_: (0, width // (2 * columns)))
    half4 = call(
        level4_kernel,
        prefetch(1, (1,), [whole((rank, columns)), extra, extra, whole(piece_shape)], whole((half, columns))),
        jax.ShapeDtypeStruct((half, columns), BF16),
    )(info, after(weight3, half3), far_parts[0], far_parts[1], pieces)
    nodes4 = groups // 2
    steps4 = [(-1, 1)] if nodes4 == 2 else [(s,) for s in (-2, -1, 1, 2)]
    weight4 = []
    for steps in steps4:
        for h in (0, 1):
            found = [[2 * (g // 2 + s) + (g % 2 ^ h) for s in steps if 0 <= g // 2 + s < nodes4] for g in range(groups)]
            weight4.append(send_each(half4, [f[0] if f else -1 for f in found]))
    weight_1, sums, leaf_c = whole((rank, columns)), whole((rows, columns)), whole((rows, 1))
    behind_b, ahead_b = merged(behind_b, ahead_b, over_b)
    before_b = after(behind_b, ahead_b, half3, cross1, *far_parts[:2])
    behind_other = [behind_other_a, move(before_b, lambda i: i ^ 1)]
    pair_1, pair_2, pair_sum = call(
        functools.partial(pair_kernel, scale_inv, width),
        prefetch(2, (), [leaf_x] * 2 + [leaf_c] * 2 + [whole((cut, wide)), whole((rows - cut, wide))] * 3 + [whole((4 * rank, columns)), weight_1] + [sums] * 2 + [whole(table_shape)],
                 [sums] * 2 + [whole((rows, 3 * columns))], [joined] * 3),
        shapes(((rows, columns), F32), ((rows, columns), F32), ((rows, 3 * columns), BF16)),
        flops=8 * rows * rows * width,
    )(info, masks, after(got, half4), other, own_column, other_column, behind_a, behind_b,
      *behind_other, ahead_a, ahead_b, weight1_all, cross1, own_sum, other_sum, tables)

    sides = 2 if per_peer % 32 == 0 else 1
    all_sums = call(
        functools.partial(far_kernel, away, len(steps4), sides, per_peer // sides, scale_inv, width),
        prefetch(2, (), [leaf_x] * 2 + [leaf_c] * 2 + [whole((rank, message)), whole((2 * rank, columns)),
                 whole(table_shape), sums, sums, whole((rows, 3 * columns))]
                 + [whole(p.shape) for p in (*far_parts, *weight4)], whole((rows // sides, 5 * sides * columns)),
                 [pltpu.VMEM((rows, columns), F32)] * 2
                 + [pltpu.VMEM((rank, 3 * columns), BF16), pltpu.VMEM((rank, 2 * columns), BF16)]),
        jax.ShapeDtypeStruct((rows // sides, 5 * sides * columns), BF16),
        flops=4 * rows * rows * width,
    )(info, masks, got, other, own_column, other_column, half2, weight2, tables, pair_1, pair_2, pair_sum,
      *far_parts, *weight4)

    home = lax.all_to_all(all_sums, "leaf", split_axis=0, concat_axis=0, tiled=True)
    return call(
        functools.partial(home_kernel, leaves, sides),
        pl.GridSpec(grid=(), in_specs=[whole((1, rows)), whole((rows // sides, 5 * sides * columns))], out_specs=whole((columns, rows)),
                    scratch_shapes=[pltpu.VMEM((rows, columns), F32)]),
        jax.ShapeDtypeStruct((columns, rows), F32),
    )(place, home).T


def solution(mesh):
    placed = (
        P("leaf", None),
        P("leaf", None),
        P("leaf"),
        P("leaf", None, None),
        P("leaf", None),
        P("leaf", None, None),
        P("leaf", None),
        P("leaf", None),
        P("leaf", None, None),
    )
    return jax.shard_map(
        local, mesh=mesh, in_specs=placed, out_specs=P("leaf", None), check_vma=False
    )
```

```python
import functools
import math

import jax
import jax.numpy as jnp
from jax import lax
from jax.experimental import pallas as pl
from jax.experimental.pallas import tpu as pltpu
from jax.sharding import PartitionSpec as P

LEVELS = 4
NWIN = 4
FWIN = 2
GROUP = 8
BF16 = jnp.bfloat16
F32 = jnp.float32
I32 = jnp.int32
NT = (((1,), (1,)), ((), ()))
TN = (((0,), (0,)), ((), ()))
CHUNK = 256


def call(kernel, grid_spec, out_shape, vmem=40, flops=0):
    return pl.pallas_call(
        kernel,
        grid_spec=grid_spec,
        out_shape=out_shape,
        compiler_params=pltpu.CompilerParams(vmem_limit_bytes=vmem * 1024 * 1024),
        cost_estimate=pl.CostEstimate(flops=flops, bytes_accessed=0, transcendentals=0),
    )


def after(value, *others):
    return lax.optimization_barrier((value, *others))[0]


def whole(shape):
    return pl.BlockSpec(shape, lambda *_: (0,) * len(shape))


def shapes(*specs):
    return [jax.ShapeDtypeStruct(shape, kind) for shape, kind in specs]


def mm(a, b):
    return jnp.dot(a, b, preferred_element_type=F32)


def mm_nt(a, b):
    return lax.dot_general(a, b, NT, preferred_element_type=F32)


def mm_tn(a, b):
    return lax.dot_general(a, b, TN, preferred_element_type=F32)


def device_of_leaf(leaf):
    group, chip = leaf // GROUP, (leaf // 2) % 4
    return group * GROUP + ((chip ^ (chip >> 1)) ^ ((group & 1) * 2)) * 2 + leaf % 2


def leaf_of_device(device):
    group, chip = device // GROUP, (device // 2) % 4 ^ ((device // GROUP & 1) * 2)
    return group * GROUP + (chip ^ (chip >> 1)) * 2 + device % 2


def move(value, target_of_leaf):
    leaves = lax.axis_size("leaf")
    pairs = []
    for leaf in range(leaves):
        target = target_of_leaf(leaf)
        if 0 <= target < leaves:
            pairs.append((device_of_leaf(leaf), device_of_leaf(target)))
    return lax.ppermute(value, "leaf", pairs)


def slot_sources(groups):
    slots = []
    for away in range(1, min(6, groups)):
        merge = away > 1 and groups <= 2 * away
        for steps in [(away, -away)] if merge else [(away,), (-away,)]:
            found = [[g + s for s in steps if 0 <= g + s < groups] for g in range(groups)]
            slots.append((away, [f[0] if f else -1 for f in found]))
    return slots


def send_each(value, source):
    pairs = [(s * GROUP + i, g * GROUP + i) for g, s in enumerate(source) if s >= 0 for i in range(GROUP)]
    return lax.ppermute(value, "leaf", pairs)


LEAF, CORE, CHIP, NODE, AT, PHYS = range(6)
SLOT0 = 6


def iota(shape, dim):
    return lax.broadcasted_iota(I32, shape, dim)


def sort_kernel(
    rows, per_peer, leaves, lanes, slot_ref, points_ref, weights_ref, skel_ref, merge_ref, near_ref, far_ref,
    send_ref, place_ref, place_s, table_s,
):
    step = pl.program_id(0)
    block, wide = send_ref.shape
    slot = slot_ref[...]

    @pl.when(step == 0)
    def _():
        dest = device_of_leaf(slot // rows)
        at = (iota((leaves, rows), 0) == dest).astype(BF16)
        earlier = (iota((rows, rows), 0) < iota((rows, rows), 1)).astype(BF16)
        rank = jnp.sum(at.astype(F32) * mm(at, earlier), axis=0, keepdims=True)
        place_s[...] = dest * per_peer + rank.astype(I32)
        place_ref[...] = place_s[...]
        skel, merge = skel_ref[...], merge_ref[...]
        end = skel.shape[1] + merge.shape[1]
        second = 2 * skel.shape[1]
        table = jnp.zeros((per_peer, lanes), F32)
        for base, values in (
            (0, skel // 32),
            (skel.shape[1], merge // 32),
            *((end + 2 * FWIN * i, far_ref[0, i : i + 1]) for i in range(LEVELS)),
            (second, skel % 32),
            (second + skel.shape[1], merge % 32),
            (second + end, near_ref[...]),
        ):
            count = values.shape[1]
            row = (base + iota((per_peer, count), 1)) // lanes == iota((per_peer, count), 0)
            spread = jnp.where(row, values, 0).astype(F32).astype(BF16)
            fold = ((base + iota((count, lanes), 0)) % lanes == iota((count, lanes), 1)).astype(BF16)
            table += mm(spread, fold)
        table_s[...] = table.astype(BF16)

    pick = (iota((block, rows), 0) + step * block == place_s[...]).astype(BF16)
    width, columns = points_ref.shape[1], weights_ref.shape[0]
    inner = slot % rows
    row = iota((16, rows), 0)
    parts = jnp.where(row == 0, inner // 32, jnp.where(row == 1, inner % 32, 0)).astype(F32).astype(BF16)
    spread = (iota((block, per_peer), 0) % per_peer == iota((block, per_peer), 1)).astype(BF16)
    values = (
        (0, mm(pick, points_ref[...])),
        (width, mm_nt(pick, weights_ref[...])),
        (width + columns, mm_nt(pick, parts)),
        (width + columns + 16, jnp.zeros((block, wide - lanes - width - columns - 16), F32)),
        (wide - lanes, mm(spread, table_s[...])),
    )
    for at, value in values:
        send_ref[:, at : at + value.shape[1]] = value.astype(BF16)


def join(whole_ref, first_ref, second_ref):
    cut = first_ref.shape[0]
    whole_ref[:cut] = first_ref[...]
    whole_ref[cut:] = second_ref[...]


def tree_rows(extra):
    lane = iota((16, extra.shape[1]), 1)
    parts = jnp.where(lane == 0, 32.0, jnp.where(lane == 1, 1.0, 0.0)).astype(BF16)
    return mm_nt(parts, extra)[0:1].astype(I32)


def entries(table, low, high, leaf):
    lane = iota((1, GROUP), 1)
    return jnp.sum(jnp.where(lane == leaf, table[low:high], 0.0), axis=1, keepdims=True).astype(I32)


def table_of(table_ref, group):
    return jnp.transpose(table_ref[pl.ds(pl.multiple_of(group * GROUP, GROUP), GROUP)])


def bounds(rank):
    ends = [rank]
    for level in range(1, LEVELS + 1):
        ends.append(ends[-1] + (rank >> level))
    return ends


def node_picks(table, rank, level, first, count):
    low, high = bounds(rank)[level - 1 : level + 1]
    rows = high - low
    several = jnp.concatenate([table[low:high]] * count)
    lane = iota((1, GROUP), 1) - first
    row = iota((rows * count, 1), 0) // rows
    return jnp.sum(jnp.where(lane == row, several, 0.0), axis=1, keepdims=True).astype(I32)


def leaf_picks(table, rank, leaf, where):
    skeleton = (entries(table, 0, rank, leaf) == where).astype(BF16)
    index1 = node_picks(table, rank, 1, leaf // 2 * 2, 2) - rank * (leaf % 2)
    return skeleton, (index1 == iota((rank, rank), 1)).astype(BF16)


def level0_kernel(info, got_ref, interp_ref, table_ref, give_ref, keep_ref, weight0_ref):
    rank, columns = weight0_ref.shape
    rows, width = got_ref.shape[0], keep_ref.shape[1]
    half = rank // 2
    where = tree_rows(got_ref[:, width + columns :])
    order = (iota((rows, rows), 0) == where).astype(BF16)
    weights = mm(order, got_ref[:, width : width + columns]).astype(BF16)
    weight0 = mm(interp_ref[...], weights).astype(BF16)
    weight0_ref[...] = weight0
    table = table_of(table_ref, info[AT])
    skeleton, pick1 = leaf_picks(table, rank, info[LEAF] % GROUP, where)
    level0 = mm(skeleton, got_ref[:, :width]).astype(BF16)
    level1 = mm(pick1, level0).astype(BF16)
    core = info[CORE]

    def part(side):
        index2 = node_picks(table, rank, 2, 4 * info[NODE] + 2 * side, 2) - rank * (info[CHIP] % 2)
        return mm((index2 == iota((half, rank), 1)).astype(BF16), level1).astype(BF16)

    keep_ref[...] = part(core)
    give_ref[:, :width] = part(1 - core)
    give_ref[:, width : width + columns] = weight0[:half]
    give_ref[:, width + columns :] = weight0[half:]


def piece(info, pieces_ref, leaf):
    return pieces_ref.at[leaf % 2 ^ info[CORE], leaf // 2 ^ info[PHYS]]


def in_order(core, mine, other):
    return jnp.where(core == 0, jnp.concatenate([mine, other]), jnp.concatenate([other, mine]))


def level1_kernel(info, other_ref, keep_ref, weight0_ref, own_piece_ref, other_piece_ref, out_ref, weight1_ref):
    rank, columns = weight1_ref.shape
    half, width = keep_ref.shape
    core = info[CORE]
    other0 = jnp.concatenate([other_ref[:, width : width + columns], other_ref[:, width + columns :]])
    both0 = in_order(core, weight0_ref[...], other0)
    weight1 = in_order(core, mm(own_piece_ref[...], both0), mm(other_piece_ref[...], both0)).astype(BF16)
    weight1_ref[...] = weight1
    out_ref[:, :width] = keep_ref[...] + other_ref[:, :width]
    out_ref[:, width : width + columns] = weight1[:half]
    out_ref[:, width + columns :] = weight1[half:]


def level23_kernel(info, m0, m1, m2, m3, pieces_ref, out_ref, weight2_ref, weight3_ref, w1_s):
    half = m0.shape[0]
    rank = 2 * half
    columns = weight2_ref.shape[1]
    width = m0.shape[1] - 2 * columns
    core, chip, node = info[CORE], info[CHIP], info[NODE]
    for k, message in enumerate((m0, m1, m2, m3)):
        at = pl.ds(pl.multiple_of((chip ^ k) * rank, rank), rank)
        w1_s[at] = jnp.concatenate([message[:, width : width + columns], message[:, width + columns :]])
    r2, r3 = rank >> 2, rank >> 3
    for n in (0, 1):
        for i in range(4):
            rows2 = piece(info, pieces_ref, 4 * n + i)[:r2]
            at = n * rank + i * r2
            weight2_ref[at : at + r2] = mm(rows2, w1_s[2 * n * rank : 2 * (n + 1) * rank]).astype(BF16)
    low = r2
    weight3 = jnp.concatenate(
        [mm(piece(info, pieces_ref, i)[low : low + r3], weight2_ref[...]) for i in range(GROUP)]
    )
    weight3_ref[...] = weight3.astype(BF16)
    own = m0[:, :width] + m1[:, :width]
    cross = m2[:, :width] + m3[:, :width]
    out_ref[:half, :width] = jnp.where(node == 0, own, cross)
    out_ref[half:, :width] = jnp.where(node == 0, cross, own)
    for n in (0, 1):
        at = pl.ds(pl.multiple_of(n * rank + core * half, half), half)
        out_ref[n * half : (n + 1) * half, width : width + columns] = weight2_ref[at]
    out_ref[:, width + columns : width + 2 * columns] = weight3.astype(BF16)
    out_ref[:, width + 2 * columns : width + 3 * columns] = w1_s[:rank]
    out_ref[:, width + 3 * columns :] = w1_s[3 * rank :]


def level3_kernel(info, own_ref, other_ref, table_ref, out_ref):
    half = out_ref.shape[0]
    rank = 2 * half
    columns = 64
    width = out_ref.shape[1] - 2 * columns
    core = info[CORE]
    index = node_picks(table_of(table_ref, info[AT]), rank, 3, 4 * core, 4)
    entry = index % rank
    at = index // rank * half + entry % half
    hit = at == iota((half, rank), 1)
    mine = (hit & (entry // half == core)).astype(BF16)
    theirs = (hit & (entry // half != core)).astype(BF16)
    out_ref[:, :width] = (mm(mine, own_ref[:, :width]) + mm(theirs, other_ref[:, :width])).astype(BF16)
    out_ref[:, width : width + columns] = own_ref[:half, width + columns : width + 2 * columns]
    out_ref[:, width + columns :] = own_ref[half:, width + columns : width + 2 * columns]


def level4_kernel(info, weight3_ref, next_ref, before_ref, pieces_ref, out_ref):
    rank, columns = weight3_ref.shape
    low = (rank >> 2) + (rank >> 3)
    sibling = jnp.where(info[AT] % 2 == 0, next_ref[:, columns:], before_ref[:, columns:])
    both = in_order(info[AT] % 2, weight3_ref[...], sibling)
    r4 = rank >> 4
    for i in range(GROUP):
        out_ref[i * r4 : (i + 1) * r4] = mm(piece(info, pieces_ref, i)[low : low + r4], both).astype(BF16)


def far_masks(info, mask_ref, leaf, source):
    def at(level, step):
        column = jnp.clip(jnp.where(step < 0, step + FWIN, step + FWIN - 1), 0, 2 * FWIN - 1)
        value = mask_ref[leaf, 2 * NWIN + (level - 1) * 2 * FWIN + column]
        return jnp.where((step != 0) & (jnp.abs(step) <= FWIN) & (source >= 0), value, 0)

    node = 2 * info[AT] + info[NODE]
    return [
        at(2, 2 * source - node),
        at(2, 2 * source + 1 - node),
        at(3, source - info[AT]),
        at(4, source // 2 - info[AT] // 2),
    ]


def row_offset(block, scale_inv):
    squares = jnp.sum(jnp.square(block.astype(F32)), axis=1, keepdims=True)
    return (squares - block.shape[1]) * (0.5 * scale_inv)


def as_row(column):
    return jnp.transpose(jnp.broadcast_to(column, (column.shape[0], 128)))[0:1]


def kernel_block(targets, target_column, sources, source_row, scale_inv):
    products = mm_nt(targets, sources)
    return jnp.exp(products * scale_inv - target_column - source_row).astype(BF16)


def as_bf16(value):
    return value.astype(F32).astype(BF16)


def far_kernel(away, parents, sides, share, scale_inv, width, info, mask_ref, x1_ref, x2_ref, c1_ref, c2_ref, half_ref, w2_ref, table_ref,
               init1_ref, init2_ref, pairs_ref, *rest):
    parts, rest = rest[: len(away)], rest[len(away) :]
    w4_refs, (result, out1_ref, out2_ref, w_s, w4_s) = rest[: 2 * parents], rest[2 * parents :]
    columns = out1_ref.shape[1]
    half = half_ref.shape[0] // 2
    rank = 2 * half
    core, node = info[CORE], info[NODE]
    offsets = (c1_ref, c2_ref)
    out1_ref[...] = init1_ref[...]
    out2_ref[...] = init2_ref[...]
    side = [info[LEAF], info[LEAF] ^ 1]

    def run(sources, weights, masks):
        row = as_row(row_offset(sources, scale_inv))
        count = weights.shape[0] // 2
        for x_ref, offset, out_ref, mask in zip((x1_ref, x2_ref), offsets, (out1_ref, out2_ref), masks, strict=True):
            scaled = jnp.concatenate(
                [
                    jnp.concatenate([weights[i * count : (i + 1) * count, j * columns : (j + 1) * columns] * as_bf16(mask[i][j])
                                     for j in range(3)], axis=1)
                    for i in (0, 1)
                ]
            )
            kernel = kernel_block(x_ref[:, :width], offset[...], sources, row, scale_inv)
            sums = mm(kernel, scaled)
            out_ref[...] += sums[:, :columns] + sums[:, columns : 2 * columns] + sums[:, 2 * columns :]

    def spread_of(i, distance, part, source):
        if distance == 1:
            w3 = part[:, width + columns : width + 2 * columns]
        else:
            w3 = jnp.concatenate([part[:, width : width + columns], part[:, width + columns :]])
        step = source // 2 - info[AT] // 2
        parent = jnp.clip(jnp.where(step < 0, step + FWIN, step + FWIN - 1), 0, 2 * FWIN - 1)
        same, cross = w4_refs[0][...], w4_refs[1][...]
        for k in range(1, parents):
            same = jnp.where(parent == k, w4_refs[2 * k][...], same)
            cross = jnp.where(parent == k, w4_refs[2 * k + 1][...], cross)
        even = source - source % 2
        index = [node_picks(table_of(table_ref, group), rank, 4, 0, GROUP) for group in (even, even + 1)]
        index = jnp.concatenate(index) - rank * (source % 2)
        w4 = in_order(info[AT] % 2, same, cross)
        w4 = mm_tn((index == iota((rank, rank), 1)).astype(BF16), w4).astype(BF16)
        if distance == 1:
            index3 = node_picks(table_of(table_ref, source), rank, 3, 0, GROUP)
            lane = iota((rank, rank), 1)
            hit = (index3 == lane // half * rank + core * half + lane % half).astype(BF16)
            both = mm_tn(hit, jnp.concatenate([w3, w4], axis=1)).astype(BF16)
            return jnp.concatenate([part[:, width : width + columns], both], axis=1)
        w4_s[:, :columns] = w3
        w4_s[:, columns:] = w4
        rows = pl.ds(pl.multiple_of(core * half, half), half)
        return jnp.concatenate([jnp.zeros((half, columns), BF16), w4_s[rows]], axis=1)

    zero = jnp.zeros((), I32)
    joined = away.index(2) if 2 in away else -1
    for i, distance in enumerate(away):
        source = info[SLOT0 + i]
        known = jnp.maximum(source, 0)
        masks = [far_masks(info, mask_ref, leaf, source) for leaf in side]
        if distance == 1:
            used = sum(sum(m) for m in masks) > 0
            lists = [[[m[0], m[2], m[3]], [m[1], m[2], m[3]]] for m in masks]
        else:
            used = sum(m[2] + m[3] for m in masks) > 0
            lists = [[[zero, m[2], m[3]]] * 2 for m in masks]
        if i != joined:

            @pl.when(used)
            def _(i=i, distance=distance, known=known, lists=lists):
                run(parts[i][:, :width], spread_of(i, distance, parts[i], known), lists)

            continue
        cross = pl.ds(pl.multiple_of((1 - node) * half, half), half)
        column = jnp.where(node == 0, 2 * NWIN + 2 * FWIN + FWIN, 2 * NWIN + 2 * FWIN + FWIN - 1)
        w_s[:half, :columns] = w2_ref[pl.ds(pl.multiple_of((1 - node) * rank + core * half, half), half)]
        w_s[:half, columns:] = jnp.zeros((half, 2 * columns), BF16)
        w_s[half:] = spread_of(i, distance, parts[i], known)
        lists = [
            [[mask_ref[leaf, column], zero, zero], entry[0]] for leaf, entry in zip(side, lists, strict=True)
        ]
        run(jnp.concatenate([half_ref[cross, :width], parts[i][:, :width]]), w_s[...], lists)
    parts = (out1_ref[...].astype(BF16), out2_ref[...].astype(BF16), pairs_ref[...])
    at = 0
    for i in range(sides):
        for value in parts:
            lanes = value.shape[1]
            if sides == 2:
                value = value.reshape(-1, 2, share, lanes)[:, i].reshape(-1, lanes)
            result[:, at : at + lanes] = value
            at += lanes


def halves(value):
    half = value.shape[1] // 2
    return value[:, :half] + value[:, half:]


def masked(weights, first, second):
    lane = iota((1, weights.shape[1]), 1)
    return (weights.astype(F32) * jnp.where(lane < weights.shape[1] // 2, first, second)).astype(BF16)


def own_kernel(scale_inv, width, info, mask_ref, own_ref, other_ref, out_ref, back_ref, column_ref, column_other_ref):
    rows, columns = out_ref.shape
    half = rows // 2
    last = width + columns
    own_column = row_offset(own_ref[:, :width], scale_inv)
    other_column = row_offset(other_ref[:, :width], scale_inv)
    column_ref[...] = own_column
    column_other_ref[...] = other_column
    kernel = kernel_block(own_ref[:, :width], own_column, own_ref[:, :width], as_row(own_column), scale_inv)
    out_ref[...] = mm(kernel, own_ref[:, width:last])
    back_ref[...] = jnp.zeros_like(back_ref)
    near = mask_ref[info[LEAF] // 2 * 2, NWIN] > 0

    def pair(first, count):
        mine = own_ref[first:, :width]
        theirs = other_ref[:count, :width]
        kernel = kernel_block(mine, own_column[first:], theirs, as_row(other_column[:count]), scale_inv)
        out_ref[first:] += mm(kernel, other_ref[:count, width:last])
        back_ref[:count] = mm_tn(kernel, own_ref[first:, width:last])

    @pl.when(near & (info[CORE] == 0))
    def _():
        pair(0, half)

    @pl.when(near & (info[CORE] == 1))
    def _():
        pair(half, rows)


def leaf_weights(x, width, columns, weight1, table_ref, leaf):
    rank = weight1.shape[0]
    half = rank // 2
    extra = x[:, width:]
    row = iota((extra.shape[1], 128), 0)
    parts = jnp.where(row == columns, 32.0, jnp.where(row == columns + 1, 1.0, 0.0)).astype(BF16)
    where = mm(extra, parts)
    group = table_ref[pl.ds(pl.multiple_of(leaf // GROUP * GROUP, GROUP), GROUP), : rank + half]
    at = iota((GROUP, 1), 0)

    def of(index, low, high):
        return jnp.sum(jnp.where(at == index, group[:, low:high], 0.0), axis=0, keepdims=True)

    base = leaf % GROUP // 2 * 2
    index1 = jnp.concatenate([of(base + i, rank, rank + half) for i in (0, 1)], axis=1)
    index1 = index1 - (leaf % 2 * rank).astype(F32)
    pick1 = (iota((rank, rank), 0).astype(F32) == index1).astype(BF16)
    level0 = mm(pick1, weight1).astype(BF16)
    skeleton = of(leaf % GROUP, 0, rank)
    hit = [(where == skeleton[:, i : i + 128]).astype(BF16) for i in range(0, rank, 128)]
    spread = mm(jnp.concatenate(hit, axis=1), level0).astype(BF16)
    return jnp.concatenate([extra[:, :columns], spread], axis=1)


def pair_masks(info, mask_ref):
    core = info[CORE]
    chip = info[LEAF] // 2
    leaves = mask_ref.shape[0]
    r_leaf = jnp.minimum(2 * chip + 2, leaves - 2) + core
    level1 = 2 * NWIN
    masks, names = [], []
    for behind in (0, 1):
        for side in (core, 1 - core):
            leaf = jnp.maximum(2 * chip - 2 * behind, 0) + side
            there = (2 * chip + 2 < leaves) & (chip >= behind)
            distance = 2 + 2 * behind + core - side
            near = jnp.where(distance <= NWIN, mask_ref[leaf, jnp.minimum(NWIN - 1 + distance, 2 * NWIN - 1)], 0)
            values = (near, mask_ref[leaf, level1 + FWIN + behind], mask_ref[r_leaf, level1 + FWIN - 1 - behind])
            masks.append([jnp.where(there, v, 0) for v in values])
            names.append(leaf)
    return masks, names, r_leaf


def pair_sums(scale_inv, width, jobs, r, r_row, r_weights, acc):
    sums = []
    for mask, ref, column, weights in jobs:
        near, far_out, far_back = (m.astype(F32) for m in mask)
        kernel = kernel_block(ref[:, :width], column, r, r_row, scale_inv)
        sums.append(halves(mm(kernel, masked(r_weights, near, far_out))))
        acc += mm_tn(masked(weights, near, far_back), kernel)
    return sums, acc


def pair_kernel(scale_inv, width, info, mask_ref, q1, q2, c1, c2, p1a, p1b, p2a, p2b, ra, rb, w_all, w_next, w_before,
                init1, init2, table_ref, out1, out2, result, p1, p2, r):
    for ref, parts in ((p1, (p1a, p1b)), (p2, (p2a, p2b)), (r, (ra, rb))):
        join(ref, *parts)
    columns = out1.shape[1]
    masks, names, r_leaf = pair_masks(info, mask_ref)
    refs = (q1, q2, p1, p2)
    chip, rank = info[CHIP], w_next.shape[0]
    last = w_all.shape[0] // rank - 1

    def of(index, inside, w_cross):
        at = pl.ds(pl.multiple_of(jnp.clip(index, 0, last) * rank, rank), rank)
        return jnp.where(inside, w_all[at], w_cross)

    over_next, over_before = w_next[:, :columns], w_before[:, columns:]
    w_q = of(chip, True, over_next)
    w_p, w_r = of(chip - 1, chip > 0, over_before), of(chip + 1, chip < last, over_next)
    r_weights = leaf_weights(r, width, columns, w_r, table_ref, r_leaf)
    r_row = as_row(row_offset(r[:, :width], scale_inv))
    acc = jnp.zeros((2 * columns, r.shape[0]), F32)
    sums = []
    for i, (mask, ref, leaf) in enumerate(zip(masks, refs, names, strict=True)):
        weights = leaf_weights(ref, width, columns, w_q if i < 2 else w_p, table_ref, leaf)
        column = (c1, c2)[i][...] if i < 2 else row_offset(ref[:, :width], scale_inv)
        near, far_out, far_back = (m.astype(F32) for m in mask)
        kernel = kernel_block(ref[:, :width], column, r[:, :width], r_row, scale_inv)
        sums.append(halves(mm(kernel, masked(r_weights, near, far_out))))
        acc += mm_tn(masked(weights, near, far_back), kernel)
    out1[...] = init1[...] + sums[0]
    out2[...] = init2[...] + sums[1]
    for i, value in enumerate((sums[2], sums[3], halves(jnp.transpose(acc)))):
        result[:, i * columns : (i + 1) * columns] = value.astype(BF16)


def home_kernel(leaves, sides, place_ref, got_ref, out_ref, sum_s):
    columns, rows = out_ref.shape
    count = rows // leaves // sides
    for leaf in range(leaves):
        sources = (leaf, leaf ^ 1, leaf + 2, (leaf ^ 1) + 2, leaf - 2)
        for i in range(sides):
            total = 0.0
            for part, source in enumerate(sources):
                if 0 <= source < leaves:
                    at, lane = device_of_leaf(source) * count, (5 * i + part) * columns
                    total += got_ref[at : at + count, lane : lane + columns].astype(F32)
            at = (device_of_leaf(leaf) * sides + i) * count
            sum_s[at : at + count] = total
    total = sum_s[...]
    high = total.astype(BF16)
    low = (total - high.astype(F32)).astype(BF16)
    pick = (iota((rows, rows), 0) == place_ref[...]).astype(BF16)
    both = mm_tn(jnp.concatenate([high, low], axis=1), pick)
    out_ref[...] = both[:columns] + both[columns:]


def local(
    points, weights, tree_slot, leaf_interp, skel_leaf, merge_interp, merge_index, near_mask, far_mask
):
    leaves = lax.axis_size("leaf")
    groups = leaves // GROUP
    rows, width = points.shape
    columns = weights.shape[1]
    per_peer = rows // leaves
    rank = skel_leaf.shape[1]
    lanes = 4 * rank // per_peer
    wide = width + -(-(columns + 16 + lanes) // 128) * 128
    half = rank // 2
    scale_inv = 1.0 / (1.75 * math.sqrt(width))
    message, message2 = width + 2 * columns, width + 4 * columns
    slots = slot_sources(groups)
    away = [a for a, _ in slots]

    def prefetch(count, grid, ins, outs, scratch=()):
        return pltpu.PrefetchScalarGridSpec(
            num_scalar_prefetch=count, grid=grid, in_specs=ins, out_specs=outs, scratch_shapes=scratch
        )

    send, place = call(
        functools.partial(sort_kernel, rows, per_peer, leaves, lanes),
        pl.GridSpec(
            grid=(4,),
            in_specs=[whole((1, rows)), whole((rows, width)), whole((columns, rows))]
            + [whole(a.shape) for a in (skel_leaf, merge_index, near_mask, far_mask)],
            out_specs=[
                pl.BlockSpec((rows // 4, wide), lambda i: (i, 0)),
                whole((1, rows)),
            ],
            scratch_shapes=[pltpu.VMEM((1, rows), I32), pltpu.VMEM((per_peer, lanes), BF16)],
        ),
        shapes(((rows, wide), BF16), ((1, rows), I32)),
        vmem=62,
    )(tree_slot.reshape(1, rows), points, weights.T, skel_leaf, merge_index, near_mask, far_mask)
    got = lax.all_to_all(send, "leaf", split_axis=0, concat_axis=0, tiled=True)

    def halo(value):
        def inside(by):
            return lambda i: i + by if (i + by) // GROUP == i // GROUP else -1

        return move(value, inside(2)), move(value, inside(-2))

    ends = []
    for g in range(1, groups):
        for i in (0, 1):
            pair = device_of_leaf(g * GROUP - 2 + i), device_of_leaf(g * GROUP + i)
            ends += [pair, pair[::-1]]

    def over_end(value):
        return lax.ppermute(value, "leaf", ends)


    device = lax.axis_index("leaf")
    leaf = leaf_of_device(device)
    group = leaf // GROUP
    source = jnp.asarray([s for _, s in slots], I32)[:, group]
    info = jnp.concatenate(
        [jnp.stack([leaf, leaf % 2, leaf // 2 % 4, leaf // 4 % 2, group, device // 2 % 4]).astype(I32), source]
    )
    interp_in, merge_in, _ = lax.optimization_barrier((leaf_interp[0], merge_interp[0], place))
    to_holder = [(i, device_of_leaf(i)) for i in range(leaves)]
    interp = lax.ppermute(interp_in, "leaf", to_holder)
    first = lax.ppermute(merge_in[:half], "leaf", to_holder)
    upper = merge_in[half:]
    uppers = [lax.ppermute(upper, "leaf", [(i, i ^ (2 * k)) for i in range(leaves)]) for k in (1, 2, 3)]
    got, interp, info, first, *uppers = lax.optimization_barrier((got, interp, info, first, *uppers))
    cut = rows * 3 // 8
    got_a, got_b = got[:cut], got[cut:]
    behind_a, ahead_a = halo(got_a)
    over_a = over_end(got_a)
    other = move(got, lambda i: i ^ 1)
    first_other = move(first, lambda i: i ^ 1)
    group_pieces = jnp.stack([upper] + uppers)
    pieces = jnp.stack([group_pieces, move(group_pieces, lambda i: i ^ 1)])
    piece_shape = pieces.shape

    coded = got[:, wide - lanes :].reshape(leaves, 4 * rank).astype(F32)
    high, low = coded[:, : 2 * rank], coded[:, 2 * rank :]
    tables = high * 32.0 + low
    mask_at = rank + merge_index.shape[1]
    masks = jnp.concatenate(
        [
            low[:, mask_at : mask_at + 2 * NWIN],
            high[:, mask_at : mask_at + LEVELS * 2 * FWIN],
        ],
        axis=1,
    ).astype(I32)
    table_shape = tables.shape

    leaf_x, joined = whole((rows, wide)), pltpu.VMEM((rows, wide), BF16)
    own_sum, other_sum, own_column, other_column = call(
        functools.partial(own_kernel, scale_inv, width),
        prefetch(2, (), [leaf_x] * 2, [whole((rows, columns))] * 2 + [whole((rows, 1))] * 2),
        shapes(*[((rows, columns), F32)] * 2, *[((rows, 1), F32)] * 2),
        flops=3 * rows * rows * width,
    )(info, masks, got, other)

    give, keep, weight0 = call(
        level0_kernel,
        prefetch(1, (), [leaf_x, whole((rank, rows)), whole(table_shape)],
                 [whole((half, message)), whole((half, width)), whole((rank, columns))]),
        shapes(((half, message), BF16), ((half, width), BF16), ((rank, columns), BF16)),
    )(info, after(got, own_sum), interp, tables)
    sent, weight1 = call(
        level1_kernel,
        prefetch(1, (), [whole((half, message)), whole((half, width)), whole((rank, columns))] + [whole((half, 2 * rank))] * 2,
                 [whole((half, message)), whole((rank, columns))]),
        shapes(((half, message), BF16), ((rank, columns), BF16)),
    )(info, move(give, lambda i: i ^ 1), keep, weight0, first, first_other)
    sent, behind_a, ahead_a, over_a, pieces = lax.optimization_barrier((sent, behind_a, ahead_a, over_a, pieces))
    over_b = over_end(after(got_b, over_a))

    def merged(behind, ahead, over):
        chip = leaf // 2 % 4
        return jnp.where(chip == 0, over, behind), jnp.where(chip == 3, over, ahead)

    behind_a, ahead_a = merged(behind_a, ahead_a, over_a)
    plane = [move(sent, lambda i, k=k: i ^ (2 * k)) for k in (1, 2, 3)]
    behind_other_a = move(behind_a, lambda i: i ^ 1)
    behind_b, ahead_b = halo(after(got_b, *plane))
    half2, weight2, weight3, weight1_all = call(
        level23_kernel,
        prefetch(1, (), [whole((half, message))] * 4 + [whole(piece_shape)],
                 [whole((rank, message2)), whole((2 * rank, columns)), whole((rank, columns)), whole((4 * rank, columns))]),
        shapes(((rank, message2), BF16), ((2 * rank, columns), BF16), ((rank, columns), BF16), ((4 * rank, columns), BF16)),
    )(info, after(sent, behind_other_a), *plane, pieces)
    half2_other = move(half2, lambda i: i ^ 1)
    half3 = call(
        level3_kernel,
        prefetch(1, (), [whole((rank, message2))] * 2 + [whole(table_shape)], whole((half, message))),
        jax.ShapeDtypeStruct((half, message), BF16),
    )(info, half2, half2_other, tables)
    half3_late = after(half3, over_b)
    far_parts = [send_each(half2 if a == 1 else half3_late, s) for a, s in slots]
    extra = pl.BlockSpec((rank, 2 * columns), lambda *_: (0, width // (2 * columns)))
    half4 = call(
        level4_kernel,
        prefetch(1, (1,), [whole((rank, columns)), extra, extra, whole(piece_shape)], whole((half, columns))),
        jax.ShapeDtypeStruct((half, columns), BF16),
    )(info, after(weight3, half3), far_parts[0], far_parts[1], pieces)
    nodes4 = groups // 2
    steps4 = [(-1, 1)] if nodes4 == 2 else [(s,) for s in (-2, -1, 1, 2)]
    weight4 = []
    for steps in steps4:
        for h in (0, 1):
            found = [[2 * (g // 2 + s) + (g % 2 ^ h) for s in steps if 0 <= g // 2 + s < nodes4] for g in range(groups)]
            weight4.append(send_each(half4, [f[0] if f else -1 for f in found]))
    ends1 = pl.BlockSpec((rank, 2 * columns), lambda *_: (0, message // (2 * columns)))
    sums, leaf_c = whole((rows, columns)), whole((rows, 1))
    behind_b, ahead_b = merged(behind_b, ahead_b, over_b)
    before_b = after(behind_b, ahead_b, half3, *far_parts[:2])
    behind_other = [behind_other_a, move(before_b, lambda i: i ^ 1)]
    pair_1, pair_2, pair_sum = call(
        functools.partial(pair_kernel, scale_inv, width),
        prefetch(2, (1,), [leaf_x] * 2 + [leaf_c] * 2 + [whole((cut, wide)), whole((rows - cut, wide))] * 3 + [whole((4 * rank, columns)), ends1, ends1] + [sums] * 2 + [whole(table_shape)],
                 [sums] * 2 + [whole((rows, 3 * columns))], [joined] * 3),
        shapes(((rows, columns), F32), ((rows, columns), F32), ((rows, 3 * columns), BF16)),
        flops=8 * rows * rows * width,
    )(info, masks, after(got, half4), other, own_column, other_column, behind_a, behind_b,
      *behind_other, ahead_a, ahead_b, weight1_all, far_parts[0], far_parts[1], own_sum, other_sum, tables)

    sides = 2 if per_peer % 32 == 0 else 1
    all_sums = call(
        functools.partial(far_kernel, away, len(steps4), sides, per_peer // sides, scale_inv, width),
        prefetch(2, (), [leaf_x] * 2 + [leaf_c] * 2 + [whole((rank, message2)), whole((2 * rank, columns)),
                 whole(table_shape), sums, sums, whole((rows, 3 * columns))]
                 + [whole(p.shape) for p in (*far_parts, *weight4)], whole((rows // sides, 5 * sides * columns)),
                 [pltpu.VMEM((rows, columns), F32)] * 2
                 + [pltpu.VMEM((rank, 3 * columns), BF16), pltpu.VMEM((rank, 2 * columns), BF16)]),
        jax.ShapeDtypeStruct((rows // sides, 5 * sides * columns), BF16),
        flops=4 * rows * rows * width,
    )(info, masks, got, other, own_column, other_column, half2, weight2, tables, pair_1, pair_2, pair_sum,
      *far_parts, *weight4)

    home = lax.all_to_all(all_sums, "leaf", split_axis=0, concat_axis=0, tiled=True)
    return call(
        functools.partial(home_kernel, leaves, sides),
        pl.GridSpec(grid=(), in_specs=[whole((1, rows)), whole((rows // sides, 5 * sides * columns))], out_specs=whole((columns, rows)),
                    scratch_shapes=[pltpu.VMEM((rows, columns), F32)]),
        jax.ShapeDtypeStruct((columns, rows), F32),
    )(place, home).T


def solution(mesh):
    placed = (
        P("leaf", None),
        P("leaf", None),
        P("leaf"),
        P("leaf", None, None),
        P("leaf", None),
        P("leaf", None, None),
        P("leaf", None),
        P("leaf", None),
        P("leaf", None, None),
    )
    return jax.shard_map(
        local, mesh=mesh, in_specs=placed, out_specs=P("leaf", None), check_vma=False
    )
```

```python
import functools
import math

import jax
import jax.numpy as jnp
from jax import lax
from jax.experimental import pallas as pl
from jax.experimental.pallas import tpu as pltpu
from jax.sharding import PartitionSpec as P

LEVELS = 4
NWIN = 4
FWIN = 2
GROUP = 8
BF16 = jnp.bfloat16
F32 = jnp.float32
I32 = jnp.int32
NT = (((1,), (1,)), ((), ()))
TN = (((0,), (0,)), ((), ()))
CHUNK = 256


def call(kernel, grid_spec, out_shape, vmem=40, flops=0):
    return pl.pallas_call(
        kernel,
        grid_spec=grid_spec,
        out_shape=out_shape,
        compiler_params=pltpu.CompilerParams(vmem_limit_bytes=vmem * 1024 * 1024),
        cost_estimate=pl.CostEstimate(flops=flops, bytes_accessed=0, transcendentals=0),
    )


def after(value, *others):
    return lax.optimization_barrier((value, *others))[0]


def whole(shape):
    return pl.BlockSpec(shape, lambda *_: (0,) * len(shape))


def shapes(*specs):
    return [jax.ShapeDtypeStruct(shape, kind) for shape, kind in specs]


def mm(a, b):
    return jnp.dot(a, b, preferred_element_type=F32)


def mm_nt(a, b):
    return lax.dot_general(a, b, NT, preferred_element_type=F32)


def mm_tn(a, b):
    return lax.dot_general(a, b, TN, preferred_element_type=F32)


def device_of_leaf(leaf):
    group, chip = leaf // GROUP, (leaf // 2) % 4
    return group * GROUP + ((chip ^ (chip >> 1)) ^ ((group & 1) * 2)) * 2 + leaf % 2


def leaf_of_device(device):
    group, chip = device // GROUP, (device // 2) % 4 ^ ((device // GROUP & 1) * 2)
    return group * GROUP + (chip ^ (chip >> 1)) * 2 + device % 2


def move(value, target_of_leaf):
    leaves = lax.axis_size("leaf")
    pairs = []
    for leaf in range(leaves):
        target = target_of_leaf(leaf)
        if 0 <= target < leaves:
            pairs.append((device_of_leaf(leaf), device_of_leaf(target)))
    return lax.ppermute(value, "leaf", pairs)


def slot_sources(groups):
    slots = []
    for away in range(1, min(6, groups)):
        merge = away > 1 and groups <= 2 * away
        for steps in [(away, -away)] if merge else [(away,), (-away,)]:
            found = [[g + s for s in steps if 0 <= g + s < groups] for g in range(groups)]
            slots.append((away, [f[0] if f else -1 for f in found]))
    return slots


def send_each(value, source):
    pairs = [(s * GROUP + i, g * GROUP + i) for g, s in enumerate(source) if s >= 0 for i in range(GROUP)]
    return lax.ppermute(value, "leaf", pairs)


LEAF, CORE, CHIP, NODE, AT, PHYS = range(6)
SLOT0 = 6


def iota(shape, dim):
    return lax.broadcasted_iota(I32, shape, dim)


def sort_kernel(
    rows, per_peer, leaves, lanes, slot_ref, points_ref, weights_ref, skel_ref, merge_ref, near_ref, far_ref,
    send_ref, place_ref, place_s, table_s,
):
    step = pl.program_id(0)
    block, wide = send_ref.shape
    slot = slot_ref[...]

    @pl.when(step == 0)
    def _():
        dest = device_of_leaf(slot // rows)
        at = (iota((leaves, rows), 0) == dest).astype(BF16)
        earlier = (iota((rows, rows), 0) < iota((rows, rows), 1)).astype(BF16)
        rank = jnp.sum(at.astype(F32) * mm(at, earlier), axis=0, keepdims=True)
        place_s[...] = dest * per_peer + rank.astype(I32)
        place_ref[...] = place_s[...]
        skel, merge = skel_ref[...], merge_ref[...]
        end = skel.shape[1] + merge.shape[1]
        second = 2 * skel.shape[1]
        table = jnp.zeros((per_peer, lanes), F32)
        for base, values in (
            (0, skel // 32),
            (skel.shape[1], merge // 32),
            *((end + 2 * FWIN * i, far_ref[0, i : i + 1]) for i in range(LEVELS)),
            (second, skel % 32),
            (second + skel.shape[1], merge % 32),
            (second + end, near_ref[...]),
        ):
            count = values.shape[1]
            row = (base + iota((per_peer, count), 1)) // lanes == iota((per_peer, count), 0)
            spread = jnp.where(row, values, 0).astype(F32).astype(BF16)
            fold = ((base + iota((count, lanes), 0)) % lanes == iota((count, lanes), 1)).astype(BF16)
            table += mm(spread, fold)
        table_s[...] = table.astype(BF16)

    pick = (iota((block, rows), 0) + step * block == place_s[...]).astype(BF16)
    width, columns = points_ref.shape[1], weights_ref.shape[0]
    inner = slot % rows
    row = iota((16, rows), 0)
    parts = jnp.where(row == 0, inner // 32, jnp.where(row == 1, inner % 32, 0)).astype(F32).astype(BF16)
    spread = (iota((block, per_peer), 0) % per_peer == iota((block, per_peer), 1)).astype(BF16)
    values = (
        (0, mm(pick, points_ref[...])),
        (width, mm_nt(pick, weights_ref[...])),
        (width + columns, mm_nt(pick, parts)),
        (width + columns + 16, jnp.zeros((block, wide - lanes - width - columns - 16), F32)),
        (wide - lanes, mm(spread, table_s[...])),
    )
    for at, value in values:
        send_ref[:, at : at + value.shape[1]] = value.astype(BF16)


def join(whole_ref, first_ref, second_ref):
    cut = first_ref.shape[0]
    whole_ref[:cut] = first_ref[...]
    whole_ref[cut:] = second_ref[...]


def tree_rows(extra):
    lane = iota((16, extra.shape[1]), 1)
    parts = jnp.where(lane == 0, 32.0, jnp.where(lane == 1, 1.0, 0.0)).astype(BF16)
    return mm_nt(parts, extra)[0:1].astype(I32)


def entries(table, low, high, leaf):
    lane = iota((1, GROUP), 1)
    return jnp.sum(jnp.where(lane == leaf, table[low:high], 0.0), axis=1, keepdims=True).astype(I32)


def table_of(table_ref, group):
    return jnp.transpose(table_ref[pl.ds(pl.multiple_of(group * GROUP, GROUP), GROUP)])


def bounds(rank):
    ends = [rank]
    for level in range(1, LEVELS + 1):
        ends.append(ends[-1] + (rank >> level))
    return ends


def node_picks(table, rank, level, first, count):
    low, high = bounds(rank)[level - 1 : level + 1]
    rows = high - low
    several = jnp.concatenate([table[low:high]] * count)
    lane = iota((1, GROUP), 1) - first
    row = iota((rows * count, 1), 0) // rows
    return jnp.sum(jnp.where(lane == row, several, 0.0), axis=1, keepdims=True).astype(I32)


def leaf_picks(table, rank, leaf, where):
    skeleton = (entries(table, 0, rank, leaf) == where).astype(BF16)
    index1 = node_picks(table, rank, 1, leaf // 2 * 2, 2) - rank * (leaf % 2)
    return skeleton, (index1 == iota((rank, rank), 1)).astype(BF16)


def level0_kernel(info, got_ref, interp_ref, table_ref, give_ref, keep_ref, weight0_ref):
    rank, columns = weight0_ref.shape
    rows, width = got_ref.shape[0], keep_ref.shape[1]
    half = rank // 2
    where = tree_rows(got_ref[:, width + columns :])
    order = (iota((rows, rows), 0) == where).astype(BF16)
    weights = mm(order, got_ref[:, width : width + columns]).astype(BF16)
    weight0 = mm(interp_ref[...], weights).astype(BF16)
    weight0_ref[...] = weight0
    table = table_of(table_ref, info[AT])
    skeleton, pick1 = leaf_picks(table, rank, info[LEAF] % GROUP, where)
    level0 = mm(skeleton, got_ref[:, :width]).astype(BF16)
    level1 = mm(pick1, level0).astype(BF16)
    core = info[CORE]

    def part(side):
        index2 = node_picks(table, rank, 2, 4 * info[NODE] + 2 * side, 2) - rank * (info[CHIP] % 2)
        return mm((index2 == iota((half, rank), 1)).astype(BF16), level1).astype(BF16)

    keep_ref[...] = part(core)
    give_ref[:, :width] = part(1 - core)
    give_ref[:, width : width + columns] = weight0[:half]
    give_ref[:, width + columns :] = weight0[half:]


def piece(info, pieces_ref, leaf):
    return pieces_ref.at[leaf % 2 ^ info[CORE], leaf // 2 ^ info[PHYS]]


def in_order(core, mine, other):
    return jnp.where(core == 0, jnp.concatenate([mine, other]), jnp.concatenate([other, mine]))


def level1_kernel(info, other_ref, keep_ref, weight0_ref, own_piece_ref, other_piece_ref, out_ref, weight1_ref):
    rank, columns = weight1_ref.shape
    half, width = keep_ref.shape
    core = info[CORE]
    other0 = jnp.concatenate([other_ref[:, width : width + columns], other_ref[:, width + columns :]])
    both0 = in_order(core, weight0_ref[...], other0)
    weight1 = in_order(core, mm(own_piece_ref[...], both0), mm(other_piece_ref[...], both0)).astype(BF16)
    weight1_ref[...] = weight1
    out_ref[:, :width] = keep_ref[...] + other_ref[:, :width]
    out_ref[:, width : width + columns] = weight1[:half]
    out_ref[:, width + columns :] = weight1[half:]


def level23_kernel(info, m0, m1, m2, m3, pieces_ref, out_ref, weight2_ref, weight3_ref, w1_s):
    half = m0.shape[0]
    rank = 2 * half
    columns = weight2_ref.shape[1]
    width = m0.shape[1] - 2 * columns
    core, chip, node = info[CORE], info[CHIP], info[NODE]
    for k, message in enumerate((m0, m1, m2, m3)):
        at = pl.ds(pl.multiple_of((chip ^ k) * rank, rank), rank)
        w1_s[at] = jnp.concatenate([message[:, width : width + columns], message[:, width + columns :]])
    r2, r3 = rank >> 2, rank >> 3
    for n in (0, 1):
        for i in range(4):
            rows2 = piece(info, pieces_ref, 4 * n + i)[:r2]
            at = n * rank + i * r2
            weight2_ref[at : at + r2] = mm(rows2, w1_s[2 * n * rank : 2 * (n + 1) * rank]).astype(BF16)
    low = r2
    weight3 = jnp.concatenate(
        [mm(piece(info, pieces_ref, i)[low : low + r3], weight2_ref[...]) for i in range(GROUP)]
    )
    weight3_ref[...] = weight3.astype(BF16)
    own = m0[:, :width] + m1[:, :width]
    cross = m2[:, :width] + m3[:, :width]
    out_ref[:half, :width] = jnp.where(node == 0, own, cross)
    out_ref[half:, :width] = jnp.where(node == 0, cross, own)
    for n in (0, 1):
        at = pl.ds(pl.multiple_of(n * rank + core * half, half), half)
        out_ref[n * half : (n + 1) * half, width : width + columns] = weight2_ref[at]
    out_ref[:, width + columns : width + 2 * columns] = weight3.astype(BF16)
    out_ref[:, width + 2 * columns : width + 3 * columns] = w1_s[:rank]
    out_ref[:, width + 3 * columns :] = w1_s[3 * rank :]


def level3_kernel(info, own_ref, other_ref, table_ref, out_ref):
    half = out_ref.shape[0]
    rank = 2 * half
    columns = 64
    width = out_ref.shape[1] - 2 * columns
    core = info[CORE]
    index = node_picks(table_of(table_ref, info[AT]), rank, 3, 4 * core, 4)
    entry = index % rank
    at = index // rank * half + entry % half
    hit = at == iota((half, rank), 1)
    mine = (hit & (entry // half == core)).astype(BF16)
    theirs = (hit & (entry // half != core)).astype(BF16)
    out_ref[:, :width] = (mm(mine, own_ref[:, :width]) + mm(theirs, other_ref[:, :width])).astype(BF16)
    out_ref[:, width : width + columns] = own_ref[:half, width + columns : width + 2 * columns]
    out_ref[:, width + columns :] = own_ref[half:, width + columns : width + 2 * columns]


def level4_kernel(info, weight3_ref, next_ref, before_ref, pieces_ref, out_ref):
    rank, columns = weight3_ref.shape
    low = (rank >> 2) + (rank >> 3)
    sibling = jnp.where(info[AT] % 2 == 0, next_ref[:, columns:], before_ref[:, columns:])
    both = in_order(info[AT] % 2, weight3_ref[...], sibling)
    r4 = rank >> 4
    for i in range(GROUP):
        out_ref[i * r4 : (i + 1) * r4] = mm(piece(info, pieces_ref, i)[low : low + r4], both).astype(BF16)


def far_masks(info, mask_ref, leaf, source):
    def at(level, step):
        column = jnp.clip(jnp.where(step < 0, step + FWIN, step + FWIN - 1), 0, 2 * FWIN - 1)
        value = mask_ref[leaf, 2 * NWIN + (level - 1) * 2 * FWIN + column]
        return jnp.where((step != 0) & (jnp.abs(step) <= FWIN) & (source >= 0), value, 0)

    node = 2 * info[AT] + info[NODE]
    return [
        at(2, 2 * source - node),
        at(2, 2 * source + 1 - node),
        at(3, source - info[AT]),
        at(4, source // 2 - info[AT] // 2),
    ]


def row_offset(block, scale_inv):
    squares = jnp.sum(jnp.square(block.astype(F32)), axis=1, keepdims=True)
    return (squares - block.shape[1]) * (0.5 * scale_inv)


def as_row(column):
    return jnp.transpose(jnp.broadcast_to(column, (column.shape[0], 128)))[0:1]


def kernel_block(targets, target_column, sources, source_row, scale_inv):
    products = mm_nt(targets, sources)
    return jnp.exp(products * scale_inv - target_column - source_row).astype(BF16)


def as_bf16(value):
    return value.astype(F32).astype(BF16)


def far_kernel(away, parents, sides, share, scale_inv, width, info, mask_ref, x1_ref, x2_ref, c1_ref, c2_ref, half_ref, w2_ref, table_ref,
               init1_ref, init2_ref, pairs_ref, *rest):
    parts, rest = rest[: len(away)], rest[len(away) :]
    w4_refs, (result, out1_ref, out2_ref, w_s, w4_s) = rest[: 2 * parents], rest[2 * parents :]
    columns = out1_ref.shape[1]
    half = half_ref.shape[0] // 2
    rank = 2 * half
    core, node = info[CORE], info[NODE]
    offsets = (c1_ref, c2_ref)
    out1_ref[...] = init1_ref[...]
    out2_ref[...] = init2_ref[...]
    side = [info[LEAF], info[LEAF] ^ 1]

    def run(sources, weights, masks):
        row = as_row(row_offset(sources, scale_inv))
        count = weights.shape[0] // 2
        for x_ref, offset, out_ref, mask in zip((x1_ref, x2_ref), offsets, (out1_ref, out2_ref), masks, strict=True):
            scaled = jnp.concatenate(
                [
                    jnp.concatenate([weights[i * count : (i + 1) * count, j * columns : (j + 1) * columns] * as_bf16(mask[i][j])
                                     for j in range(3)], axis=1)
                    for i in (0, 1)
                ]
            )
            kernel = kernel_block(x_ref[:, :width], offset[...], sources, row, scale_inv)
            sums = mm(kernel, scaled)
            out_ref[...] += sums[:, :columns] + sums[:, columns : 2 * columns] + sums[:, 2 * columns :]

    def spread_of(i, distance, part, source):
        if distance == 1:
            w3 = part[:, width + columns : width + 2 * columns]
        else:
            w3 = jnp.concatenate([part[:, width : width + columns], part[:, width + columns :]])
        step = source // 2 - info[AT] // 2
        parent = jnp.clip(jnp.where(step < 0, step + FWIN, step + FWIN - 1), 0, 2 * FWIN - 1)
        same, cross = w4_refs[0][...], w4_refs[1][...]
        for k in range(1, parents):
            same = jnp.where(parent == k, w4_refs[2 * k][...], same)
            cross = jnp.where(parent == k, w4_refs[2 * k + 1][...], cross)
        even = source - source % 2
        index = [node_picks(table_of(table_ref, group), rank, 4, 0, GROUP) for group in (even, even + 1)]
        index = jnp.concatenate(index) - rank * (source % 2)
        w4 = in_order(info[AT] % 2, same, cross)
        w4 = mm_tn((index == iota((rank, rank), 1)).astype(BF16), w4).astype(BF16)
        if distance == 1:
            index3 = node_picks(table_of(table_ref, source), rank, 3, 0, GROUP)
            lane = iota((rank, rank), 1)
            hit = (index3 == lane // half * rank + core * half + lane % half).astype(BF16)
            both = mm_tn(hit, jnp.concatenate([w3, w4], axis=1)).astype(BF16)
            return jnp.concatenate([part[:, width : width + columns], both], axis=1)
        w4_s[:, :columns] = w3
        w4_s[:, columns:] = w4
        rows = pl.ds(pl.multiple_of(core * half, half), half)
        return jnp.concatenate([jnp.zeros((half, columns), BF16), w4_s[rows]], axis=1)

    zero = jnp.zeros((), I32)
    joined = away.index(2) if 2 in away else -1
    for i, distance in enumerate(away):
        source = info[SLOT0 + i]
        known = jnp.maximum(source, 0)
        masks = [far_masks(info, mask_ref, leaf, source) for leaf in side]
        if distance == 1:
            used = sum(sum(m) for m in masks) > 0
            lists = [[[m[0], m[2], m[3]], [m[1], m[2], m[3]]] for m in masks]
        else:
            used = sum(m[2] + m[3] for m in masks) > 0
            lists = [[[zero, m[2], m[3]]] * 2 for m in masks]
        if i != joined:

            @pl.when(used)
            def _(i=i, distance=distance, known=known, lists=lists):
                run(parts[i][:, :width], spread_of(i, distance, parts[i], known), lists)

            continue
        cross = pl.ds(pl.multiple_of((1 - node) * half, half), half)
        column = jnp.where(node == 0, 2 * NWIN + 2 * FWIN + FWIN, 2 * NWIN + 2 * FWIN + FWIN - 1)
        w_s[:half, :columns] = w2_ref[pl.ds(pl.multiple_of((1 - node) * rank + core * half, half), half)]
        w_s[:half, columns:] = jnp.zeros((half, 2 * columns), BF16)
        w_s[half:] = spread_of(i, distance, parts[i], known)
        lists = [
            [[mask_ref[leaf, column], zero, zero], entry[0]] for leaf, entry in zip(side, lists, strict=True)
        ]
        run(jnp.concatenate([half_ref[cross, :width], parts[i][:, :width]]), w_s[...], lists)
    parts = (out1_ref[...].astype(BF16), out2_ref[...].astype(BF16), pairs_ref[...])
    at = 0
    for i in range(sides):
        for value in parts:
            lanes = value.shape[1]
            if sides == 2:
                value = value.reshape(-1, 2, share, lanes)[:, i].reshape(-1, lanes)
            result[:, at : at + lanes] = value
            at += lanes


def halves(value):
    half = value.shape[1] // 2
    return value[:, :half] + value[:, half:]


def masked(weights, first, second):
    lane = iota((1, weights.shape[1]), 1)
    return (weights.astype(F32) * jnp.where(lane < weights.shape[1] // 2, first, second)).astype(BF16)


def own_kernel(scale_inv, width, info, mask_ref, own_ref, other_ref, out_ref, back_ref, column_ref, column_other_ref):
    rows, columns = out_ref.shape
    half = rows // 2
    last = width + columns
    own_column = row_offset(own_ref[:, :width], scale_inv)
    other_column = row_offset(other_ref[:, :width], scale_inv)
    column_ref[...] = own_column
    column_other_ref[...] = other_column
    kernel = kernel_block(own_ref[:, :width], own_column, own_ref[:, :width], as_row(own_column), scale_inv)
    out_ref[...] = mm(kernel, own_ref[:, width:last])
    back_ref[...] = jnp.zeros_like(back_ref)
    near = mask_ref[info[LEAF] // 2 * 2, NWIN] > 0

    def pair(first, count):
        mine = own_ref[first:, :width]
        theirs = other_ref[:count, :width]
        kernel = kernel_block(mine, own_column[first:], theirs, as_row(other_column[:count]), scale_inv)
        out_ref[first:] += mm(kernel, other_ref[:count, width:last])
        back_ref[:count] = mm_tn(kernel, own_ref[first:, width:last])

    @pl.when(near & (info[CORE] == 0))
    def _():
        pair(0, half)

    @pl.when(near & (info[CORE] == 1))
    def _():
        pair(half, rows)


def leaf_weights(x, width, columns, weight1, table_ref, leaf):
    rank = weight1.shape[0]
    half = rank // 2
    extra = x[:, width:]
    row = iota((extra.shape[1], 128), 0)
    parts = jnp.where(row == columns, 32.0, jnp.where(row == columns + 1, 1.0, 0.0)).astype(BF16)
    where = mm(extra, parts)
    group = table_ref[pl.ds(pl.multiple_of(leaf // GROUP * GROUP, GROUP), GROUP), : rank + half]
    at = iota((GROUP, 1), 0)

    def of(index, low, high):
        return jnp.sum(jnp.where(at == index, group[:, low:high], 0.0), axis=0, keepdims=True)

    base = leaf % GROUP // 2 * 2
    index1 = jnp.concatenate([of(base + i, rank, rank + half) for i in (0, 1)], axis=1)
    index1 = index1 - (leaf % 2 * rank).astype(F32)
    pick1 = (iota((rank, rank), 0).astype(F32) == index1).astype(BF16)
    level0 = mm(pick1, weight1).astype(BF16)
    skeleton = of(leaf % GROUP, 0, rank)
    hit = [(where == skeleton[:, i : i + 128]).astype(BF16) for i in range(0, rank, 128)]
    spread = mm(jnp.concatenate(hit, axis=1), level0).astype(BF16)
    return jnp.concatenate([extra[:, :columns], spread], axis=1)


def pair_masks(info, mask_ref):
    core = info[CORE]
    chip = info[LEAF] // 2
    leaves = mask_ref.shape[0]
    r_leaf = jnp.minimum(2 * chip + 2, leaves - 2) + core
    level1 = 2 * NWIN
    masks, names = [], []
    for behind in (0, 1):
        for side in (core, 1 - core):
            leaf = jnp.maximum(2 * chip - 2 * behind, 0) + side
            there = (2 * chip + 2 < leaves) & (chip >= behind)
            distance = 2 + 2 * behind + core - side
            near = jnp.where(distance <= NWIN, mask_ref[leaf, jnp.minimum(NWIN - 1 + distance, 2 * NWIN - 1)], 0)
            values = (near, mask_ref[leaf, level1 + FWIN + behind], mask_ref[r_leaf, level1 + FWIN - 1 - behind])
            masks.append([jnp.where(there, v, 0) for v in values])
            names.append(leaf)
    return masks, names, r_leaf


def pair_sums(scale_inv, width, jobs, r, r_row, r_weights, acc):
    sums = []
    for mask, ref, column, weights in jobs:
        near, far_out, far_back = (m.astype(F32) for m in mask)
        kernel = kernel_block(ref[:, :width], column, r, r_row, scale_inv)
        sums.append(halves(mm(kernel, masked(r_weights, near, far_out))))
        acc += mm_tn(masked(weights, near, far_back), kernel)
    return sums, acc


def pair_kernel(scale_inv, width, info, mask_ref, q1, q2, c1, c2, p1a, p1b, p2a, p2b, ra, rb, w_all, w_next, w_before,
                init1, init2, table_ref, out1, out2, result, p1, p2, r):
    for ref, parts in ((p1, (p1a, p1b)), (p2, (p2a, p2b)), (r, (ra, rb))):
        join(ref, *parts)
    columns = out1.shape[1]
    masks, names, r_leaf = pair_masks(info, mask_ref)
    refs = (q1, q2, p1, p2)
    chip, rank = info[CHIP], w_next.shape[0]
    last = w_all.shape[0] // rank - 1

    def of(index, inside, w_cross):
        at = pl.ds(pl.multiple_of(jnp.clip(index, 0, last) * rank, rank), rank)
        return jnp.where(inside, w_all[at], w_cross)

    over_next, over_before = w_next[:, :columns], w_before[:, columns:]
    w_q = of(chip, True, over_next)
    w_p, w_r = of(chip - 1, chip > 0, over_before), of(chip + 1, chip < last, over_next)
    r_weights = leaf_weights(r, width, columns, w_r, table_ref, r_leaf)
    r_row = as_row(row_offset(r[:, :width], scale_inv))
    acc = jnp.zeros((2 * columns, r.shape[0]), F32)
    sums = []
    for i, (mask, ref, leaf) in enumerate(zip(masks, refs, names, strict=True)):
        weights = leaf_weights(ref, width, columns, w_q if i < 2 else w_p, table_ref, leaf)
        column = (c1, c2)[i][...] if i < 2 else row_offset(ref[:, :width], scale_inv)
        near, far_out, far_back = (m.astype(F32) for m in mask)
        kernel = kernel_block(ref[:, :width], column, r[:, :width], r_row, scale_inv)
        sums.append(halves(mm(kernel, masked(r_weights, near, far_out))))
        acc += mm_tn(masked(weights, near, far_back), kernel)
    out1[...] = init1[...] + sums[0]
    out2[...] = init2[...] + sums[1]
    for i, value in enumerate((sums[2], sums[3], halves(jnp.transpose(acc)))):
        result[:, i * columns : (i + 1) * columns] = value.astype(BF16)


def home_kernel(leaves, sides, place_ref, got_ref, out_ref, sum_s):
    columns, rows = out_ref.shape
    count = rows // leaves // sides
    for leaf in range(leaves):
        sources = (leaf, leaf ^ 1, leaf + 2, (leaf ^ 1) + 2, leaf - 2)
        for i in range(sides):
            total = 0.0
            for part, source in enumerate(sources):
                if 0 <= source < leaves:
                    at, lane = device_of_leaf(source) * count, (5 * i + part) * columns
                    total += got_ref[at : at + count, lane : lane + columns].astype(F32)
            at = (device_of_leaf(leaf) * sides + i) * count
            sum_s[at : at + count] = total
    total = sum_s[...]
    high = total.astype(BF16)
    low = (total - high.astype(F32)).astype(BF16)
    pick = (iota((rows, rows), 0) == place_ref[...]).astype(BF16)
    both = mm_tn(jnp.concatenate([high, low], axis=1), pick)
    out_ref[...] = both[:columns] + both[columns:]


def local(
    points, weights, tree_slot, leaf_interp, skel_leaf, merge_interp, merge_index, near_mask, far_mask
):
    leaves = lax.axis_size("leaf")
    groups = leaves // GROUP
    rows, width = points.shape
    columns = weights.shape[1]
    per_peer = rows // leaves
    rank = skel_leaf.shape[1]
    lanes = 4 * rank // per_peer
    wide = width + -(-(columns + 16 + lanes) // 128) * 128
    half = rank // 2
    scale_inv = 1.0 / (1.75 * math.sqrt(width))
    message, message2 = width + 2 * columns, width + 4 * columns
    slots = slot_sources(groups)
    away = [a for a, _ in slots]

    def prefetch(count, grid, ins, outs, scratch=()):
        return pltpu.PrefetchScalarGridSpec(
            num_scalar_prefetch=count, grid=grid, in_specs=ins, out_specs=outs, scratch_shapes=scratch
        )

    send, place = call(
        functools.partial(sort_kernel, rows, per_peer, leaves, lanes),
        pl.GridSpec(
            grid=(2,),
            in_specs=[whole((1, rows)), whole((rows, width)), whole((columns, rows))]
            + [whole(a.shape) for a in (skel_leaf, merge_index, near_mask, far_mask)],
            out_specs=[
                pl.BlockSpec((rows // 2, wide), lambda i: (i, 0)),
                whole((1, rows)),
            ],
            scratch_shapes=[pltpu.VMEM((1, rows), I32), pltpu.VMEM((per_peer, lanes), BF16)],
        ),
        shapes(((rows, wide), BF16), ((1, rows), I32)),
        vmem=62,
    )(tree_slot.reshape(1, rows), points, weights.T, skel_leaf, merge_index, near_mask, far_mask)
    got = lax.all_to_all(send, "leaf", split_axis=0, concat_axis=0, tiled=True)

    def halo(value):
        def inside(by):
            return lambda i: i + by if (i + by) // GROUP == i // GROUP else -1

        return move(value, inside(2)), move(value, inside(-2))

    ends = []
    for g in range(1, groups):
        for i in (0, 1):
            pair = device_of_leaf(g * GROUP - 2 + i), device_of_leaf(g * GROUP + i)
            ends += [pair, pair[::-1]]

    def over_end(value):
        return lax.ppermute(value, "leaf", ends)


    device = lax.axis_index("leaf")
    leaf = leaf_of_device(device)
    group = leaf // GROUP
    source = jnp.asarray([s for _, s in slots], I32)[:, group]
    info = jnp.concatenate(
        [jnp.stack([leaf, leaf % 2, leaf // 2 % 4, leaf // 4 % 2, group, device // 2 % 4]).astype(I32), source]
    )
    interp_in, merge_in, _ = lax.optimization_barrier((leaf_interp[0], merge_interp[0], place))
    to_holder = [(i, device_of_leaf(i)) for i in range(leaves)]
    interp = lax.ppermute(interp_in, "leaf", to_holder)
    first = lax.ppermute(merge_in[:half], "leaf", to_holder)
    upper = merge_in[half:]
    uppers = [lax.ppermute(upper, "leaf", [(i, i ^ (2 * k)) for i in range(leaves)]) for k in (1, 2, 3)]
    got, interp, info, first, *uppers = lax.optimization_barrier((got, interp, info, first, *uppers))
    cut = rows * 3 // 8
    got_a, got_b = got[:cut], got[cut:]
    behind_a, ahead_a = halo(got_a)
    over_a = over_end(got_a)
    other = move(got, lambda i: i ^ 1)
    first_other = move(first, lambda i: i ^ 1)
    group_pieces = jnp.stack([upper] + uppers)
    pieces = jnp.stack([group_pieces, move(group_pieces, lambda i: i ^ 1)])
    piece_shape = pieces.shape

    coded = got[:, wide - lanes :].reshape(leaves, 4 * rank).astype(F32)
    high, low = coded[:, : 2 * rank], coded[:, 2 * rank :]
    tables = high * 32.0 + low
    mask_at = rank + merge_index.shape[1]
    masks = jnp.concatenate(
        [
            low[:, mask_at : mask_at + 2 * NWIN],
            high[:, mask_at : mask_at + LEVELS * 2 * FWIN],
        ],
        axis=1,
    ).astype(I32)
    table_shape = tables.shape

    leaf_x, joined = whole((rows, wide)), pltpu.VMEM((rows, wide), BF16)
    own_sum, other_sum, own_column, other_column = call(
        functools.partial(own_kernel, scale_inv, width),
        prefetch(2, (), [leaf_x] * 2, [whole((rows, columns))] * 2 + [whole((rows, 1))] * 2),
        shapes(*[((rows, columns), F32)] * 2, *[((rows, 1), F32)] * 2),
        flops=3 * rows * rows * width,
    )(info, masks, got, other)

    give, keep, weight0 = call(
        level0_kernel,
        prefetch(1, (), [leaf_x, whole((rank, rows)), whole(table_shape)],
                 [whole((half, message)), whole((half, width)), whole((rank, columns))]),
        shapes(((half, message), BF16), ((half, width), BF16), ((rank, columns), BF16)),
    )(info, after(got, own_sum), interp, tables)
    sent, weight1 = call(
        level1_kernel,
        prefetch(1, (), [whole((half, message)), whole((half, width)), whole((rank, columns))] + [whole((half, 2 * rank))] * 2,
                 [whole((half, message)), whole((rank, columns))]),
        shapes(((half, message), BF16), ((rank, columns), BF16)),
    )(info, move(give, lambda i: i ^ 1), keep, weight0, first, first_other)
    sent, behind_a, ahead_a, over_a, pieces = lax.optimization_barrier((sent, behind_a, ahead_a, over_a, pieces))
    over_b = over_end(after(got_b, over_a))

    def merged(behind, ahead, over):
        chip = leaf // 2 % 4
        return jnp.where(chip == 0, over, behind), jnp.where(chip == 3, over, ahead)

    behind_a, ahead_a = merged(behind_a, ahead_a, over_a)
    plane = [move(sent, lambda i, k=k: i ^ (2 * k)) for k in (1, 2, 3)]
    behind_other_a = move(behind_a, lambda i: i ^ 1)
    behind_b, ahead_b = halo(after(got_b, *plane))
    half2, weight2, weight3, weight1_all = call(
        level23_kernel,
        prefetch(1, (), [whole((half, message))] * 4 + [whole(piece_shape)],
                 [whole((rank, message2)), whole((2 * rank, columns)), whole((rank, columns)), whole((4 * rank, columns))]),
        shapes(((rank, message2), BF16), ((2 * rank, columns), BF16), ((rank, columns), BF16), ((4 * rank, columns), BF16)),
    )(info, after(sent, behind_other_a), *plane, pieces)
    half2_other = move(half2, lambda i: i ^ 1)
    half3 = call(
        level3_kernel,
        prefetch(1, (), [whole((rank, message2))] * 2 + [whole(table_shape)], whole((half, message))),
        jax.ShapeDtypeStruct((half, message), BF16),
    )(info, half2, half2_other, tables)
    half3_late = after(half3, over_b)
    far_parts = [send_each(half2 if a == 1 else half3_late, s) for a, s in slots]
    extra = pl.BlockSpec((rank, 2 * columns), lambda *_: (0, width // (2 * columns)))
    half4 = call(
        level4_kernel,
        prefetch(1, (1,), [whole((rank, columns)), extra, extra, whole(piece_shape)], whole((half, columns))),
        jax.ShapeDtypeStruct((half, columns), BF16),
    )(info, after(weight3, half3), far_parts[0], far_parts[1], pieces)
    nodes4 = groups // 2
    steps4 = [(-1, 1)] if nodes4 == 2 else [(s,) for s in (-2, -1, 1, 2)]
    weight4 = []
    for steps in steps4:
        for h in (0, 1):
            found = [[2 * (g // 2 + s) + (g % 2 ^ h) for s in steps if 0 <= g // 2 + s < nodes4] for g in range(groups)]
            weight4.append(send_each(half4, [f[0] if f else -1 for f in found]))
    ends1 = pl.BlockSpec((rank, 2 * columns), lambda *_: (0, message // (2 * columns)))
    sums, leaf_c = whole((rows, columns)), whole((rows, 1))
    behind_b, ahead_b = merged(behind_b, ahead_b, over_b)
    before_b = after(behind_b, ahead_b, half3, *far_parts[:2])
    behind_other = [behind_other_a, move(before_b, lambda i: i ^ 1)]
    pair_1, pair_2, pair_sum = call(
        functools.partial(pair_kernel, scale_inv, width),
        prefetch(2, (1,), [leaf_x] * 2 + [leaf_c] * 2 + [whole((cut, wide)), whole((rows - cut, wide))] * 3 + [whole((4 * rank, columns)), ends1, ends1] + [sums] * 2 + [whole(table_shape)],
                 [sums] * 2 + [whole((rows, 3 * columns))], [joined] * 3),
        shapes(((rows, columns), F32), ((rows, columns), F32), ((rows, 3 * columns), BF16)),
        flops=8 * rows * rows * width,
    )(info, masks, after(got, half4), other, own_column, other_column, behind_a, behind_b,
      *behind_other, ahead_a, ahead_b, weight1_all, far_parts[0], far_parts[1], own_sum, other_sum, tables)

    sides = 2 if per_peer % 32 == 0 else 1
    all_sums = call(
        functools.partial(far_kernel, away, len(steps4), sides, per_peer // sides, scale_inv, width),
        prefetch(2, (), [leaf_x] * 2 + [leaf_c] * 2 + [whole((rank, message2)), whole((2 * rank, columns)),
                 whole(table_shape), sums, sums, whole((rows, 3 * columns))]
                 + [whole(p.shape) for p in (*far_parts, *weight4)], whole((rows // sides, 5 * sides * columns)),
                 [pltpu.VMEM((rows, columns), F32)] * 2
                 + [pltpu.VMEM((rank, 3 * columns), BF16), pltpu.VMEM((rank, 2 * columns), BF16)]),
        jax.ShapeDtypeStruct((rows // sides, 5 * sides * columns), BF16),
        flops=4 * rows * rows * width,
    )(info, masks, got, other, own_column, other_column, half2, weight2, tables, pair_1, pair_2, pair_sum,
      *far_parts, *weight4)

    home = lax.all_to_all(all_sums, "leaf", split_axis=0, concat_axis=0, tiled=True)
    return call(
        functools.partial(home_kernel, leaves, sides),
        pl.GridSpec(grid=(), in_specs=[whole((1, rows)), whole((rows // sides, 5 * sides * columns))], out_specs=whole((columns, rows)),
                    scratch_shapes=[pltpu.VMEM((rows, columns), F32)]),
        jax.ShapeDtypeStruct((columns, rows), F32),
    )(place, home).T


def solution(mesh):
    placed = (
        P("leaf", None),
        P("leaf", None),
        P("leaf"),
        P("leaf", None, None),
        P("leaf", None),
        P("leaf", None, None),
        P("leaf", None),
        P("leaf", None),
        P("leaf", None, None),
    )
    return jax.shard_map(
        local, mesh=mesh, in_specs=placed, out_specs=P("leaf", None), check_vma=False
    )
```
